128 devices in a mesh: tile: 32 (over z, y, core), rep: 4 (over x).
Axes of the slice: x: 4, y: 4, z: 4, core: 2. Of those that a mesh axis runs over, the one named last changes fastest.
Arguments:
- features: bfloat16 [4, 64, 64, 2048], P('rep', 'tile'), may hold values from -7 to 7
- head_grad: bfloat16 [4, 64, 64, 256], P('rep', 'tile'), may hold values from -6 to 6
- branch_weight: bfloat16 [29, 2048, 256], P(None, 'tile'), may hold values from -0.046875 to 0.046875
- proj_weight: bfloat16 [1280, 256], replicated, may hold values from -0.15625 to 0.15625
Outputs:
- head_out: bfloat16 [4, 64, 64, 256], P('rep', 'tile')
- grad_features: bfloat16 [4, 64, 64, 2048], P('rep', None, None, 'tile')
- grad_branch: float32 [29, 2048, 256], P(None, 'tile')
- grad_proj: float32 [1280, 256], replicated
The draws below stay inside these ranges and needn't reach their ends.
All inputs are finite; a program needn't handle non-finite values.
Results may differ from the reference program's by a relative error of at most 0.01.
Values may be sent and summed in bfloat16 or wider, within the bound.
No kernel may reach another device: no remote copies, remote signals or barrier semaphores. Data moves between devices by JAX's collectives and lax.ppermute only.
A program may use at most 320 MiB of HBM per device.

```python
import jax
import jax.numpy as jnp
from jax import lax

C_IN = 2048
BR = 256
COLS = 64
TAPS = 29
ROWS = 64
SLABS = 4
CAT = 1280


def draw_features(key, part):
    key = jax.random.fold_in(key, 11)
    key_offset, key_noise = jax.random.split(key, 2)
    shape = (SLABS, ROWS, COLS, C_IN)
    offset = jax.random.uniform(key_offset, (SLABS, 1, 1, C_IN), jnp.float32, -1.0, 1.0)
    noise = jax.random.normal(key_noise, shape, jnp.float32)
    values = offset + jnp.clip(noise, -5.9, 5.9)
    return values.astype(jnp.bfloat16)


def block_levels(key, extent, cuts, smallest, top_value):
    def one(position, parts):
        heights = jax.random.uniform(jax.random.fold_in(jax.random.fold_in(key, 6), position), (parts,), jnp.float32, smallest / len(cuts), top_value / len(cuts))
        return jnp.repeat(jnp.exp(heights), extent[position] // parts).reshape((-1,) + (1,) * (len(extent) - position - 1))

    loudness = one(*cuts[0])
    for cut in cuts[1:]:
        loudness = loudness * one(*cut)
    return loudness


def gaussian(rng, extent, scale, limit, shards=(), kind=jnp.bfloat16):
    array = jax.random.normal(rng, extent, jnp.float32) * scale
    if len(shards) > 0:
        array = block_levels(rng, extent, shards, -0.22, 0.18) * array
    return jnp.clip(array, min=-limit, max=limit).astype(kind)


def setup_inputs(seed: int = 0) -> dict:
    arg_keys = jax.random.split(jax.random.key(seed), 5)
    features = draw_features(jax.random.fold_in(arg_keys[4], 71), 0)
    head_grad = gaussian(arg_keys[1], (SLABS, ROWS, COLS, BR), 1.0, 6.0, ((0, 4), (1, 32)))
    branch_weight = gaussian(arg_keys[2], (TAPS, C_IN, BR), (9 * C_IN) ** -0.5, 0.046875, ((1, 32),))
    proj_weight = gaussian(arg_keys[3], (CAT, BR), CAT ** -0.5, 0.15625)
    return {"features": features, "head_grad": head_grad, "branch_weight": branch_weight, "proj_weight": proj_weight}


reach_cells = 36


def tap_offsets():
    offsets = [(0, 0)]
    for dilation_index in range(3):
        spacing = 12 * (dilation_index + 1)
        for row_step in range(3):
            for col_step in range(3):
                offsets.append(((row_step - 1) * spacing, (col_step - 1) * spacing))
    return offsets


def tap_range(branch):
    if branch == 0:
        return 0, 1
    return 1 + 9 * (branch - 1), 10 + 9 * (branch - 1)


def shifted(field, row_shift, col_shift):
    padded = jnp.pad(field, ((reach_cells, reach_cells), (reach_cells, reach_cells), (0, 0)))
    return lax.slice(padded, (reach_cells + row_shift, reach_cells + col_shift, 0),
                     (reach_cells + row_shift + field.shape[0], reach_cells + col_shift + field.shape[1], field.shape[2]))


def one_slab(features, head_grad, branch_weight, proj_weight):
    offsets = tap_offsets()
    pixels = ROWS * COLS
    pooled = jnp.mean(features.astype(jnp.float32), axis=(0, 1))
    pool_pre = jnp.dot(pooled, branch_weight[28].astype(jnp.float32), precision=lax.Precision.HIGHEST)
    columns = []
    for branch in range(4):
        low, high = tap_range(branch)
        stacked = jnp.concatenate([shifted(features, *offsets[tap_index]) for tap_index in range(low, high)], axis=2)
        columns.append(jnp.dot(stacked.reshape(pixels, -1), branch_weight[low:high].reshape(-1, BR), preferred_element_type=jnp.float32))
    columns.append(jnp.broadcast_to(pool_pre, (pixels, BR)))
    pre = jnp.concatenate(columns, axis=1)
    act = jnp.maximum(pre, 0.0).astype(jnp.bfloat16)
    grad_rows = head_grad.reshape(pixels, BR)
    head_out = jnp.dot(act, proj_weight, preferred_element_type=jnp.float32).astype(jnp.bfloat16)
    grad_proj = jnp.dot(act.T, grad_rows, preferred_element_type=jnp.float32)
    back = jnp.dot(grad_rows, proj_weight.T, preferred_element_type=jnp.float32)
    grad_pre = jnp.where(pre > 0, back, 0.0).astype(jnp.bfloat16)
    pool_grad = jnp.sum(grad_pre[:, 4 * BR:].astype(jnp.float32), axis=0)
    weight_parts = []
    field_grad = jnp.zeros((ROWS, COLS, C_IN), jnp.float32)
    for branch in range(4):
        low, high = tap_range(branch)
        grads = grad_pre[:, branch * BR:(branch + 1) * BR]
        stacked = jnp.concatenate([shifted(features, *offsets[tap_index]) for tap_index in range(low, high)], axis=2)
        weight_parts.append(jnp.dot(stacked.reshape(pixels, -1).T, grads, preferred_element_type=jnp.float32).reshape(high - low, C_IN, BR))
        spread = jnp.dot(grads, branch_weight[low:high].reshape(-1, BR).T, preferred_element_type=jnp.float32)
        spread = spread.reshape(ROWS, COLS, high - low, C_IN)
        for slot in range(high - low):
            row_shift, col_shift = offsets[low + slot]
            field_grad = field_grad + shifted(spread[:, :, slot, :], -row_shift, -col_shift)
    weight_parts.append(jnp.outer(pooled, pool_grad)[None])
    pool_field = jnp.dot(pool_grad, branch_weight[28].astype(jnp.float32).T, precision=lax.Precision.HIGHEST) / pixels
    grad_features = (field_grad + pool_field).astype(jnp.bfloat16)
    return head_out.reshape(ROWS, COLS, BR), grad_features, jnp.concatenate(weight_parts, axis=0), grad_proj


def reference(features, head_grad, branch_weight, proj_weight):
    outputs = []
    grads_out = []
    grad_branch = jnp.zeros((TAPS, C_IN, BR), jnp.float32)
    grad_proj = jnp.zeros((CAT, BR), jnp.float32)
    for slab in range(SLABS):
        head_part, field_part, branch_part, proj_part = one_slab(features[slab], head_grad[slab], branch_weight, proj_weight)
        outputs.append(head_part)
        grads_out.append(field_part)
        grad_branch = grad_branch + branch_part
        grad_proj = grad_proj + proj_part
    return jnp.stack(outputs), jnp.stack(grads_out), grad_branch, grad_proj
```

```python
import functools

import jax
import jax.numpy as jnp
from jax import lax
from jax.experimental import pallas as pl
from jax.experimental.pallas import tpu as pltpu
from jax.sharding import Mesh, PartitionSpec as P

GROUPS = 16
GP = 128
HALF = GROUPS * GP
COLS = 64
CH = 128
BR = 256
PAD = 9
SHIFTS = (0, -12, 12, -24, 24, -36, 36)
F32 = jnp.float32
BF = jnp.bfloat16
HIGH = lax.Precision.HIGHEST


def shift_slot(j, b):
    return SHIFTS.index((b - 1) * 12 * (j + 1))


def column_shift(value, amount):
    if amount == 0:
        return value
    n = value.shape[0]
    col = lax.broadcasted_iota(jnp.int32, value.shape, 0) & (COLS - 1)
    rolled = pltpu.roll(value, (-amount) % n, 0)
    return jnp.where((col + amount >= 0) & (col + amount < COLS), rolled, 0.0)


def join_weights(c, own, other, w):
    w[:, pl.ds(pl.multiple_of(c * 64, 64), 64), :] = own[...]
    w[:, pl.ds(pl.multiple_of((1 - c) * 64, 64), 64), :] = other[...]


def valid_steps(j, m, sign):
    steps = []
    for a in range(3):
        delta = 3 * (j + 1) * (a - 1)
        low = 4 * m + sign * delta
        if low + 3 >= 0 and low < GROUPS:
            steps.append((a, low))
    return steps


def forward_kernel(core_ref, x_ref, hg_ref, own, other, p_ref, colsum_ref, w, xs):
    join_weights(core_ref[0], own, other, w)
    xs[:, : PAD * GP, :] = jnp.zeros((7, PAD * GP, CH), BF)
    xs[:, PAD * GP + HALF :, :] = jnp.zeros((7, PAD * GP, CH), BF)
    total = jnp.zeros((1, CH), F32)
    for m in range(4):
        rows = pl.ds(m * 512, 512)
        chunk = x_ref[rows, :]
        wide = chunk.astype(F32)
        total = total + jnp.sum(wide, axis=0, keepdims=True)
        for slot, amount in enumerate(SHIFTS):
            xs[slot, pl.ds(PAD * GP + m * 512, 512), :] = column_shift(wide, amount).astype(BF)
    total8 = jnp.broadcast_to(total, (8, CH))
    colsum_ref[...] = total8
    pool = jnp.dot(total8, w[28].astype(F32), precision=HIGH, preferred_element_type=F32)
    hsum = jnp.broadcast_to(jnp.sum(hg_ref[...].astype(F32), axis=0, keepdims=True), (8, BR))
    extra = jnp.concatenate([pool, hsum, jnp.zeros((8, 512), F32)], axis=1)
    for s in range(GROUPS):
        p_ref[s, pl.ds(GP, 8), :] = extra
    for m in range(4):
        first = jnp.dot(x_ref[pl.ds(m * 512, 512), :], w[0], preferred_element_type=F32)
        for k in range(4):
            p_ref[4 * m + k, 0:GP, 0:BR] = first[k * GP : (k + 1) * GP]
        for j in range(3):
            steps = valid_steps(j, m, 1)
            left = jnp.concatenate(
                [xs[shift_slot(j, b), pl.ds((PAD + low) * GP, 512), :] for _, low in steps for b in range(3)], axis=1
            )
            start = 1 + 9 * j + 3 * steps[0][0]
            right = w[start : start + 3 * len(steps)].reshape(-1, BR)
            acc = jnp.dot(left, right, preferred_element_type=F32)
            for k in range(4):
                p_ref[4 * m + k, 0:GP, (j + 1) * BR : (j + 2) * BR] = acc[k * GP : (k + 1) * GP]


def turn_kernel(x_ref, xt_ref):
    for m in range(4):
        wide = x_ref[pl.ds(m * 512, 512), :].astype(F32)
        for slot, amount in enumerate(SHIFTS):
            xt_ref[slot, :, pl.ds(m * 512, 512)] = column_shift(wide, amount).T.astype(BF)


def middle_kernel(pre_ref, sums_ref, hg_ref, pw_ref, out_ref, gp_ref, gproj_ref, vec_ref):
    pre = pre_ref[0:GP, :]
    act = jnp.maximum(pre, 0.0).astype(BF)
    pool = sums_ref[:, 0:BR] * (1.0 / 4096.0)
    hsum = sums_ref[:, BR : 2 * BR]
    act4 = jnp.maximum(pool, 0.0).astype(BF)
    low = pw_ref[0:1024, :]
    high = pw_ref[1024:1280, :]
    const = jnp.dot(act4, high, preferred_element_type=F32)
    head = jnp.dot(act, low, preferred_element_type=F32) + const[0:1, :]
    out_ref[...] = head.astype(BF)
    hg = hg_ref[...]
    back = lax.dot_general(hg, low, (((1,), (1,)), ((), ())), preferred_element_type=F32)
    gp_ref[...] = jnp.where(pre > 0, back, 0.0).astype(BF)
    gproj_ref[...] = lax.dot_general(act, hg, (((0,), (0,)), ((), ())), preferred_element_type=F32).astype(BF)
    pool_grad = lax.dot_general(
        hsum, high.astype(F32), (((1,), (1,)), ((), ())), precision=HIGH, preferred_element_type=F32
    )
    vec_ref[:, 0:BR] = jnp.where(pool > 0, pool_grad, 0.0)
    vec_ref[:, BR : 2 * BR] = act4.astype(F32)
    vec_ref[:, 2 * BR : 3 * BR] = hsum


def backward_kernel(core_ref, xt_ref, g_ref, own, other, colsum_ref, vec_ref, dx_ref, dws_ref, dwo_ref, w, gpad, dw):
    c = core_ref[0]
    join_weights(c, own, other, w)
    gpad[0 : PAD * GP, :] = jnp.zeros((PAD * GP, 768), BF)
    gpad[PAD * GP + HALF :, :] = jnp.zeros((PAD * GP, 768), BF)
    gpad[PAD * GP : PAD * GP + HALF, :] = g_ref[:, BR:]
    dw[0] = jnp.dot(xt_ref[0], g_ref[:, 0:BR], preferred_element_type=F32)
    for j in range(3):
        cols = slice((j + 1) * BR, (j + 2) * BR)
        for a in range(3):
            delta = 3 * (j + 1) * (a - 1) * GP
            x_low, x_high = max(delta, 0), HALF + min(delta, 0)
            g_low, g_high = max(-delta, 0), HALF - max(delta, 0)
            left = jnp.concatenate([xt_ref[shift_slot(j, b), :, x_low:x_high] for b in range(3)], axis=0)
            part = jnp.dot(left, g_ref[g_low:g_high, cols], preferred_element_type=F32)
            start = 1 + 9 * j + 3 * a
            dw[start : start + 3] = part.reshape(3, CH, BR)
    pool_grad = vec_ref[:, 0:BR]
    dw[28] = lax.dot_general(
        colsum_ref[...], pool_grad, (((0,), (0,)), ((), ())), precision=HIGH, preferred_element_type=F32
    ) * (0.125 / 4096.0)
    field = lax.dot_general(
        pool_grad, w[28].astype(F32), (((1,), (1,)), ((), ())), precision=HIGH, preferred_element_type=F32
    )[0:1, :] * (1.0 / 4096.0)
    for m in range(4):
        rows = pl.ds(m * 512, 512)
        acc = field + lax.dot_general(
            g_ref[rows, 0:BR], w[0], (((1,), (1,)), ((), ())), preferred_element_type=F32
        )
        for j in range(3):
            steps = valid_steps(j, m, -1)
            left = jnp.concatenate([gpad[pl.ds((PAD + low) * GP, 512), j * BR : (j + 1) * BR] for _, low in steps], axis=1)
            right = jnp.concatenate(
                [w[1 + 9 * j + 3 * a : 4 + 9 * j + 3 * a].reshape(3 * CH, BR) for a, _ in steps], axis=1
            )
            spread = lax.dot_general(left, right, (((1,), (1,)), ((), ())), preferred_element_type=F32)
            for b in range(3):
                acc = acc + column_shift(spread[:, b * CH : (b + 1) * CH], -(b - 1) * 12 * (j + 1))
        low, high = acc[:, 0:64], acc[:, 64:128]
        dx_ref[0, rows, :] = jnp.where(c == 0, low, high).astype(BF)
        dx_ref[1, rows, :] = jnp.where(c == 0, high, low).astype(BF)
    dws_ref[...] = dw[:, pl.ds(pl.multiple_of(c * 64, 64), 64), :]
    dwo_ref[...] = dw[:, pl.ds(pl.multiple_of((1 - c) * 64, 64), 64), :].astype(BF)


def call(kernel, out_shape, scratch, flops, *args, scalar=False):
    specs = [pl.BlockSpec(memory_space=pltpu.VMEM) for _ in args]
    if scalar:
        specs[0] = pl.BlockSpec(memory_space=pltpu.SMEM)
    moved = sum(a.size * a.dtype.itemsize for a in jax.tree.leaves((args, out_shape)))
    return pl.pallas_call(
        kernel,
        out_shape=out_shape,
        in_specs=specs,
        out_specs=jax.tree.map(lambda _: pl.BlockSpec(memory_space=pltpu.VMEM), out_shape),
        scratch_shapes=scratch,
        compiler_params=pltpu.CompilerParams(vmem_limit_bytes=56 * 2**20),
        cost_estimate=pl.CostEstimate(flops=flops, bytes_accessed=moved, transcendentals=0),
    )(*args)


def swap(value):
    return lax.ppermute(value, "core", [(0, 1), (1, 0)])


def local(features, head_grad, branch_weight, proj_weight):
    shape = jax.ShapeDtypeStruct
    plane = ("z", "y")
    core = lax.axis_index("core").astype(jnp.int32).reshape(1)
    other = swap(branch_weight)
    grouped = features.reshape(GP, GROUPS, CH).transpose(1, 0, 2)
    x = lax.all_to_all(grouped, plane, split_axis=0, concat_axis=0, tiled=True).reshape(HALF, CH)
    hg = head_grad.reshape(GP, BR)
    sums, colsum = call(
        forward_kernel,
        (shape((GROUPS, GP + 8, 1024), F32), shape((8, CH), F32)),
        [pltpu.VMEM((29, CH, BR), BF), pltpu.VMEM((7, HALF + 2 * PAD * GP, CH), BF)],
        4 * 10**9,
        core, x, hg, branch_weight, other, scalar=True,
    )
    pre = lax.psum_scatter(sums, plane, scatter_dimension=0, tiled=True)[0]
    turned = call(turn_kernel, shape((7, CH, HALF), BF), [], 10**8, x)
    vectors = pre[GP:, 0:512]
    vectors = vectors + swap(vectors)
    head_out, gp, gproj, vec = call(
        middle_kernel,
        (shape((GP, BR), BF), shape((GP, 1024), BF), shape((1024, BR), BF), shape((8, 768), F32)),
        [], 2 * 10**8,
        pre, vectors, hg, proj_weight,
    )
    every = lax.all_gather(gp, plane, axis=0, tiled=True)
    part = lax.all_to_all(gproj.reshape(GROUPS, 64, BR), plane, split_axis=0, concat_axis=0, tiled=True)
    part = jnp.sum(part.astype(F32), axis=0)
    part = part + swap(part)
    part = part + lax.ppermute(part, "rep", [(0, 1), (1, 0), (2, 3), (3, 2)])
    part = part + lax.ppermute(part, "rep", [(0, 2), (2, 0), (1, 3), (3, 1)])
    spread = jnp.broadcast_to(part.astype(BF)[None], (GROUPS, 64, BR))
    spread = lax.all_to_all(spread, plane, split_axis=0, concat_axis=0, tiled=True).reshape(1024, BR)
    slabs = lax.all_gather(vec[0, BR:].reshape(2, BR), "rep", axis=0, tiled=False)
    last = jnp.einsum("sa,sb->ab", slabs[:, 0], slabs[:, 1], precision=HIGH)
    grad_proj = jnp.concatenate([spread.astype(F32), last], axis=0)
    dx, dws, dwo = call(
        backward_kernel,
        (shape((2, HALF, 64), BF), shape((29, 64, BR), F32), shape((29, 64, BR), BF)),
        [pltpu.VMEM((29, CH, BR), BF), pltpu.VMEM((HALF + 2 * PAD * GP, 768), BF), pltpu.VMEM((29, CH, BR), F32)],
        8 * 10**9,
        core, turned, every, branch_weight, other, colsum, vec, scalar=True,
    )
    mine, theirs = dx[0], swap(dx[1])
    first = jnp.where(core[0] == 0, mine, theirs).reshape(GROUPS, 1, 2, COLS, 64)
    second = jnp.where(core[0] == 0, theirs, mine).reshape(GROUPS, 1, 2, COLS, 64)
    grad_features = jnp.concatenate([first, second], axis=1).reshape(1, 64, COLS, 64)
    dw = (dws + swap(dwo).astype(F32)).astype(BF).reshape(4, 464, BR)
    dw = lax.all_to_all(dw, "rep", split_axis=0, concat_axis=0, tiled=True)
    dw = jnp.sum(dw.astype(F32), axis=0).astype(BF)
    grad_branch = lax.all_gather(dw, "rep", axis=0, tiled=True).astype(F32).reshape(29, 64, BR)
    return head_out.reshape(head_grad.shape), grad_features, grad_branch, grad_proj


def solution(mesh):
    fine = Mesh(mesh.devices.reshape(4, 4, 2, 4), ("z", "y", "core", "rep"))
    tile = ("z", "y", "core")
    return jax.shard_map(
        local,
        mesh=fine,
        in_specs=(P("rep", tile, None, None), P("rep", tile, None, None), P(None, tile, None), P()),
        out_specs=(P("rep", tile, None, None), P("rep", None, None, tile), P(None, tile, None), P()),
        check_vma=False,
    )
```

```python
import jax
import jax.numpy as jnp
from jax import lax
from jax.experimental import pallas as pl
from jax.experimental.pallas import tpu as pltpu
from jax.sharding import Mesh, PartitionSpec as P

GROUPS = 16
CH = 128
KCH = 512
BR = 256
HALF = 2048
PAD = 9
CUT = 15
SHIFTS = (0, -3, 3, -6, 6, -9, 9)
F32 = jnp.float32
BF = jnp.bfloat16
HIGH = lax.Precision.HIGHEST
ROWS_BY_COLS = (((1,), (1,)), ((), ()))
COLS_BY_COLS = (((0,), (0,)), ((), ()))


def shift_slot(j, b):
    return SHIFTS.index((b - 1) * 3 * (j + 1))


def column_shift(value, amount):
    if amount == 0:
        return value
    n = value.shape[0]
    col = lax.broadcasted_iota(jnp.int32, value.shape, 0) & 15
    rolled = pltpu.roll(value, (-amount) % n, 0)
    return jnp.where((col + amount >= 0) & (col + amount < 16), rolled, 0.0)


def wrap(value):
    return lax.rem(value + 8, 4)


def split_kernel(x_ref, hg_ref, first_ref, second_ref, wide):
    for t in range(GROUPS):
        wide[t] = x_ref[:, CH * t : CH * (t + 1)].astype(F32)
    for t in range(2):
        wide[GROUPS + t] = hg_ref[:, CH * t : CH * (t + 1)].astype(F32)
    for v in range(4):
        for t in range(GROUPS + 2):
            part = wide[t, pl.ds(v, 32, stride=4), :].astype(BF)
            if t < GROUPS:
                second_ref[t, 16 * v : 16 * (v + 1), :] = part[0:16]
                second_ref[t, 64 + 16 * v : 80 + 16 * v, :] = part[16:32]
                place = CH * (t % 4)
                first_ref[4 * (t // 4) + v, :, place : place + CH] = part
            else:
                place = KCH + CH * (t - GROUPS)
                for z in range(4):
                    first_ref[4 * z + v, :, place : place + CH] = part


def weight_copies(pos_ref, blocks, w, sem):
    y, c = pos_ref[1], pos_ref[2]
    places = [(0, 0, 29), (-1, 0, 29), (1, 0, 29), (2, 0, CUT), (2, CUT, 29)]
    copies = []
    for side in range(2):
        for k, (step, low, high) in enumerate(places):
            core = c if side == 0 else 1 - c
            start = pl.multiple_of(wrap(y + step) * CH + core * 64, 64)
            n = len(copies)
            copies.append(
                pltpu.make_async_copy(blocks[n], w.at[pl.ds(low, high - low), pl.ds(start, 64), :], sem.at[n])
            )
    return copies


def forward_kernel(pos_ref, x_ref, hg_ref, *refs):
    blocks, outs, (w, xs, total, sem) = refs[:10], refs[10:15], refs[15:]
    own_ref, plus_ref, minus_ref, plus_half, minus_half = outs
    copies = weight_copies(pos_ref, blocks, w, sem)
    for copy in copies:
        copy.start()
    wide = x_ref[:, 0:KCH].astype(F32)
    colsum = jnp.broadcast_to(jnp.sum(wide, axis=0, keepdims=True), (8, KCH))
    for slot, amount in enumerate(SHIFTS):
        if amount:
            xs[slot] = column_shift(wide, amount).astype(BF)
        else:
            xs[slot] = x_ref[:, 0:KCH]
    hsum = jnp.broadcast_to(jnp.sum(hg_ref[...].astype(F32), axis=0, keepdims=True), (8, BR))
    for copy in copies:
        copy.wait()
    pool = jnp.dot(colsum, w[28].astype(F32), precision=HIGH, preferred_element_type=F32)
    total[:, 0:BR] = jnp.dot(xs[0], w[0], preferred_element_type=F32)
    for j in range(3):
        cols = slice((j + 1) * BR, (j + 2) * BR)
        for a in (1, 0, 2):
            delta = 96 * (j + 1) * (a - 1)
            in_low, in_high = max(delta, 0), 512 + min(delta, 0)
            out_low, out_high = max(-delta, 0), 512 - max(delta, 0)
            left = jnp.concatenate([xs[shift_slot(j, b), in_low:in_high, :] for b in range(3)], axis=1)
            start = 1 + 9 * j + 3 * a
            part = jnp.dot(left, w[start : start + 3].reshape(3 * KCH, BR), preferred_element_type=F32)
            if a == 1:
                total[:, cols] = part
            else:
                total[out_low:out_high, cols] += part
    extra = jnp.concatenate([pool, hsum, jnp.zeros((8, 512), F32)], axis=1)
    z = pos_ref[0]

    def rows(step, low, size):
        return total[pl.ds(pl.multiple_of(wrap(z + step) * 128 + low, 64), size), :]

    own_ref[0:128, :] = rows(0, 0, 128)
    own_ref[128:136, :] = extra
    plus_ref[0:64, :] = rows(2, 0, 64)
    plus_ref[64:128, :] = rows(1, 64, 64)
    plus_ref[128:136, :] = extra
    minus_ref[0:64, :] = rows(2, 64, 64)
    minus_ref[64:72, :] = extra
    minus_ref[72:136, :] = rows(-1, 0, 64)
    plus_half[...] = rows(1, 0, 64)
    minus_half[0:64, :] = rows(-1, 64, 64)
    minus_half[64:72, :] = extra


def turn_kernel(x_ref, xt_ref, colsum_ref):
    total = jnp.zeros((1, CH), F32)
    for m in range(4):
        wide = x_ref[pl.ds(m * 512, 512), :].astype(F32)
        total = total + jnp.sum(wide, axis=0, keepdims=True)
        for slot, amount in enumerate(SHIFTS):
            xt_ref[slot, :, pl.ds(m * 512, 512)] = column_shift(wide, amount).T.astype(BF)
    colsum_ref[...] = jnp.broadcast_to(total, (8, CH))


def middle_kernel(pos_ref, own, from_low, from_high, half_a, half_b, x_ref, pw_ref, _, keep_ref, give_ref, pay_ref):
    top = own[0:64, :] + from_high[72:136, :] + half_a[...]
    bottom = own[64:136, :] + from_low[64:136, :] + half_b[...]
    pre = jnp.concatenate([top, bottom[0:64, :]], axis=0)
    act = jnp.maximum(pre, 0.0).astype(BF)
    low = pw_ref[0:1024, :]
    hg = x_ref[pl.ds(pl.multiple_of(pos_ref[0] * 128, 128), 128), KCH:]
    back = lax.dot_general(hg, low, ROWS_BY_COLS, preferred_element_type=F32)
    grads = jnp.where(pre > 0, back, 0.0)
    first = pos_ref[2] == 0
    keep_ref[0:8] = jnp.where(first, grads[:, 0:512], grads[:, 512:1024]).astype(BF).reshape(8, 16, 512)
    give_ref[0:8] = jnp.where(first, grads[:, 512:1024], grads[:, 0:512]).astype(BF).reshape(8, 16, 512)
    sums = jnp.concatenate([bottom[64:72, 0:512]] * 2, axis=0)
    one = sums.astype(BF).astype(F32)
    two = (sums - one).astype(BF).astype(F32)
    row = lax.broadcasted_iota(jnp.int32, sums.shape, 0)
    terms = jnp.where(row == 0, one, jnp.where(row == 1, two, jnp.where(row == 2, sums - one - two, 0.0))).astype(BF)
    keep_ref[8] = terms
    give_ref[8] = terms
    head = jnp.dot(act, low, preferred_element_type=F32).astype(BF)
    proj = lax.dot_general(act, hg, COLS_BY_COLS, preferred_element_type=F32).astype(BF)
    for t in range(GROUPS):
        pay_ref[t, 0:64, :] = proj[64 * t : 64 * (t + 1), :]
        pay_ref[t, 64:96, :] = head[32 * (t % 4) : 32 * (t % 4 + 1), :]


def pool_kernel(pos_ref, sums_ref, pw_ref, const_ref, grad_ref, outer_ref, whole):
    pool = sums_ref[:, 0:BR] * (1.0 / 4096.0)
    hsum = sums_ref[:, BR : 2 * BR]
    act = jnp.maximum(pool, 0.0).astype(BF)
    high = pw_ref[1024:1280, :]
    const_ref[...] = jnp.dot(act, high, preferred_element_type=F32)
    grad = lax.dot_general(hsum, high.astype(F32), ROWS_BY_COLS, precision=HIGH, preferred_element_type=F32)
    grad_ref[...] = jnp.where(pool > 0, grad, 0.0)
    whole[...] = 0.125 * lax.dot_general(
        act.astype(F32), hsum, COLS_BY_COLS, precision=HIGH, preferred_element_type=F32
    )
    chunk = pos_ref[0] * 4 + pos_ref[1]
    outer_ref[...] = whole[pl.ds(pl.multiple_of(chunk * 16, 16), 16), :]


def collect_kernel(pos_ref, pay_ref, const_ref, part_ref, head_ref, wide):
    total = pay_ref[0, 0:64, :].astype(F32)
    for t in range(1, GROUPS):
        total = total + pay_ref[t, 0:64, :].astype(F32)
    part_ref[...] = total
    for v in range(4):
        piece = pay_ref[4 * pos_ref[0] + v, 64:96, :].astype(F32) + const_ref[0:1, :]
        wide[0, pl.ds(v, 32, stride=4), :] = piece[:, 0:128]
        wide[1, pl.ds(v, 32, stride=4), :] = piece[:, 128:256]
    head_ref[:, 0:128] = wide[0].astype(BF)
    head_ref[:, 128:256] = wide[1].astype(BF)


def gather_copies(pos_ref, blocks, g, sem, pad):
    z, y, c = pos_ref[0], pos_ref[1], pos_ref[2]
    copies = []
    for side in range(2):
        half = c if side == 0 else 1 - c
        for place, far in enumerate((0, -1, 1, 2)):
            for k, step in enumerate((0, -1, 1, 2)):
                src = blocks[8 * side + 2 * place + k // 2].at[k % 2, side]
                v = wrap(y + jnp.where(half == 0, step, far))
                group = wrap(z + jnp.where(half == 0, far, step))
                cols = pl.ds(pl.multiple_of(512 * half, 512), 512)
                dst = g.at[pl.ds(2 * pad + 8 * group, 8), v, :, cols]
                copies.append(pltpu.make_async_copy(src, dst, sem.at[len(copies)]))
    return copies


def weight_grad_kernel(pos_ref, xt_ref, colsum_ref, grad_ref, *refs):
    blocks, (own_ref, other_ref), (g, dw, sem) = refs[:16], refs[-5:-3], refs[-3:]
    copies = gather_copies(pos_ref, blocks, g, sem, 0)
    for copy in copies:
        copy.start()
    for copy in copies:
        copy.wait()

    def grads(low, high, cols):
        return g[low // 64 : high // 64, :, :, cols].reshape(high - low, BR)

    dw[0] = jnp.dot(xt_ref[0], grads(0, HALF, slice(0, BR)), preferred_element_type=F32)
    for j in range(3):
        cols = slice((j + 1) * BR, (j + 2) * BR)
        for a in range(3):
            delta = 3 * (j + 1) * (a - 1) * 128
            x_low, x_high = max(delta, 0), HALF + min(delta, 0)
            g_low, g_high = max(-delta, 0), HALF - max(delta, 0)
            left = jnp.concatenate([xt_ref[shift_slot(j, b), :, x_low:x_high] for b in range(3)], axis=0)
            part = jnp.dot(left, grads(g_low, g_high, cols), preferred_element_type=F32)
            start = 1 + 9 * j + 3 * a
            dw[start : start + 3] = part.reshape(3, CH, BR)
    dw[28] = lax.dot_general(
        colsum_ref[...], grad_ref[...], COLS_BY_COLS, precision=HIGH, preferred_element_type=F32
    ) * (0.125 / 4096.0)
    c = pos_ref[2]
    own_ref[...] = dw[:, pl.ds(pl.multiple_of(c * 64, 64), 64), :].astype(BF)
    other_ref[...] = dw[:, pl.ds(pl.multiple_of((1 - c) * 64, 64), 64), :].astype(BF)


def field_grad_kernel(pos_ref, grad_ref, own, other, *refs):
    blocks, dx_ref, (g, w, whole, sem) = refs[:16], refs[-5], refs[-4:]
    copies = gather_copies(pos_ref, blocks, g, sem, PAD)
    for copy in copies:
        copy.start()
    c = pos_ref[2]
    w[:, pl.ds(pl.multiple_of(c * 64, 64), 64), :] = own[...]
    w[:, pl.ds(pl.multiple_of((1 - c) * 64, 64), 64), :] = other[...]
    g[0 : 2 * PAD] = jnp.zeros((2 * PAD, 4, 16, 1024), BF)
    g[2 * (PAD + GROUPS) :] = jnp.zeros((2 * PAD, 4, 16, 1024), BF)
    field = lax.dot_general(
        grad_ref[...], w[28].astype(F32), ROWS_BY_COLS, precision=HIGH, preferred_element_type=F32
    )[0:1, :] * (1.0 / 4096.0)
    for copy in copies:
        copy.wait()

    def grads(low, cols):
        return g[2 * (PAD + low) : 2 * (PAD + low + 4), :, :, cols].reshape(512, BR)

    for m in range(4):
        acc = field + lax.dot_general(
            grads(4 * m, slice(0, BR)), w[0], ROWS_BY_COLS, preferred_element_type=F32
        )
        for j in range(3):
            steps = []
            for a in range(3):
                low = 4 * m - 3 * (j + 1) * (a - 1)
                if low + 3 >= 0 and low < GROUPS:
                    steps.append((a, low))
            left = jnp.concatenate([grads(low, slice((j + 1) * BR, (j + 2) * BR)) for _, low in steps], axis=1)
            right = jnp.concatenate(
                [w[1 + 9 * j + 3 * a : 4 + 9 * j + 3 * a].reshape(3 * CH, BR) for a, _ in steps], axis=1
            )
            spread = lax.dot_general(left, right, ROWS_BY_COLS, preferred_element_type=F32)
            for b in range(3):
                acc = acc + column_shift(spread[:, b * CH : (b + 1) * CH], -(b - 1) * 3 * (j + 1))
        for row in range(8):
            for v in range(4):
                place = (4 * row + v) * 16
                whole[pl.ds(512 * m + 64 * row + v, 16, stride=4), :] = acc[place : place + 16, :]
    low, high = whole[:, 0:64], whole[:, 64:128]
    dx_ref[0] = jnp.where(c == 0, low, high).astype(BF)
    dx_ref[1] = jnp.where(c == 0, high, low).astype(BF)


def add_kernel(pos_ref, own, other, *outs):
    r = pos_ref[3]
    for k in range(4):
        rows = pl.ds(pl.multiple_of(wrap(r + k) * 464, 16), 464)
        outs[k][...] = (own[rows, :].astype(F32) + other[rows, :].astype(F32)).astype(BF)


def join_kernel(pos_ref, own, below, above, far_low, far_high, out_ref):
    r = pos_ref[3]

    def place(step, low, size):
        return pl.ds(pl.multiple_of(wrap(r + step) * 464 + low, 8), size)

    out_ref[place(0, 0, 464), :] = own[...].astype(F32)
    out_ref[place(-1, 0, 464), :] = below[...].astype(F32)
    out_ref[place(1, 0, 464), :] = above[...].astype(F32)
    out_ref[place(2, 0, 240), :] = far_low[...].astype(F32)
    out_ref[place(2, 240, 224), :] = far_high[...].astype(F32)


def call(kernel, out_shape, scratch, flops, *args, scalar=True, raw=0):
    specs = [pl.BlockSpec(memory_space=pltpu.VMEM) for _ in args]
    if scalar:
        specs[0] = pl.BlockSpec(memory_space=pltpu.SMEM)
    for k in range(raw):
        specs[len(args) - 1 - k] = pl.BlockSpec(memory_space=pl.ANY)
    moved = sum(a.size * a.dtype.itemsize for a in jax.tree.leaves((args, out_shape)))
    return pl.pallas_call(
        kernel,
        out_shape=out_shape,
        in_specs=specs,
        out_specs=jax.tree.map(lambda _: pl.BlockSpec(memory_space=pltpu.VMEM), out_shape),
        scratch_shapes=scratch,
        compiler_params=pltpu.CompilerParams(vmem_limit_bytes=60 * 2**20),
        cost_estimate=pl.CostEstimate(flops=flops, bytes_accessed=moved, transcendentals=0),
    )(*args)


def gate(values, after):
    anywhere = pl.BlockSpec(memory_space=pl.ANY)
    return pl.pallas_call(
        lambda *refs: None,
        out_shape=tuple(jax.ShapeDtypeStruct(v.shape, v.dtype) for v in values),
        in_specs=[anywhere] * (len(values) + len(after)),
        out_specs=(anywhere,) * len(values),
        input_output_aliases={k: k for k in range(len(values))},
        cost_estimate=pl.CostEstimate(flops=0, bytes_accessed=0, transcendentals=0),
    )(*values, *after)


def swap(value):
    return lax.ppermute(value, "core", [(0, 1), (1, 0)])


def send(value, axis, step):
    return lax.ppermute(value, axis, [(k, (k + step) % 4) for k in range(4)])


def pair(value, axis, bit):
    return lax.ppermute(value, axis, [(k, k ^ bit) for k in range(4)])


def cross(value, step, turn):
    pairs = []
    for z in range(4):
        for y in range(4):
            for c in range(2):
                along_y = (c == 0) != turn
                to = (z, (y + step) % 4) if along_y else ((z + step) % 4, y)
                pairs.append(((4 * z + y) * 2 + c, (4 * to[0] + to[1]) * 2 + c))
    return lax.ppermute(value, ("z", "y", "core"), pairs)


def local(features, head_grad, branch_weight, proj_weight):
    shape = jax.ShapeDtypeStruct
    plane = ("z", "y")
    pos = jnp.stack([lax.axis_index(n).astype(jnp.int32) for n in ("z", "y", "core", "rep")])

    def exchange(value):
        return lax.all_to_all(value, plane, split_axis=0, concat_axis=0, tiled=True)

    first, second = call(
        split_kernel,
        (shape((GROUPS, 32, KCH + BR), BF), shape((GROUPS, 128, CH), BF)),
        [pltpu.VMEM((GROUPS + 2, 128, CH), F32)], 10**6,
        features.reshape(128, 2048), head_grad.reshape(128, BR), scalar=False,
    )
    below, above = send(branch_weight, "y", 1), send(branch_weight, "y", -1)
    x = exchange(first).reshape(512, KCH + BR)
    below, above = gate((below, above), (x,))
    blocks = [branch_weight, below, above, send(below[0:CUT], "y", 1), send(above[CUT:29], "y", -1)]
    blocks = blocks + [swap(b) for b in blocks]
    own, plus, minus, plus_half, minus_half = call(
        forward_kernel,
        tuple(shape((n, 1024), F32) for n in (136, 136, 136, 64, 72)),
        [
            pltpu.VMEM((29, KCH, BR), BF), pltpu.VMEM((7, 512, KCH), BF), pltpu.VMEM((512, 1024), F32),
            pltpu.SemaphoreType.DMA((10,)),
        ],
        4 * 10**9, pos, x, head_grad.reshape(128, BR), *blocks, raw=10,
    )
    from_low, from_high = send(plus, "z", 1), send(minus, "z", -1)
    half_a = send(plus_half + from_low[0:64], "z", 1)
    half_b = send(minus_half + from_high[0:72], "z", -1)
    (second,) = gate((second,), (own,))
    turned, colsum = call(
        turn_kernel, (shape((7, CH, HALF), BF), shape((8, CH), F32)), [], 10**8,
        exchange(second).reshape(HALF, CH), scalar=False,
    )
    keep, give, pay = call(
        middle_kernel,
        (shape((9, 16, 512), BF), shape((9, 16, 512), BF), shape((GROUPS, 96, BR), BF)),
        [], 2 * 10**8, pos, own, from_low, from_high, half_a, half_b, x, proj_weight, turned, raw=1,
    )
    block = jnp.stack([keep, swap(give)])
    near = [block, cross(block, 1, False), cross(block, -1, False), cross(block, 2, False)]
    low = jnp.stack([near[0][:, 0:8], near[1][:, 0:8]])
    high = jnp.stack([near[2][:, 0:8], near[3][:, 0:8]])
    low_below, high_above = cross(low, 1, True), cross(high, -1, True)
    high_below, low_above = cross(high, 1, True), cross(low, -1, True)
    every = [
        low, high, low_below, high_below, low_above, high_above, cross(low_below, 1, True), cross(high_above, -1, True)
    ]
    every = every + [swap(piece) for piece in every]
    sums = jnp.sum(jnp.stack([piece[:, 8] for piece in near]).astype(F32), axis=(0, 1, 2))
    sums = jnp.broadcast_to(sums[None], (8, 512))
    sums = jnp.where(pos[2] == 0, sums, swap(sums))
    const, pool_grad, outer = call(
        pool_kernel, (shape((8, BR), F32), shape((8, BR), F32), shape((16, BR), F32)), [pltpu.VMEM((256, BR), F32)],
        10**7, pos, sums, proj_weight,
    )
    (pay,) = gate((pay,), (low, high))
    part, head_out = call(
        collect_kernel, (shape((64, BR), F32), shape((128, BR), BF)), [pltpu.VMEM((2, 128, 128), F32)],
        10**6, pos, exchange(pay), const,
    )
    part = jnp.concatenate([part + swap(part), outer], axis=0)
    part = part + pair(part, "rep", 1)
    part = part + pair(part, "rep", 2)
    part = exchange(jnp.broadcast_to(part.astype(BF)[None], (GROUPS, 80, BR))).astype(F32)
    grad_proj = jnp.concatenate([part[:, 0:64].reshape(1024, BR), part[:, 64:80].reshape(256, BR)], axis=0)
    dw, dw_other = call(
        weight_grad_kernel,
        (shape((29, 64, BR), BF), shape((29, 64, BR), BF)),
        [pltpu.VMEM((2 * GROUPS, 4, 16, 1024), BF), pltpu.VMEM((29, CH, BR), F32), pltpu.SemaphoreType.DMA((32,))],
        4 * 10**9, pos, turned, colsum, pool_grad, *every, raw=16,
    )
    quarters = call(
        add_kernel, (shape((464, BR), BF),) * 4, [], 10**6, pos, dw.reshape(1856, BR), swap(dw_other).reshape(1856, BR)
    )
    dx = call(
        field_grad_kernel,
        shape((2, HALF, 64), BF),
        [
            pltpu.VMEM((2 * (GROUPS + 2 * PAD), 4, 16, 1024), BF), pltpu.VMEM((29, CH, BR), BF),
            pltpu.VMEM((HALF, CH), F32), pltpu.SemaphoreType.DMA((32,)),
        ],
        4 * 10**9, pos, pool_grad, branch_weight, blocks[5], *every, quarters[0], raw=17,
    )
    terms = [quarters[0]] + [send(quarters[k], "rep", k) for k in (1, 3, 2)]
    dw = sum(term.astype(F32) for term in terms).astype(BF)
    below, above = send(dw, "rep", 1), send(dw, "rep", -1)
    far_low, far_high = send(below[0:240], "rep", 1), send(above[240:464], "rep", -1)
    grad_branch = call(
        join_kernel, shape((1856, BR), F32), [], 10**6, pos, dw, below, above, far_low, far_high
    ).reshape(29, 64, BR)
    mine, theirs = dx[0], swap(dx[1])
    even = jnp.where(pos[2] == 0, mine, theirs).reshape(GROUPS, 1, 2, 64, 64)
    odd = jnp.where(pos[2] == 0, theirs, mine).reshape(GROUPS, 1, 2, 64, 64)
    grad_features = jnp.concatenate([even, odd], axis=1).reshape(1, 64, 64, 64)
    return head_out.reshape(head_grad.shape), grad_features, grad_branch, grad_proj


def solution(mesh):
    fine = Mesh(mesh.devices.reshape(4, 4, 2, 4), ("z", "y", "core", "rep"))
    tile = ("z", "y", "core")
    return jax.shard_map(
        local,
        mesh=fine,
        in_specs=(P("rep", tile, None, None), P("rep", tile, None, None), P(None, tile, None), P()),
        out_specs=(P("rep", tile, None, None), P("rep", None, None, tile), P(None, tile, None), P()),
        check_vma=False,
    )
```

```python
import jax
import jax.numpy as jnp
from jax import lax
from jax.experimental import pallas as pl
from jax.experimental.pallas import tpu as pltpu
from jax.sharding import Mesh, PartitionSpec as P

GROUPS = 16
CH = 128
KCH = 512
BR = 256
HALF = 2048
PAD = 9
CUT = 15
SHIFTS = (0, -3, 3, -6, 6, -9, 9)
F32 = jnp.float32
BF = jnp.bfloat16
HIGH = lax.Precision.HIGHEST
ROWS_BY_COLS = (((1,), (1,)), ((), ()))
COLS_BY_COLS = (((0,), (0,)), ((), ()))


def shift_slot(j, b):
    return SHIFTS.index((b - 1) * 3 * (j + 1))


def column_shift(value, amount):
    if amount == 0:
        return value
    n = value.shape[0]
    col = lax.broadcasted_iota(jnp.int32, value.shape, 0) & 15
    rolled = pltpu.roll(value, (-amount) % n, 0)
    return jnp.where((col + amount >= 0) & (col + amount < 16), rolled, 0.0)


def wrap(value):
    return lax.rem(value + 8, 4)


def split_kernel(x_ref, hg_ref, first_ref, second_ref, wide):
    for t in range(GROUPS):
        wide[t] = x_ref[:, CH * t : CH * (t + 1)].astype(F32)
    for t in range(2):
        wide[GROUPS + t] = hg_ref[:, CH * t : CH * (t + 1)].astype(F32)
    for v in range(4):
        for t in range(GROUPS + 2):
            part = wide[t, pl.ds(v, 32, stride=4), :].astype(BF)
            if t < GROUPS:
                second_ref[t, 16 * v : 16 * (v + 1), :] = part[0:16]
                second_ref[t, 64 + 16 * v : 80 + 16 * v, :] = part[16:32]
                place = CH * (t % 4)
                first_ref[4 * (t // 4) + v, :, place : place + CH] = part
            else:
                place = KCH + CH * (t - GROUPS)
                for z in range(4):
                    first_ref[4 * z + v, :, place : place + CH] = part


def weight_copies(pos_ref, blocks, w, sem):
    y, c = pos_ref[1], pos_ref[2]
    places = [(0, 0, 29), (-1, 0, 29), (1, 0, 29), (2, 0, CUT), (2, CUT, 29)]
    copies = []
    for side in range(2):
        for k, (step, low, high) in enumerate(places):
            core = c if side == 0 else 1 - c
            start = pl.multiple_of(wrap(y + step) * CH + core * 64, 64)
            n = len(copies)
            copies.append(
                pltpu.make_async_copy(blocks[n], w.at[pl.ds(low, high - low), pl.ds(start, 64), :], sem.at[n])
            )
    return copies


def forward_kernel(pos_ref, x_ref, hg_ref, *refs):
    blocks, outs, (w, xs, total, sem) = refs[:10], refs[10:15], refs[15:]
    own_ref, plus_ref, minus_ref, plus_half, minus_half = outs
    copies = weight_copies(pos_ref, blocks, w, sem)
    for copy in copies:
        copy.start()
    wide = x_ref[:, 0:KCH].astype(F32)
    colsum = jnp.broadcast_to(jnp.sum(wide, axis=0, keepdims=True), (8, KCH))
    for slot, amount in enumerate(SHIFTS):
        if amount:
            xs[slot] = column_shift(wide, amount).astype(BF)
        else:
            xs[slot] = x_ref[:, 0:KCH]
    hsum = jnp.broadcast_to(jnp.sum(hg_ref[...].astype(F32), axis=0, keepdims=True), (8, BR))
    for copy in copies:
        copy.wait()
    pool = jnp.dot(colsum, w[28].astype(F32), precision=HIGH, preferred_element_type=F32)
    total[:, 0:BR] = jnp.dot(xs[0], w[0], preferred_element_type=F32)
    for j in range(3):
        cols = slice((j + 1) * BR, (j + 2) * BR)
        for a in (1, 0, 2):
            delta = 96 * (j + 1) * (a - 1)
            in_low, in_high = max(delta, 0), 512 + min(delta, 0)
            out_low, out_high = max(-delta, 0), 512 - max(delta, 0)
            left = jnp.concatenate([xs[shift_slot(j, b), in_low:in_high, :] for b in range(3)], axis=1)
            start = 1 + 9 * j + 3 * a
            part = jnp.dot(left, w[start : start + 3].reshape(3 * KCH, BR), preferred_element_type=F32)
            if a == 1:
                total[:, cols] = part
            else:
                total[out_low:out_high, cols] += part
    extra = jnp.concatenate([pool, hsum, jnp.zeros((8, 512), F32)], axis=1)
    z = pos_ref[0]

    def rows(step, low, size):
        return total[pl.ds(pl.multiple_of(wrap(z + step) * 128 + low, 64), size), :]

    own_ref[0:128, :] = rows(0, 0, 128)
    own_ref[128:136, :] = extra
    plus_ref[0:64, :] = rows(2, 0, 64)
    plus_ref[64:128, :] = rows(1, 64, 64)
    plus_ref[128:136, :] = extra
    minus_ref[0:64, :] = rows(2, 64, 64)
    minus_ref[64:72, :] = extra
    minus_ref[72:136, :] = rows(-1, 0, 64)
    plus_half[...] = rows(1, 0, 64)
    minus_half[0:64, :] = rows(-1, 64, 64)
    minus_half[64:72, :] = extra


def pair_kernel(first_ref, second_ref, out_ref):
    out_ref[0] = first_ref[...]
    out_ref[1] = second_ref[...]


def stack_kernel(first_ref, second_ref, out_ref, sums_ref):
    total = jnp.zeros((16, 512), F32)
    for k, ref in enumerate((first_ref, second_ref)):
        for side in range(2):
            out_ref[k, side] = ref[side, 0:8]
            total = total + ref[side, 8].astype(F32)
    sums_ref[...] = jnp.broadcast_to(jnp.sum(total, axis=0, keepdims=True), (8, 512))


def turn_kernel(x_ref, xt_ref, colsum_ref):
    total = jnp.zeros((1, CH), F32)
    for m in range(4):
        wide = x_ref[pl.ds(m * 512, 512), :].astype(F32)
        total = total + jnp.sum(wide, axis=0, keepdims=True)
        for slot, amount in enumerate(SHIFTS):
            xt_ref[slot, :, pl.ds(m * 512, 512)] = column_shift(wide, amount).T.astype(BF)
    colsum_ref[...] = jnp.broadcast_to(total, (8, CH))


def middle_kernel(pos_ref, own, from_low, from_high, half_a, half_b, x_ref, pw_ref, _, keep_ref, give_ref, pay_ref):
    top = own[0:64, :] + from_high[72:136, :] + half_a[...]
    bottom = own[64:136, :] + from_low[64:136, :] + half_b[...]
    pre = jnp.concatenate([top, bottom[0:64, :]], axis=0)
    act = jnp.maximum(pre, 0.0).astype(BF)
    low = pw_ref[0:1024, :]
    hg = x_ref[pl.ds(pl.multiple_of(pos_ref[0] * 128, 128), 128), KCH:]
    back = lax.dot_general(hg, low, ROWS_BY_COLS, preferred_element_type=F32)
    grads = jnp.where(pre > 0, back, 0.0)
    first = pos_ref[2] == 0
    keep_ref[0:8] = jnp.where(first, grads[:, 0:512], grads[:, 512:1024]).astype(BF).reshape(8, 16, 512)
    give_ref[0:8] = jnp.where(first, grads[:, 512:1024], grads[:, 0:512]).astype(BF).reshape(8, 16, 512)
    sums = jnp.concatenate([bottom[64:72, 0:512]] * 2, axis=0)
    one = sums.astype(BF).astype(F32)
    two = (sums - one).astype(BF).astype(F32)
    row = lax.broadcasted_iota(jnp.int32, sums.shape, 0)
    terms = jnp.where(row == 0, one, jnp.where(row == 1, two, jnp.where(row == 2, sums - one - two, 0.0))).astype(BF)
    keep_ref[8] = terms
    give_ref[8] = terms
    head = jnp.dot(act, low, preferred_element_type=F32).astype(BF)
    proj = lax.dot_general(act, hg, COLS_BY_COLS, preferred_element_type=F32).astype(BF)
    for t in range(GROUPS):
        pay_ref[t, 0:64, :] = proj[64 * t : 64 * (t + 1), :]
        pay_ref[t, 64:96, :] = head[32 * (t % 4) : 32 * (t % 4 + 1), :]


def pool_kernel(pos_ref, sums_ref, pw_ref, const_ref, grad_ref, outer_ref, whole):
    pool = sums_ref[:, 0:BR] * (1.0 / 4096.0)
    hsum = sums_ref[:, BR : 2 * BR]
    act = jnp.maximum(pool, 0.0).astype(BF)
    high = pw_ref[1024:1280, :]
    const_ref[...] = jnp.dot(act, high, preferred_element_type=F32)
    grad = lax.dot_general(hsum, high.astype(F32), ROWS_BY_COLS, precision=HIGH, preferred_element_type=F32)
    grad_ref[...] = jnp.where(pool > 0, grad, 0.0)
    whole[...] = 0.125 * lax.dot_general(
        act.astype(F32), hsum, COLS_BY_COLS, precision=HIGH, preferred_element_type=F32
    )
    chunk = pos_ref[0] * 4 + pos_ref[1]
    outer_ref[...] = whole[pl.ds(pl.multiple_of(chunk * 16, 16), 16), :]


def collect_kernel(pos_ref, pay_ref, const_ref, part_ref, head_ref, wide):
    total = pay_ref[0, 0:64, :].astype(F32)
    for t in range(1, GROUPS):
        total = total + pay_ref[t, 0:64, :].astype(F32)
    part_ref[...] = total
    for v in range(4):
        piece = pay_ref[4 * pos_ref[0] + v, 64:96, :].astype(F32) + const_ref[0:1, :]
        wide[0, pl.ds(v, 32, stride=4), :] = piece[:, 0:128]
        wide[1, pl.ds(v, 32, stride=4), :] = piece[:, 128:256]
    head_ref[:, 0:128] = wide[0].astype(BF)
    head_ref[:, 128:256] = wide[1].astype(BF)


def gather_copies(pos_ref, blocks, g, sem, pad):
    z, y, c = pos_ref[0], pos_ref[1], pos_ref[2]
    copies = []
    for side in range(2):
        half = c if side == 0 else 1 - c
        for place, far in enumerate((0, -1, 1, 2)):
            for k, step in enumerate((0, -1, 1, 2)):
                src = blocks[8 * side + 2 * place + k // 2].at[k % 2, side]
                v = wrap(y + jnp.where(half == 0, step, far))
                group = wrap(z + jnp.where(half == 0, far, step))
                cols = pl.ds(pl.multiple_of(512 * half, 512), 512)
                dst = g.at[pl.ds(2 * pad + 8 * group, 8), v, :, cols]
                copies.append(pltpu.make_async_copy(src, dst, sem.at[len(copies)]))
    return copies


def weight_grad_kernel(pos_ref, xt_ref, colsum_ref, grad_ref, *refs):
    blocks, (own_ref, other_ref), (g, dw, sem) = refs[:16], refs[-5:-3], refs[-3:]
    copies = gather_copies(pos_ref, blocks, g, sem, 0)
    for copy in copies:
        copy.start()
    for copy in copies:
        copy.wait()

    def grads(low, high, cols):
        return g[low // 64 : high // 64, :, :, cols].reshape(high - low, BR)

    dw[0] = jnp.dot(xt_ref[0], grads(0, HALF, slice(0, BR)), preferred_element_type=F32)
    for j in range(3):
        cols = slice((j + 1) * BR, (j + 2) * BR)
        for a in range(3):
            delta = 3 * (j + 1) * (a - 1) * 128
            x_low, x_high = max(delta, 0), HALF + min(delta, 0)
            g_low, g_high = max(-delta, 0), HALF - max(delta, 0)
            left = jnp.concatenate([xt_ref[shift_slot(j, b), :, x_low:x_high] for b in range(3)], axis=0)
            part = jnp.dot(left, grads(g_low, g_high, cols), preferred_element_type=F32)
            start = 1 + 9 * j + 3 * a
            dw[start : start + 3] = part.reshape(3, CH, BR)
    dw[28] = lax.dot_general(
        colsum_ref[...], grad_ref[...], COLS_BY_COLS, precision=HIGH, preferred_element_type=F32
    ) * (0.125 / 4096.0)
    c = pos_ref[2]
    own_ref[...] = dw[:, pl.ds(pl.multiple_of(c * 64, 64), 64), :].astype(BF)
    other_ref[...] = dw[:, pl.ds(pl.multiple_of((1 - c) * 64, 64), 64), :].astype(BF)


def field_grad_kernel(pos_ref, grad_ref, own, other, *refs):
    blocks, dx_ref, (g, w, whole, sem) = refs[:16], refs[-5], refs[-4:]
    copies = gather_copies(pos_ref, blocks, g, sem, PAD)
    for copy in copies:
        copy.start()
    c = pos_ref[2]
    w[:, pl.ds(pl.multiple_of(c * 64, 64), 64), :] = own[...]
    w[:, pl.ds(pl.multiple_of((1 - c) * 64, 64), 64), :] = other[...]
    g[0 : 2 * PAD] = jnp.zeros((2 * PAD, 4, 16, 1024), BF)
    g[2 * (PAD + GROUPS) :] = jnp.zeros((2 * PAD, 4, 16, 1024), BF)
    field = lax.dot_general(
        grad_ref[...], w[28].astype(F32), ROWS_BY_COLS, precision=HIGH, preferred_element_type=F32
    )[0:1, :] * (1.0 / 4096.0)
    for copy in copies:
        copy.wait()

    def grads(low, cols):
        return g[2 * (PAD + low) : 2 * (PAD + low + 4), :, :, cols].reshape(512, BR)

    for m in range(4):
        acc = field + lax.dot_general(
            grads(4 * m, slice(0, BR)), w[0], ROWS_BY_COLS, preferred_element_type=F32
        )
        for j in range(3):
            steps = []
            for a in range(3):
                low = 4 * m - 3 * (j + 1) * (a - 1)
                if low + 3 >= 0 and low < GROUPS:
                    steps.append((a, low))
            left = jnp.concatenate([grads(low, slice((j + 1) * BR, (j + 2) * BR)) for _, low in steps], axis=1)
            right = jnp.concatenate(
                [w[1 + 9 * j + 3 * a : 4 + 9 * j + 3 * a].reshape(3 * CH, BR) for a, _ in steps], axis=1
            )
            spread = lax.dot_general(left, right, ROWS_BY_COLS, preferred_element_type=F32)
            for b in range(3):
                acc = acc + column_shift(spread[:, b * CH : (b + 1) * CH], -(b - 1) * 3 * (j + 1))
        for row in range(8):
            for v in range(4):
                place = (4 * row + v) * 16
                whole[pl.ds(512 * m + 64 * row + v, 16, stride=4), :] = acc[place : place + 16, :]
    low, high = whole[:, 0:64], whole[:, 64:128]
    dx_ref[0] = jnp.where(c == 0, low, high).astype(BF)
    dx_ref[1] = jnp.where(c == 0, high, low).astype(BF)


def add_kernel(pos_ref, own, other, *outs):
    r = pos_ref[3]
    for k in range(4):
        rows = pl.ds(pl.multiple_of(wrap(r + k) * 464, 16), 464)
        outs[k][...] = (own[rows, :].astype(F32) + other[rows, :].astype(F32)).astype(BF)


def join_kernel(pos_ref, *refs):
    for k, step in enumerate((0, -1, 1, 2)):
        rows = pl.ds(pl.multiple_of(wrap(pos_ref[3] + step) * 464, 8), 464)
        refs[4][rows, :] = refs[k][...].astype(F32)


def call(kernel, out_shape, scratch, flops, *args, scalar=True, raw=0):
    specs = [pl.BlockSpec(memory_space=pltpu.VMEM) for _ in args]
    if scalar:
        specs[0] = pl.BlockSpec(memory_space=pltpu.SMEM)
    for k in range(raw):
        specs[len(args) - 1 - k] = pl.BlockSpec(memory_space=pl.ANY)
    moved = sum(a.size * a.dtype.itemsize for a in jax.tree.leaves((args, out_shape)))
    return pl.pallas_call(
        kernel,
        out_shape=out_shape,
        in_specs=specs,
        out_specs=jax.tree.map(lambda _: pl.BlockSpec(memory_space=pltpu.VMEM), out_shape),
        scratch_shapes=scratch,
        compiler_params=pltpu.CompilerParams(vmem_limit_bytes=60 * 2**20),
        cost_estimate=pl.CostEstimate(flops=flops, bytes_accessed=moved, transcendentals=0),
        name=kernel.__name__,
    )(*args)


def gate(values, after):
    anywhere = pl.BlockSpec(memory_space=pl.ANY)
    return pl.pallas_call(
        lambda *refs: None,
        out_shape=tuple(jax.ShapeDtypeStruct(v.shape, v.dtype) for v in values),
        in_specs=[anywhere] * (len(values) + len(after)),
        out_specs=(anywhere,) * len(values),
        input_output_aliases={k: k for k in range(len(values))},
        cost_estimate=pl.CostEstimate(flops=0, bytes_accessed=0, transcendentals=0),
    )(*values, *after)


def swap(value):
    return lax.ppermute(value, "core", [(0, 1), (1, 0)])


def send(value, axis, step):
    return lax.ppermute(value, axis, [(k, (k + step) % 4) for k in range(4)])


def pair(value, axis, bit):
    return lax.ppermute(value, axis, [(k, k ^ bit) for k in range(4)])


def cross(value, step, turn):
    pairs = []
    for z in range(4):
        for y in range(4):
            for c in range(2):
                along_y = (c == 0) != turn
                to = (z, (y + step) % 4) if along_y else ((z + step) % 4, y)
                pairs.append(((4 * z + y) * 2 + c, (4 * to[0] + to[1]) * 2 + c))
    return lax.ppermute(value, ("z", "y", "core"), pairs)


def local(features, head_grad, branch_weight, proj_weight):
    shape = jax.ShapeDtypeStruct
    plane = ("z", "y")
    pos = jnp.stack([lax.axis_index(n).astype(jnp.int32) for n in ("z", "y", "core", "rep")])

    def exchange(value):
        return lax.all_to_all(value, plane, split_axis=0, concat_axis=0, tiled=True)

    first, second = call(
        split_kernel,
        (shape((GROUPS, 32, KCH + BR), BF), shape((GROUPS, 128, CH), BF)),
        [pltpu.VMEM((GROUPS + 2, 128, CH), F32)], 10**6,
        features.reshape(128, 2048), head_grad.reshape(128, BR), scalar=False,
    )
    below, above = send(branch_weight, "y", 1), send(branch_weight, "y", -1)
    x = exchange(first).reshape(512, KCH + BR)
    below, above = gate((below, above), (x,))
    blocks = [branch_weight, below, above, send(below[0:CUT], "y", 1), send(above[CUT:29], "y", -1)]
    blocks = blocks + [swap(b) for b in blocks]
    own, plus, minus, plus_half, minus_half = call(
        forward_kernel,
        tuple(shape((n, 1024), F32) for n in (136, 136, 136, 64, 72)),
        [
            pltpu.VMEM((29, KCH, BR), BF), pltpu.VMEM((7, 512, KCH), BF), pltpu.VMEM((512, 1024), F32),
            pltpu.SemaphoreType.DMA((10,)),
        ],
        4 * 10**9, pos, x, head_grad.reshape(128, BR), *blocks, raw=10,
    )
    from_low, from_high = send(plus, "z", 1), send(minus, "z", -1)
    half_a = send(plus_half + from_low[0:64], "z", 1)
    half_b = send(minus_half + from_high[0:72], "z", -1)
    (second,) = gate((second,), (own,))
    turned, colsum = call(
        turn_kernel, (shape((7, CH, HALF), BF), shape((8, CH), F32)), [], 10**8,
        exchange(second).reshape(HALF, CH), scalar=False,
    )
    keep, give, pay = call(
        middle_kernel,
        (shape((9, 16, 512), BF), shape((9, 16, 512), BF), shape((GROUPS, 96, BR), BF)),
        [], 2 * 10**8, pos, own, from_low, from_high, half_a, half_b, x, proj_weight, turned, raw=1,
    )
    block = call(pair_kernel, shape((2, 9, 16, 512), BF), [], 10**5, keep, swap(give), scalar=False)
    near = [block, cross(block, 1, False), cross(block, -1, False), cross(block, 2, False)]
    stacked = (shape((2, 2, 8, 16, 512), BF), shape((8, 512), F32))
    low, low_sums = call(stack_kernel, stacked, [], 10**5, near[0], near[1], scalar=False)
    high, high_sums = call(stack_kernel, stacked, [], 10**5, near[2], near[3], scalar=False)
    low_below, high_above = cross(low, 1, True), cross(high, -1, True)
    high_below, low_above = cross(high, 1, True), cross(low, -1, True)
    every = [
        low, high, low_below, high_below, low_above, high_above, cross(low_below, 1, True), cross(high_above, -1, True)
    ]
    every = every + [swap(piece) for piece in every]
    sums = low_sums + high_sums
    sums = jnp.where(pos[2] == 0, sums, swap(sums))
    const, pool_grad, outer = call(
        pool_kernel, (shape((8, BR), F32), shape((8, BR), F32), shape((16, BR), F32)), [pltpu.VMEM((256, BR), F32)],
        10**7, pos, sums, proj_weight,
    )
    (pay,) = gate((pay,), (low, high))
    pay = exchange(pay)
    dw, dw_other = call(
        weight_grad_kernel,
        (shape((29, 64, BR), BF), shape((29, 64, BR), BF)),
        [pltpu.VMEM((2 * GROUPS, 4, 16, 1024), BF), pltpu.VMEM((29, CH, BR), F32), pltpu.SemaphoreType.DMA((32,))],
        4 * 10**9, pos, turned, colsum, pool_grad, *every, pay, raw=17,
    )
    quarters = call(
        add_kernel, (shape((464, BR), BF),) * 4, [], 10**6, pos, dw.reshape(1856, BR), swap(dw_other).reshape(1856, BR)
    )
    dx = call(
        field_grad_kernel,
        shape((2, HALF, 64), BF),
        [
            pltpu.VMEM((2 * (GROUPS + 2 * PAD), 4, 16, 1024), BF), pltpu.VMEM((29, CH, BR), BF),
            pltpu.VMEM((HALF, CH), F32), pltpu.SemaphoreType.DMA((32,)),
        ],
        4 * 10**9, pos, pool_grad, branch_weight, blocks[5], *every, quarters[0], raw=17,
    )
    terms = [quarters[0]] + [send(quarters[k], "rep", k) for k in (1, 3, 2)]
    dw = sum(term.astype(F32) for term in terms).astype(BF)
    dw = [dw] + [send(dw, "rep", step) for step in (1, -1, 2)]
    grad_branch = call(join_kernel, shape((1856, BR), F32), [], 10**6, pos, *dw).reshape(29, 64, BR)
    (pay,) = gate((pay,), (quarters[0],))
    part, head_out = call(
        collect_kernel, (shape((64, BR), F32), shape((128, BR), BF)), [pltpu.VMEM((2, 128, 128), F32)],
        10**6, pos, pay, const,
    )
    part = jnp.concatenate([part + swap(part), outer], axis=0)
    part = part + pair(part, "rep", 1)
    part = part + pair(part, "rep", 2)
    part = jnp.broadcast_to(part.astype(BF)[None], (GROUPS, 80, BR))
    (part,) = gate((part,), (dw[0],))
    part = exchange(part).astype(F32)
    grad_proj = jnp.concatenate([part[:, 0:64].reshape(1024, BR), part[:, 64:80].reshape(256, BR)], axis=0)
    mine, theirs = dx[0], swap(dx[1])
    even = jnp.where(pos[2] == 0, mine, theirs).reshape(GROUPS, 1, 2, 64, 64)
    odd = jnp.where(pos[2] == 0, theirs, mine).reshape(GROUPS, 1, 2, 64, 64)
    grad_features = jnp.concatenate([even, odd], axis=1).reshape(1, 64, 64, 64)
    return head_out.reshape(head_grad.shape), grad_features, grad_branch, grad_proj


def solution(mesh):
    fine = Mesh(mesh.devices.reshape(4, 4, 2, 4), ("z", "y", "core", "rep"))
    tile = ("z", "y", "core")
    return jax.shard_map(
        local,
        mesh=fine,
        in_specs=(P("rep", tile, None, None), P("rep", tile, None, None), P(None, tile, None), P()),
        out_specs=(P("rep", tile, None, None), P("rep", None, None, tile), P(None, tile, None), P()),
        check_vma=False,
    )
```

```python
import jax
import jax.numpy as jnp
from jax import lax
from jax.experimental import pallas as pl
from jax.experimental.pallas import tpu as pltpu
from jax.sharding import Mesh, PartitionSpec as P

GROUPS = 16
CH = 128
KCH = 512
BR = 256
HALF = 2048
PAD = 9
CUT = 15
SHIFTS = (0, -3, 3, -6, 6, -9, 9)
F32 = jnp.float32
BF = jnp.bfloat16
HIGH = lax.Precision.HIGHEST
ROWS_BY_COLS = (((1,), (1,)), ((), ()))
COLS_BY_COLS = (((0,), (0,)), ((), ()))


def shift_slot(j, b):
    return SHIFTS.index((b - 1) * 3 * (j + 1))


def column_shift(value, amount):
    if amount == 0:
        return value
    n = value.shape[0]
    col = lax.broadcasted_iota(jnp.int32, value.shape, 0) & 15
    rolled = pltpu.roll(value, (-amount) % n, 0)
    return jnp.where((col + amount >= 0) & (col + amount < 16), rolled, 0.0)


def wrap(value):
    return lax.rem(value + 8, 4)


def split_kernel(x_ref, hg_ref, first_ref, wide):
    for t in range(GROUPS):
        wide[t] = x_ref[:, CH * t : CH * (t + 1)].astype(F32)
    for t in range(2):
        wide[GROUPS + t] = hg_ref[:, CH * t : CH * (t + 1)].astype(F32)
    for v in range(4):
        for t in range(GROUPS + 2):
            part = wide[t, pl.ds(v, 32, stride=4), :].astype(BF)
            if t < GROUPS:
                place = CH * (t % 4)
                first_ref[4 * (t // 4) + v, :, place : place + CH] = part
            else:
                place = KCH + CH * (t - GROUPS)
                for z in range(4):
                    first_ref[4 * z + v, :, place : place + CH] = part


def weight_copies(pos_ref, blocks, w, sem):
    y, c = pos_ref[1], pos_ref[2]
    places = [(0, 0, 29), (-1, 0, 29), (1, 0, 29), (2, 0, CUT), (2, CUT, 29)]
    copies = []
    for side in range(2):
        for k, (step, low, high) in enumerate(places):
            core = c if side == 0 else 1 - c
            start = pl.multiple_of(wrap(y + step) * CH + core * 64, 64)
            n = len(copies)
            copies.append(
                pltpu.make_async_copy(blocks[n], w.at[pl.ds(low, high - low), pl.ds(start, 64), :], sem.at[n])
            )
    return copies


def forward_kernel(pos_ref, x_ref, hg_ref, *refs):
    blocks, outs, pieces, (w, xs, total, sem) = refs[:10], refs[10:14], refs[14:18], refs[18:]
    copies = weight_copies(pos_ref, blocks, w, sem)
    for copy in copies:
        copy.start()
    for step in range(4):
        pieces[step][...] = x_ref[:, pl.ds(pl.multiple_of(wrap(pos_ref[1] + step) * CH, CH), CH)]
    wide = x_ref[:, 0:KCH].astype(F32)
    colsum = jnp.broadcast_to(jnp.sum(wide, axis=0, keepdims=True), (8, KCH))
    for slot, amount in enumerate(SHIFTS):
        if amount:
            xs[slot] = column_shift(wide, amount).astype(BF)
        else:
            xs[slot] = x_ref[:, 0:KCH]
    hsum = jnp.broadcast_to(jnp.sum(hg_ref[...].astype(F32), axis=0, keepdims=True), (8, BR))
    for copy in copies:
        copy.wait()
    pool = jnp.dot(colsum, w[28].astype(F32), precision=HIGH, preferred_element_type=F32)
    total[:, 0:BR] = jnp.dot(xs[0], w[0], preferred_element_type=F32)
    for j in range(3):
        cols = slice((j + 1) * BR, (j + 2) * BR)
        for a in (1, 0, 2):
            delta = 96 * (j + 1) * (a - 1)
            in_low, in_high = max(delta, 0), 512 + min(delta, 0)
            out_low, out_high = max(-delta, 0), 512 - max(delta, 0)
            left = jnp.concatenate([xs[shift_slot(j, b), in_low:in_high, :] for b in range(3)], axis=1)
            start = 1 + 9 * j + 3 * a
            part = jnp.dot(left, w[start : start + 3].reshape(3 * KCH, BR), preferred_element_type=F32)
            if a == 1:
                total[:, cols] = part
            else:
                total[out_low:out_high, cols] += part
    extra = jnp.concatenate([pool, hsum, jnp.zeros((8, 512), F32)], axis=1)
    for step in range(4):
        rows = pl.ds(pl.multiple_of(wrap(pos_ref[0] + step) * 128, 128), 128)
        outs[step][0:128, :] = total[rows, :]
        outs[step][128:136, :] = extra


def pair_kernel(first_ref, second_ref, out_ref):
    out_ref[0] = first_ref[...]
    out_ref[1] = second_ref[...]


def group_kernel(*refs):
    parts, (out_ref, sums_ref) = refs[:4], refs[4:]
    total = jnp.zeros((16, 512), F32)
    for k in range(4):
        for side in range(2):
            out_ref[k, side] = parts[k][side, 0:8]
            total = total + parts[k][side, 8].astype(F32)
    sums_ref[...] = jnp.broadcast_to(jnp.sum(total, axis=0, keepdims=True), (8, 512))


def turn_kernel(pos_ref, *refs):
    pieces, (xt_ref, colsum_ref, joined) = refs[:4], refs[4:]
    for k in range(4):
        joined[:, wrap(pos_ref[1] - k)] = pieces[k][...].reshape(32, 16, CH)
    total = jnp.zeros((1, CH), F32)
    for m in range(4):
        wide = joined[8 * m : 8 * (m + 1)].reshape(512, CH).astype(F32)
        total = total + jnp.sum(wide, axis=0, keepdims=True)
        for slot, amount in enumerate(SHIFTS):
            xt_ref[slot, :, pl.ds(m * 512, 512)] = column_shift(wide, amount).T.astype(BF)
    colsum_ref[...] = jnp.broadcast_to(total, (8, CH))


def middle_kernel(pos_ref, *refs):
    parts, (x_ref, pw_ref, _, keep_ref, give_ref, pay_ref) = refs[:4], refs[4:]
    whole = parts[0][...] + parts[1][...] + parts[2][...] + parts[3][...]
    pre = whole[0:128, :]
    act = jnp.maximum(pre, 0.0).astype(BF)
    low = pw_ref[0:1024, :]
    hg = x_ref[pl.ds(pl.multiple_of(pos_ref[0] * 128, 128), 128), KCH:]
    back = lax.dot_general(hg, low, ROWS_BY_COLS, preferred_element_type=F32)
    grads = jnp.where(pre > 0, back, 0.0)
    first = pos_ref[2] == 0
    keep_ref[0:8] = jnp.where(first, grads[:, 0:512], grads[:, 512:1024]).astype(BF).reshape(8, 16, 512)
    give_ref[0:8] = jnp.where(first, grads[:, 512:1024], grads[:, 0:512]).astype(BF).reshape(8, 16, 512)
    sums = jnp.concatenate([whole[128:136, 0:512]] * 2, axis=0)
    one = sums.astype(BF).astype(F32)
    two = (sums - one).astype(BF).astype(F32)
    row = lax.broadcasted_iota(jnp.int32, sums.shape, 0)
    terms = jnp.where(row == 0, one, jnp.where(row == 1, two, jnp.where(row == 2, sums - one - two, 0.0))).astype(BF)
    keep_ref[8] = terms
    give_ref[8] = terms
    head = jnp.dot(act, low, preferred_element_type=F32).astype(BF)
    proj = lax.dot_general(act, hg, COLS_BY_COLS, preferred_element_type=F32).astype(BF)
    for t in range(GROUPS):
        pay_ref[t, 0:64, :] = proj[64 * t : 64 * (t + 1), :]
        pay_ref[t, 64:96, :] = head[32 * (t % 4) : 32 * (t % 4 + 1), :]


def pool_kernel(pos_ref, sums_ref, pw_ref, const_ref, grad_ref, outer_ref, whole):
    pool = sums_ref[:, 0:BR] * (1.0 / 4096.0)
    hsum = sums_ref[:, BR : 2 * BR]
    act = jnp.maximum(pool, 0.0).astype(BF)
    high = pw_ref[1024:1280, :]
    const_ref[...] = jnp.dot(act, high, preferred_element_type=F32)
    grad = lax.dot_general(hsum, high.astype(F32), ROWS_BY_COLS, precision=HIGH, preferred_element_type=F32)
    grad_ref[...] = jnp.where(pool > 0, grad, 0.0)
    whole[...] = 0.125 * lax.dot_general(
        act.astype(F32), hsum, COLS_BY_COLS, precision=HIGH, preferred_element_type=F32
    )
    chunk = pos_ref[0] * 4 + pos_ref[1]
    outer_ref[...] = whole[pl.ds(pl.multiple_of(chunk * 16, 16), 16), :]


def collect_kernel(pay_ref, part_ref):
    total = pay_ref[0, 0:64, :].astype(F32)
    for t in range(1, GROUPS):
        total = total + pay_ref[t, 0:64, :].astype(F32)
    part_ref[...] = total


def head_kernel(pos_ref, pay_ref, const_ref, head_ref, wide):
    for v in range(4):
        piece = pay_ref[4 * pos_ref[0] + v, 64:96, :].astype(F32) + const_ref[0:1, :]
        wide[0, pl.ds(v, 32, stride=4), :] = piece[:, 0:128]
        wide[1, pl.ds(v, 32, stride=4), :] = piece[:, 128:256]
    head_ref[:, 0:128] = wide[0].astype(BF)
    head_ref[:, 128:256] = wide[1].astype(BF)


def gather_copies(pos_ref, blocks, g, sem, pad):
    z, y, c = pos_ref[0], pos_ref[1], pos_ref[2]
    copies = []
    for side in range(2):
        half = c if side == 0 else 1 - c
        for place, far in enumerate((0, -1, 1, 2)):
            for k, step in enumerate((0, -1, 1, 2)):
                src = blocks[4 * side + place].at[k, side]
                v = wrap(y + jnp.where(half == 0, step, far))
                group = wrap(z + jnp.where(half == 0, far, step))
                cols = pl.ds(pl.multiple_of(512 * half, 512), 512)
                dst = g.at[pl.ds(2 * pad + 8 * group, 8), v, :, cols]
                copies.append(pltpu.make_async_copy(src, dst, sem.at[len(copies)]))
    return copies


def weight_grad_kernel(pos_ref, xt_ref, colsum_ref, grad_ref, *refs):
    blocks, (own_ref, other_ref), (g, dw, sem) = refs[:8], refs[-5:-3], refs[-3:]
    copies = gather_copies(pos_ref, blocks, g, sem, 0)
    for copy in copies:
        copy.start()
    for copy in copies:
        copy.wait()

    def grads(low, high, cols):
        return g[low // 64 : high // 64, :, :, cols].reshape(high - low, BR)

    dw[0] = jnp.dot(xt_ref[0], grads(0, HALF, slice(0, BR)), preferred_element_type=F32)
    for j in range(3):
        cols = slice((j + 1) * BR, (j + 2) * BR)
        for a in range(3):
            delta = 3 * (j + 1) * (a - 1) * 128
            x_low, x_high = max(delta, 0), HALF + min(delta, 0)
            g_low, g_high = max(-delta, 0), HALF - max(delta, 0)
            left = jnp.concatenate([xt_ref[shift_slot(j, b), :, x_low:x_high] for b in range(3)], axis=0)
            part = jnp.dot(left, grads(g_low, g_high, cols), preferred_element_type=F32)
            start = 1 + 9 * j + 3 * a
            dw[start : start + 3] = part.reshape(3, CH, BR)
    dw[28] = lax.dot_general(
        colsum_ref[...], grad_ref[...], COLS_BY_COLS, precision=HIGH, preferred_element_type=F32
    ) * (0.125 / 4096.0)
    c = pos_ref[2]
    own_ref[...] = dw[:, pl.ds(pl.multiple_of(c * 64, 64), 64), :].astype(BF)
    other_ref[...] = dw[:, pl.ds(pl.multiple_of((1 - c) * 64, 64), 64), :].astype(BF)


def field_grad_kernel(pos_ref, grad_ref, own, other, *refs):
    blocks, dx_ref, (g, w, whole, sem) = refs[:8], refs[-5], refs[-4:]
    copies = gather_copies(pos_ref, blocks, g, sem, PAD)
    for copy in copies:
        copy.start()
    c = pos_ref[2]
    w[:, pl.ds(pl.multiple_of(c * 64, 64), 64), :] = own[...]
    w[:, pl.ds(pl.multiple_of((1 - c) * 64, 64), 64), :] = other[...]
    g[0 : 2 * PAD] = jnp.zeros((2 * PAD, 4, 16, 1024), BF)
    g[2 * (PAD + GROUPS) :] = jnp.zeros((2 * PAD, 4, 16, 1024), BF)
    field = lax.dot_general(
        grad_ref[...], w[28].astype(F32), ROWS_BY_COLS, precision=HIGH, preferred_element_type=F32
    )[0:1, :] * (1.0 / 4096.0)
    for copy in copies:
        copy.wait()

    def grads(low, cols):
        return g[2 * (PAD + low) : 2 * (PAD + low + 4), :, :, cols].reshape(512, BR)

    for m in range(4):
        acc = field + lax.dot_general(
            grads(4 * m, slice(0, BR)), w[0], ROWS_BY_COLS, preferred_element_type=F32
        )
        for j in range(3):
            steps = []
            for a in range(3):
                low = 4 * m - 3 * (j + 1) * (a - 1)
                if low + 3 >= 0 and low < GROUPS:
                    steps.append((a, low))
            left = jnp.concatenate([grads(low, slice((j + 1) * BR, (j + 2) * BR)) for _, low in steps], axis=1)
            right = jnp.concatenate(
                [w[1 + 9 * j + 3 * a : 4 + 9 * j + 3 * a].reshape(3 * CH, BR) for a, _ in steps], axis=1
            )
            spread = lax.dot_general(left, right, ROWS_BY_COLS, preferred_element_type=F32)
            for b in range(3):
                acc = acc + column_shift(spread[:, b * CH : (b + 1) * CH], -(b - 1) * 3 * (j + 1))
        for row in range(8):
            for v in range(4):
                place = (4 * row + v) * 16
                whole[pl.ds(512 * m + 64 * row + v, 16, stride=4), :] = acc[place : place + 16, :]
    low, high = whole[:, 0:64], whole[:, 64:128]
    dx_ref[0] = jnp.where(c == 0, low, high).astype(BF)
    dx_ref[1] = jnp.where(c == 0, high, low).astype(BF)


def add_kernel(pos_ref, own, other, *outs):
    r = pos_ref[3]
    for k in range(4):
        rows = pl.ds(pl.multiple_of(wrap(r + k) * 464, 16), 464)
        outs[k][...] = (own[rows, :].astype(F32) + other[rows, :].astype(F32)).astype(BF)


def join_kernel(pos_ref, *refs):
    for k, step in enumerate((0, -1, 1, 2)):
        rows = pl.ds(pl.multiple_of(wrap(pos_ref[3] + step) * 464, 8), 464)
        refs[4][rows, :] = refs[k][...].astype(F32)


def call(kernel, out_shape, scratch, flops, *args, scalar=True, raw=0):
    specs = [pl.BlockSpec(memory_space=pltpu.VMEM) for _ in args]
    if scalar:
        specs[0] = pl.BlockSpec(memory_space=pltpu.SMEM)
    for k in range(raw):
        specs[len(args) - 1 - k] = pl.BlockSpec(memory_space=pl.ANY)
    moved = sum(a.size * a.dtype.itemsize for a in jax.tree.leaves((args, out_shape)))
    return pl.pallas_call(
        kernel,
        out_shape=out_shape,
        in_specs=specs,
        out_specs=jax.tree.map(lambda _: pl.BlockSpec(memory_space=pltpu.VMEM), out_shape),
        scratch_shapes=scratch,
        compiler_params=pltpu.CompilerParams(vmem_limit_bytes=60 * 2**20),
        cost_estimate=pl.CostEstimate(flops=flops, bytes_accessed=moved, transcendentals=0),
        name=kernel.__name__,
    )(*args)


def gate(values, after):
    anywhere = pl.BlockSpec(memory_space=pl.ANY)
    return pl.pallas_call(
        lambda *refs: None,
        out_shape=tuple(jax.ShapeDtypeStruct(v.shape, v.dtype) for v in values),
        in_specs=[anywhere] * (len(values) + len(after)),
        out_specs=(anywhere,) * len(values),
        input_output_aliases={k: k for k in range(len(values))},
        cost_estimate=pl.CostEstimate(flops=0, bytes_accessed=0, transcendentals=0),
    )(*values, *after)


def swap(value):
    return lax.ppermute(value, "core", [(0, 1), (1, 0)])


def send(value, axis, step):
    return lax.ppermute(value, axis, [(k, (k + step) % 4) for k in range(4)])


def pair(value, axis, bit):
    return lax.ppermute(value, axis, [(k, k ^ bit) for k in range(4)])


def cross(value, step, turn):
    pairs = []
    for z in range(4):
        for y in range(4):
            for c in range(2):
                along_y = (c == 0) != turn
                to = (z, (y + step) % 4) if along_y else ((z + step) % 4, y)
                pairs.append(((4 * z + y) * 2 + c, (4 * to[0] + to[1]) * 2 + c))
    return lax.ppermute(value, ("z", "y", "core"), pairs)


def local(features, head_grad, branch_weight, proj_weight):
    shape = jax.ShapeDtypeStruct
    plane = ("z", "y")
    pos = jnp.stack([lax.axis_index(n).astype(jnp.int32) for n in ("z", "y", "core", "rep")])

    def exchange(value):
        return lax.all_to_all(value, plane, split_axis=0, concat_axis=0, tiled=True)

    first = call(
        split_kernel, shape((GROUPS, 32, KCH + BR), BF),
        [pltpu.VMEM((GROUPS + 2, 128, CH), F32)], 10**6,
        features.reshape(128, 2048), head_grad.reshape(128, BR), scalar=False,
    )
    below, above = send(branch_weight, "y", 1), send(branch_weight, "y", -1)
    x = exchange(first).reshape(512, KCH + BR)
    below, above = gate((below, above), (x,))
    blocks = [branch_weight, below, above, send(below[0:CUT], "y", 1), send(above[CUT:29], "y", -1)]
    blocks = blocks + [swap(b) for b in blocks]
    results = call(
        forward_kernel,
        (shape((136, 1024), F32),) * 4 + (shape((512, CH), BF),) * 4,
        [
            pltpu.VMEM((29, KCH, BR), BF), pltpu.VMEM((7, 512, KCH), BF), pltpu.VMEM((512, 1024), F32),
            pltpu.SemaphoreType.DMA((10,)),
        ],
        4 * 10**9, pos, x, head_grad.reshape(128, BR), *blocks, raw=10,
    )
    sums = [results[0]] + [send(results[k], "z", k) for k in (1, 3, 2)]
    pieces = [results[4]] + [send(results[4 + k], "y", k) for k in (1, 2, 3)]
    turned, colsum = call(
        turn_kernel, (shape((7, CH, HALF), BF), shape((8, CH), F32)), [pltpu.VMEM((32, 4, 16, CH), BF)], 10**8,
        pos, *pieces,
    )
    keep, give, pay = call(
        middle_kernel,
        (shape((9, 16, 512), BF), shape((9, 16, 512), BF), shape((GROUPS, 96, BR), BF)),
        [], 2 * 10**8, pos, *sums, x, proj_weight, turned, raw=1,
    )
    block = call(pair_kernel, shape((2, 9, 16, 512), BF), [], 10**5, keep, swap(give), scalar=False)
    near = [block, cross(block, 1, False), cross(block, -1, False), cross(block, 2, False)]
    group, sums = call(
        group_kernel, (shape((4, 2, 8, 16, 512), BF), shape((8, 512), F32)), [], 10**5, *near, scalar=False
    )
    every = [group] + [cross(group, step, True) for step in (1, -1, 2)]
    sums = jnp.where(pos[2] == 0, sums, swap(sums))
    const, pool_grad, outer = call(
        pool_kernel, (shape((8, BR), F32), shape((8, BR), F32), shape((16, BR), F32)), [pltpu.VMEM((256, BR), F32)],
        10**7, pos, sums, proj_weight,
    )
    pay = exchange(pay)
    part = call(collect_kernel, shape((64, BR), F32), [], 10**6, pay, scalar=False)
    part = jnp.concatenate([part + swap(part), outer], axis=0)
    part = part + pair(part, "rep", 1)
    part = part + pair(part, "rep", 2)
    part = jnp.broadcast_to(part.astype(BF)[None], (GROUPS, 80, BR))
    theirs = [swap(piece) for piece in every[0:3]]
    (far,) = gate((every[3],), (part, theirs[1], theirs[2]))
    every = every[0:3] + [far] + theirs + [swap(far)]
    dw, dw_other = call(
        weight_grad_kernel,
        (shape((29, 64, BR), BF), shape((29, 64, BR), BF)),
        [pltpu.VMEM((2 * GROUPS, 4, 16, 1024), BF), pltpu.VMEM((29, CH, BR), F32), pltpu.SemaphoreType.DMA((32,))],
        4 * 10**9, pos, turned, colsum, pool_grad, *every, raw=8,
    )
    quarters = call(
        add_kernel, (shape((464, BR), BF),) * 4, [], 10**6, pos, dw.reshape(1856, BR), swap(dw_other).reshape(1856, BR)
    )
    dx = call(
        field_grad_kernel,
        shape((2, HALF, 64), BF),
        [
            pltpu.VMEM((2 * (GROUPS + 2 * PAD), 4, 16, 1024), BF), pltpu.VMEM((29, CH, BR), BF),
            pltpu.VMEM((HALF, CH), F32), pltpu.SemaphoreType.DMA((32,)),
        ],
        4 * 10**9, pos, pool_grad, branch_weight, blocks[5], *every, quarters[0], raw=9,
    )
    terms = [quarters[0]] + [send(quarters[k], "rep", k) for k in (1, 3, 2)]
    dw = sum(term.astype(F32) for term in terms).astype(BF)
    dw = [dw] + [send(dw, "rep", step) for step in (1, -1, 2)]
    grad_branch = call(join_kernel, shape((1856, BR), F32), [], 10**6, pos, *dw).reshape(29, 64, BR)
    (part,) = gate((exchange(part),), (dw[0],))
    part = part.astype(F32)
    grad_proj = jnp.concatenate([part[:, 0:64].reshape(1024, BR), part[:, 64:80].reshape(256, BR)], axis=0)
    (const,) = gate((const,), (dw[0],))
    head_out = call(head_kernel, shape((128, BR), BF), [pltpu.VMEM((2, 128, 128), F32)], 10**6, pos, pay, const)
    mine, theirs = dx[0], swap(dx[1])
    even = jnp.where(pos[2] == 0, mine, theirs).reshape(GROUPS, 1, 2, 64, 64)
    odd = jnp.where(pos[2] == 0, theirs, mine).reshape(GROUPS, 1, 2, 64, 64)
    grad_features = jnp.concatenate([even, odd], axis=1).reshape(1, 64, 64, 64)
    return head_out.reshape(head_grad.shape), grad_features, grad_branch, grad_proj


def solution(mesh):
    fine = Mesh(mesh.devices.reshape(4, 4, 2, 4), ("z", "y", "core", "rep"))
    tile = ("z", "y", "core")
    return jax.shard_map(
        local,
        mesh=fine,
        in_specs=(P("rep", tile, None, None), P("rep", tile, None, None), P(None, tile, None), P()),
        out_specs=(P("rep", tile, None, None), P("rep", None, None, tile), P(None, tile, None), P()),
        check_vma=False,
    )
```

```python
import jax
import jax.numpy as jnp
from jax import lax
from jax.experimental import pallas as pl
from jax.experimental.pallas import tpu as pltpu
from jax.sharding import Mesh, PartitionSpec as P

GROUPS = 16
CH = 128
KCH = 512
BR = 256
HALF = 2048
PAD = 9
CUT = 15
SHIFTS = (0, -3, 3, -6, 6, -9, 9)
F32 = jnp.float32
BF = jnp.bfloat16
HIGH = lax.Precision.HIGHEST
ROWS_BY_COLS = (((1,), (1,)), ((), ()))
COLS_BY_COLS = (((0,), (0,)), ((), ()))


def shift_slot(j, b):
    return SHIFTS.index((b - 1) * 3 * (j + 1))


def column_shift(value, amount):
    if amount == 0:
        return value
    n = value.shape[0]
    col = lax.broadcasted_iota(jnp.int32, value.shape, 0) & 15
    rolled = pltpu.roll(value, (-amount) % n, 0)
    return jnp.where((col + amount >= 0) & (col + amount < 16), rolled, 0.0)


def wrap(value):
    return lax.rem(value + 8, 4)


def split_kernel(x_ref, hg_ref, first_ref, wide):
    for t in range(GROUPS):
        wide[t] = x_ref[:, CH * t : CH * (t + 1)].astype(F32)
    for t in range(2):
        wide[GROUPS + t] = hg_ref[:, CH * t : CH * (t + 1)].astype(F32)
    for v in range(4):
        for t in range(GROUPS + 2):
            part = wide[t, pl.ds(v, 32, stride=4), :].astype(BF)
            if t < GROUPS:
                place = CH * (t % 4)
                first_ref[4 * (t // 4) + v, :, place : place + CH] = part
            else:
                place = KCH + CH * (t - GROUPS)
                for z in range(4):
                    first_ref[4 * z + v, :, place : place + CH] = part


def weight_copies(pos_ref, blocks, w, sem):
    y, c = pos_ref[1], pos_ref[2]
    places = [(0, 0, 29), (-1, 0, 29), (1, 0, 29), (2, 0, CUT), (2, CUT, 29)]
    copies = []
    for side in range(2):
        for k, (step, low, high) in enumerate(places):
            core = c if side == 0 else 1 - c
            start = pl.multiple_of(wrap(y + step) * CH + core * 64, 64)
            n = len(copies)
            copies.append(
                pltpu.make_async_copy(blocks[n], w.at[pl.ds(low, high - low), pl.ds(start, 64), :], sem.at[n])
            )
    return copies


def forward_kernel(pos_ref, x_ref, hg_ref, *refs):
    blocks, outs, pieces, (w, xs, total, sem) = refs[:10], refs[10:14], refs[14:18], refs[18:]
    copies = weight_copies(pos_ref, blocks, w, sem)
    for copy in copies:
        copy.start()
    for step in range(4):
        pieces[step][...] = x_ref[:, pl.ds(pl.multiple_of(wrap(pos_ref[1] + step) * CH, CH), CH)]
    wide = x_ref[:, 0:KCH].astype(F32)
    colsum = jnp.broadcast_to(jnp.sum(wide, axis=0, keepdims=True), (8, KCH))
    for slot, amount in enumerate(SHIFTS):
        if amount:
            xs[slot] = column_shift(wide, amount).astype(BF)
        else:
            xs[slot] = x_ref[:, 0:KCH]
    hsum = jnp.broadcast_to(jnp.sum(hg_ref[...].astype(F32), axis=0, keepdims=True), (8, BR))
    for copy in copies:
        copy.wait()
    pool = jnp.dot(colsum, w[28].astype(F32), precision=HIGH, preferred_element_type=F32)
    total[:, 0:BR] = jnp.dot(xs[0], w[0], preferred_element_type=F32)
    for j in range(3):
        cols = slice((j + 1) * BR, (j + 2) * BR)
        for a in (1, 0, 2):
            delta = 96 * (j + 1) * (a - 1)
            in_low, in_high = max(delta, 0), 512 + min(delta, 0)
            out_low, out_high = max(-delta, 0), 512 - max(delta, 0)
            left = jnp.concatenate([xs[shift_slot(j, b), in_low:in_high, :] for b in range(3)], axis=1)
            start = 1 + 9 * j + 3 * a
            part = jnp.dot(left, w[start : start + 3].reshape(3 * KCH, BR), preferred_element_type=F32)
            if a == 1:
                total[:, cols] = part
            else:
                total[out_low:out_high, cols] += part
    extra = jnp.concatenate([pool, hsum, jnp.zeros((8, 512), F32)], axis=1)
    for step in range(4):
        rows = pl.ds(pl.multiple_of(wrap(pos_ref[0] + step) * 128, 128), 128)
        outs[step][0:128, :] = total[rows, :]
        outs[step][128:136, :] = extra


def pair_kernel(first_ref, second_ref, out_ref):
    out_ref[0] = first_ref[...]
    out_ref[1] = second_ref[...]


def group_kernel(*refs):
    parts, (out_ref, sums_ref) = refs[:4], refs[4:]
    total = jnp.zeros((16, 512), F32)
    for k in range(4):
        for side in range(2):
            out_ref[k, side] = parts[k][side, 0:8]
            total = total + parts[k][side, 8].astype(F32)
    sums_ref[...] = jnp.broadcast_to(jnp.sum(total, axis=0, keepdims=True), (8, 512))


def turn_kernel(pos_ref, *refs):
    pieces, (xt_ref, colsum_ref, joined) = refs[:4], refs[4:]
    for k in range(4):
        joined[:, wrap(pos_ref[1] - k)] = pieces[k][...].reshape(32, 16, CH)
    total = jnp.zeros((1, CH), F32)
    for m in range(4):
        wide = joined[8 * m : 8 * (m + 1)].reshape(512, CH).astype(F32)
        total = total + jnp.sum(wide, axis=0, keepdims=True)
        for slot, amount in enumerate(SHIFTS):
            xt_ref[slot, :, pl.ds(m * 512, 512)] = column_shift(wide, amount).T.astype(BF)
    colsum_ref[...] = jnp.broadcast_to(total, (8, CH))


def middle_kernel(pos_ref, *refs):
    parts, (x_ref, pw_ref, _, keep_ref, give_ref, pay_ref) = refs[:4], refs[4:]
    whole = parts[0][...] + parts[1][...] + parts[2][...] + parts[3][...]
    pre = whole[0:128, :]
    act = jnp.maximum(pre, 0.0).astype(BF)
    low = pw_ref[0:1024, :]
    hg = x_ref[pl.ds(pl.multiple_of(pos_ref[0] * 128, 128), 128), KCH:]
    back = lax.dot_general(hg, low, ROWS_BY_COLS, preferred_element_type=F32)
    grads = jnp.where(pre > 0, back, 0.0)
    first = pos_ref[2] == 0
    keep_ref[0:8] = jnp.where(first, grads[:, 0:512], grads[:, 512:1024]).astype(BF).reshape(8, 16, 512)
    give_ref[0:8] = jnp.where(first, grads[:, 512:1024], grads[:, 0:512]).astype(BF).reshape(8, 16, 512)
    sums = jnp.concatenate([whole[128:136, 0:512]] * 2, axis=0)
    one = sums.astype(BF).astype(F32)
    two = (sums - one).astype(BF).astype(F32)
    row = lax.broadcasted_iota(jnp.int32, sums.shape, 0)
    terms = jnp.where(row == 0, one, jnp.where(row == 1, two, jnp.where(row == 2, sums - one - two, 0.0))).astype(BF)
    keep_ref[8] = terms
    give_ref[8] = terms
    head = jnp.dot(act, low, preferred_element_type=F32).astype(BF)
    proj = lax.dot_general(act, hg, COLS_BY_COLS, preferred_element_type=F32).astype(BF)
    for t in range(GROUPS):
        pay_ref[t, 0:64, :] = proj[64 * t : 64 * (t + 1), :]
        pay_ref[t, 64:96, :] = head[32 * (t % 4) : 32 * (t % 4 + 1), :]


def pool_kernel(pos_ref, sums_ref, pw_ref, const_ref, grad_ref, outer_ref, whole):
    pool = sums_ref[:, 0:BR] * (1.0 / 4096.0)
    hsum = sums_ref[:, BR : 2 * BR]
    act = jnp.maximum(pool, 0.0).astype(BF)
    high = pw_ref[1024:1280, :]
    const_ref[...] = jnp.dot(act, high, preferred_element_type=F32)
    grad = lax.dot_general(hsum, high.astype(F32), ROWS_BY_COLS, precision=HIGH, preferred_element_type=F32)
    grad_ref[...] = jnp.where(pool > 0, grad, 0.0)
    whole[...] = 0.125 * lax.dot_general(
        act.astype(F32), hsum, COLS_BY_COLS, precision=HIGH, preferred_element_type=F32
    )
    chunk = pos_ref[0] * 4 + pos_ref[1]
    outer_ref[...] = whole[pl.ds(pl.multiple_of(chunk * 16, 16), 16), :]


def collect_kernel(pay_ref, part_ref):
    total = pay_ref[0, 0:64, :].astype(F32)
    for t in range(1, GROUPS):
        total = total + pay_ref[t, 0:64, :].astype(F32)
    part_ref[...] = total


def head_kernel(pos_ref, pay_ref, const_ref, head_ref, wide):
    for v in range(4):
        piece = pay_ref[4 * pos_ref[0] + v, 64:96, :].astype(F32) + const_ref[0:1, :]
        wide[0, pl.ds(v, 32, stride=4), :] = piece[:, 0:128]
        wide[1, pl.ds(v, 32, stride=4), :] = piece[:, 128:256]
    head_ref[:, 0:128] = wide[0].astype(BF)
    head_ref[:, 128:256] = wide[1].astype(BF)


def gather_copies(pos_ref, blocks, g, sem, pad):
    z, y, c = pos_ref[0], pos_ref[1], pos_ref[2]
    copies = []
    for side in range(2):
        half = c if side == 0 else 1 - c
        for place, far in enumerate((0, -1, 1, 2)):
            for k, step in enumerate((0, -1, 1, 2)):
                src = blocks[4 * side + place].at[k, side]
                v = wrap(y + jnp.where(half == 0, step, far))
                group = wrap(z + jnp.where(half == 0, far, step))
                cols = pl.ds(pl.multiple_of(512 * half, 512), 512)
                dst = g.at[pl.ds(2 * pad + 8 * group, 8), v, :, cols]
                copies.append(pltpu.make_async_copy(src, dst, sem.at[len(copies)]))
    return copies


def weight_grad_kernel(pos_ref, xt_ref, colsum_ref, grad_ref, *refs):
    blocks, (own_ref, other_ref), (g, dw, sem) = refs[:8], refs[-5:-3], refs[-3:]
    copies = gather_copies(pos_ref, blocks, g, sem, 0)
    for copy in copies:
        copy.start()
    for copy in copies:
        copy.wait()

    def grads(low, high, cols):
        return g[low // 64 : high // 64, :, :, cols].reshape(high - low, BR)

    dw[0] = jnp.dot(xt_ref[0], grads(0, HALF, slice(0, BR)), preferred_element_type=F32)
    for j in range(3):
        cols = slice((j + 1) * BR, (j + 2) * BR)
        for a in range(3):
            delta = 3 * (j + 1) * (a - 1) * 128
            x_low, x_high = max(delta, 0), HALF + min(delta, 0)
            g_low, g_high = max(-delta, 0), HALF - max(delta, 0)
            left = jnp.concatenate([xt_ref[shift_slot(j, b), :, x_low:x_high] for b in range(3)], axis=0)
            part = jnp.dot(left, grads(g_low, g_high, cols), preferred_element_type=F32)
            start = 1 + 9 * j + 3 * a
            dw[start : start + 3] = part.reshape(3, CH, BR)
    dw[28] = lax.dot_general(
        colsum_ref[...], grad_ref[...], COLS_BY_COLS, precision=HIGH, preferred_element_type=F32
    ) * (0.125 / 4096.0)
    c = pos_ref[2]
    own_ref[...] = dw[:, pl.ds(pl.multiple_of(c * 64, 64), 64), :].astype(BF)
    other_ref[...] = dw[:, pl.ds(pl.multiple_of((1 - c) * 64, 64), 64), :].astype(BF)


def field_grad_kernel(pos_ref, grad_ref, own, other, *refs):
    blocks, dx_ref, (g, w, whole, sem) = refs[:8], refs[-5], refs[-4:]
    copies = gather_copies(pos_ref, blocks, g, sem, PAD)
    for copy in copies:
        copy.start()
    c = pos_ref[2]
    w[:, pl.ds(pl.multiple_of(c * 64, 64), 64), :] = own[...]
    w[:, pl.ds(pl.multiple_of((1 - c) * 64, 64), 64), :] = other[...]
    g[0 : 2 * PAD] = jnp.zeros((2 * PAD, 4, 16, 1024), BF)
    g[2 * (PAD + GROUPS) :] = jnp.zeros((2 * PAD, 4, 16, 1024), BF)
    field = lax.dot_general(
        grad_ref[...], w[28].astype(F32), ROWS_BY_COLS, precision=HIGH, preferred_element_type=F32
    )[0:1, :] * (1.0 / 4096.0)
    for copy in copies:
        copy.wait()

    def grads(low, cols):
        return g[2 * (PAD + low) : 2 * (PAD + low + 4), :, :, cols].reshape(512, BR)

    for m in range(4):
        acc = field + lax.dot_general(
            grads(4 * m, slice(0, BR)), w[0], ROWS_BY_COLS, preferred_element_type=F32
        )
        for j in range(3):
            steps = []
            for a in range(3):
                low = 4 * m - 3 * (j + 1) * (a - 1)
                if low + 3 >= 0 and low < GROUPS:
                    steps.append((a, low))
            left = jnp.concatenate([grads(low, slice((j + 1) * BR, (j + 2) * BR)) for _, low in steps], axis=1)
            right = jnp.concatenate(
                [w[1 + 9 * j + 3 * a : 4 + 9 * j + 3 * a].reshape(3 * CH, BR) for a, _ in steps], axis=1
            )
            spread = lax.dot_general(left, right, ROWS_BY_COLS, preferred_element_type=F32)
            for b in range(3):
                acc = acc + column_shift(spread[:, b * CH : (b + 1) * CH], -(b - 1) * 3 * (j + 1))
        for row in range(8):
            for v in range(4):
                place = (4 * row + v) * 16
                whole[pl.ds(512 * m + 64 * row + v, 16, stride=4), :] = acc[place : place + 16, :]
    low, high = whole[:, 0:64], whole[:, 64:128]
    dx_ref[0] = jnp.where(c == 0, low, high).astype(BF)
    dx_ref[1] = jnp.where(c == 0, high, low).astype(BF)


def add_kernel(pos_ref, own, other, *outs):
    r = pos_ref[3]
    for k in range(4):
        rows = pl.ds(pl.multiple_of(wrap(r + k) * 464, 16), 464)
        outs[k][...] = (own[rows, :].astype(F32) + other[rows, :].astype(F32)).astype(BF)


def join_kernel(pos_ref, *refs):
    for k, step in enumerate((0, -1, 1, 2)):
        rows = pl.ds(pl.multiple_of(wrap(pos_ref[3] + step) * 464, 8), 464)
        refs[4][rows, :] = refs[k][...].astype(F32)


ROOM = {"forward_kernel": 28, "weight_grad_kernel": 26, "field_grad_kernel": 28, "turn_kernel": 16, "middle_kernel": 16}


def call(kernel, out_shape, scratch, flops, *args, scalar=True, raw=0):
    specs = [pl.BlockSpec(memory_space=pltpu.VMEM) for _ in args]
    if scalar:
        specs[0] = pl.BlockSpec(memory_space=pltpu.SMEM)
    for k in range(raw):
        specs[len(args) - 1 - k] = pl.BlockSpec(memory_space=pl.ANY)
    moved = sum(a.size * a.dtype.itemsize for a in jax.tree.leaves((args, out_shape)))
    return pl.pallas_call(
        kernel,
        out_shape=out_shape,
        in_specs=specs,
        out_specs=jax.tree.map(lambda _: pl.BlockSpec(memory_space=pltpu.VMEM), out_shape),
        scratch_shapes=scratch,
        compiler_params=pltpu.CompilerParams(vmem_limit_bytes=ROOM.get(kernel.__name__, 12) * 2**20),
        cost_estimate=pl.CostEstimate(flops=flops, bytes_accessed=moved, transcendentals=0),
        name=kernel.__name__,
    )(*args)


def gate(values, after):
    anywhere = pl.BlockSpec(memory_space=pl.ANY)
    return pl.pallas_call(
        lambda *refs: None,
        out_shape=tuple(jax.ShapeDtypeStruct(v.shape, v.dtype) for v in values),
        in_specs=[anywhere] * (len(values) + len(after)),
        out_specs=(anywhere,) * len(values),
        input_output_aliases={k: k for k in range(len(values))},
        cost_estimate=pl.CostEstimate(flops=0, bytes_accessed=0, transcendentals=0),
    )(*values, *after)


def swap(value):
    return lax.ppermute(value, "core", [(0, 1), (1, 0)])


def send(value, axis, step):
    return lax.ppermute(value, axis, [(k, (k + step) % 4) for k in range(4)])


def pair(value, axis, bit):
    return lax.ppermute(value, axis, [(k, k ^ bit) for k in range(4)])


def cross(value, step, turn):
    pairs = []
    for z in range(4):
        for y in range(4):
            for c in range(2):
                along_y = (c == 0) != turn
                to = (z, (y + step) % 4) if along_y else ((z + step) % 4, y)
                pairs.append(((4 * z + y) * 2 + c, (4 * to[0] + to[1]) * 2 + c))
    return lax.ppermute(value, ("z", "y", "core"), pairs)


def local(features, head_grad, branch_weight, proj_weight):
    shape = jax.ShapeDtypeStruct
    plane = ("z", "y")
    pos = jnp.stack([lax.axis_index(n).astype(jnp.int32) for n in ("z", "y", "core", "rep")])

    def exchange(value):
        return lax.all_to_all(value, plane, split_axis=0, concat_axis=0, tiled=True)

    first = call(
        split_kernel, shape((GROUPS, 32, KCH + BR), BF),
        [pltpu.VMEM((GROUPS + 2, 128, CH), F32)], 10**6,
        features.reshape(128, 2048), head_grad.reshape(128, BR), scalar=False,
    )
    below, above = send(branch_weight, "y", 1), send(branch_weight, "y", -1)
    x = exchange(first).reshape(512, KCH + BR)
    below, above = gate((below, above), (x,))
    blocks = [branch_weight, below, above, send(below[0:CUT], "y", 1), send(above[CUT:29], "y", -1)]
    blocks = blocks + [swap(b) for b in blocks]
    results = call(
        forward_kernel,
        (shape((136, 1024), F32),) * 4 + (shape((512, CH), BF),) * 4,
        [
            pltpu.VMEM((29, KCH, BR), BF), pltpu.VMEM((7, 512, KCH), BF), pltpu.VMEM((512, 1024), F32),
            pltpu.SemaphoreType.DMA((10,)),
        ],
        4 * 10**9, pos, x, head_grad.reshape(128, BR), *blocks, raw=10,
    )
    sums = [results[0]] + [send(results[k], "z", k) for k in (1, 3, 2)]
    pieces = [results[4]] + [send(results[4 + k], "y", k) for k in (1, 2, 3)]
    turned, colsum = call(
        turn_kernel, (shape((7, CH, HALF), BF), shape((8, CH), F32)), [pltpu.VMEM((32, 4, 16, CH), BF)], 10**8,
        pos, *pieces,
    )
    keep, give, pay = call(
        middle_kernel,
        (shape((9, 16, 512), BF), shape((9, 16, 512), BF), shape((GROUPS, 96, BR), BF)),
        [], 2 * 10**8, pos, *sums, x, proj_weight, turned, raw=1,
    )
    block = call(pair_kernel, shape((2, 9, 16, 512), BF), [], 10**5, keep, swap(give), scalar=False)
    near = [block, cross(block, 1, False), cross(block, -1, False), cross(block, 2, False)]
    group, sums = call(
        group_kernel, (shape((4, 2, 8, 16, 512), BF), shape((8, 512), F32)), [], 10**5, *near, scalar=False
    )
    every = [group] + [cross(group, step, True) for step in (1, -1, 2)]
    sums = jnp.where(pos[2] == 0, sums, swap(sums))
    const, pool_grad, outer = call(
        pool_kernel, (shape((8, BR), F32), shape((8, BR), F32), shape((16, BR), F32)), [pltpu.VMEM((256, BR), F32)],
        10**7, pos, sums, proj_weight,
    )
    pay = exchange(pay)
    part = call(collect_kernel, shape((64, BR), F32), [], 10**6, pay, scalar=False)
    part = jnp.concatenate([part + swap(part), outer], axis=0)
    part = part + pair(part, "rep", 1)
    part = part + pair(part, "rep", 2)
    part = jnp.broadcast_to(part.astype(BF)[None], (GROUPS, 80, BR))
    below, = gate((every[1],), (part,))
    every = [every[0], below] + every[2:4]
    every = every + [swap(piece) for piece in every]
    dw, dw_other = call(
        weight_grad_kernel,
        (shape((29, 64, BR), BF), shape((29, 64, BR), BF)),
        [pltpu.VMEM((2 * GROUPS, 4, 16, 1024), BF), pltpu.VMEM((29, CH, BR), F32), pltpu.SemaphoreType.DMA((32,))],
        4 * 10**9, pos, turned, colsum, pool_grad, *every, raw=8,
    )
    quarters = call(
        add_kernel, (shape((464, BR), BF),) * 4, [], 10**6, pos, dw.reshape(1856, BR), swap(dw_other).reshape(1856, BR)
    )
    dx = call(
        field_grad_kernel,
        shape((2, HALF, 64), BF),
        [
            pltpu.VMEM((2 * (GROUPS + 2 * PAD), 4, 16, 1024), BF), pltpu.VMEM((29, CH, BR), BF),
            pltpu.VMEM((HALF, CH), F32), pltpu.SemaphoreType.DMA((32,)),
        ],
        4 * 10**9, pos, pool_grad, branch_weight, blocks[5], *every, quarters[0], raw=9,
    )
    terms = [quarters[0]] + [send(quarters[k], "rep", k) for k in (1, 3, 2)]
    dw = sum(term.astype(F32) for term in terms).astype(BF)
    dw = [dw] + [send(dw, "rep", step) for step in (1, -1, 2)]
    grad_branch = call(join_kernel, shape((1856, BR), F32), [], 10**6, pos, *dw).reshape(29, 64, BR)
    (part,) = gate((exchange(part),), (dw[0],))
    part = part.astype(F32)
    grad_proj = jnp.concatenate([part[:, 0:64].reshape(1024, BR), part[:, 64:80].reshape(256, BR)], axis=0)
    (const,) = gate((const,), (dw[0],))
    head_out = call(head_kernel, shape((128, BR), BF), [pltpu.VMEM((2, 128, 128), F32)], 10**6, pos, pay, const)
    mine, theirs = dx[0], swap(dx[1])
    even = jnp.where(pos[2] == 0, mine, theirs).reshape(GROUPS, 1, 2, 64, 64)
    odd = jnp.where(pos[2] == 0, theirs, mine).reshape(GROUPS, 1, 2, 64, 64)
    grad_features = jnp.concatenate([even, odd], axis=1).reshape(1, 64, 64, 64)
    return head_out.reshape(head_grad.shape), grad_features, grad_branch, grad_proj


def solution(mesh):
    fine = Mesh(mesh.devices.reshape(4, 4, 2, 4), ("z", "y", "core", "rep"))
    tile = ("z", "y", "core")
    return jax.shard_map(
        local,
        mesh=fine,
        in_specs=(P("rep", tile, None, None), P("rep", tile, None, None), P(None, tile, None), P()),
        out_specs=(P("rep", tile, None, None), P("rep", None, None, tile), P(None, tile, None), P()),
        check_vma=False,
    )
```

```python
import jax
import jax.numpy as jnp
from jax import lax
from jax.experimental import pallas as pl
from jax.experimental.pallas import tpu as pltpu
from jax.sharding import Mesh, PartitionSpec as P

GROUPS = 16
CH = 128
KCH = 512
BR = 256
HALF = 2048
PAD = 9
CUT = 15
SHIFTS = (0, -3, 3, -6, 6, -9, 9)
F32 = jnp.float32
BF = jnp.bfloat16
HIGH = lax.Precision.HIGHEST
ROWS_BY_COLS = (((1,), (1,)), ((), ()))
COLS_BY_COLS = (((0,), (0,)), ((), ()))


def shift_slot(j, b):
    return SHIFTS.index((b - 1) * 3 * (j + 1))


def column_shift(value, amount):
    if amount == 0:
        return value
    n = value.shape[0]
    col = lax.broadcasted_iota(jnp.int32, value.shape, 0) & 15
    rolled = pltpu.roll(value, (-amount) % n, 0)
    return jnp.where((col + amount >= 0) & (col + amount < 16), rolled, 0.0)


def wrap(value):
    return lax.rem(value + 8, 4)


def split_kernel(x_ref, hg_ref, first_ref, wide):
    for t in range(GROUPS):
        wide[t] = x_ref[:, CH * t : CH * (t + 1)].astype(F32)
    for t in range(2):
        wide[GROUPS + t] = hg_ref[:, CH * t : CH * (t + 1)].astype(F32)
    for v in range(4):
        for t in range(GROUPS + 2):
            part = wide[t, pl.ds(v, 32, stride=4), :].astype(BF)
            if t < GROUPS:
                place = CH * (t % 4)
                first_ref[4 * (t // 4) + v, :, place : place + CH] = part
            else:
                place = KCH + CH * (t - GROUPS)
                for z in range(4):
                    first_ref[4 * z + v, :, place : place + CH] = part


def weight_copies(pos_ref, blocks, w, sem):
    y, c = pos_ref[1], pos_ref[2]
    places = [(0, 0, 29), (-1, 0, 29), (1, 0, 29), (2, 0, CUT), (2, CUT, 29)]
    copies = []
    for side in range(2):
        for k, (step, low, high) in enumerate(places):
            core = c if side == 0 else 1 - c
            start = pl.multiple_of(wrap(y + step) * CH + core * 64, 64)
            n = len(copies)
            copies.append(
                pltpu.make_async_copy(blocks[n], w.at[pl.ds(low, high - low), pl.ds(start, 64), :], sem.at[n])
            )
    return copies


def forward_kernel(pos_ref, x_ref, hg_ref, *refs):
    blocks, outs, pieces, (w, xs, total, sem) = refs[:10], refs[10:15], refs[15:19], refs[19:]
    own_ref, plus_ref, minus_ref, plus_half, minus_half = outs
    copies = weight_copies(pos_ref, blocks, w, sem)
    for copy in copies:
        copy.start()
    for step in range(4):
        pieces[step][...] = x_ref[:, pl.ds(pl.multiple_of(wrap(pos_ref[1] + step) * CH, CH), CH)]
    wide = x_ref[:, 0:KCH].astype(F32)
    colsum = jnp.broadcast_to(jnp.sum(wide, axis=0, keepdims=True), (8, KCH))
    for slot, amount in enumerate(SHIFTS):
        if amount:
            xs[slot] = column_shift(wide, amount).astype(BF)
        else:
            xs[slot] = x_ref[:, 0:KCH]
    hsum = jnp.broadcast_to(jnp.sum(hg_ref[...].astype(F32), axis=0, keepdims=True), (8, BR))
    for copy in copies:
        copy.wait()
    pool = jnp.dot(colsum, w[28].astype(F32), precision=HIGH, preferred_element_type=F32)
    total[:, 0:BR] = jnp.dot(xs[0], w[0], preferred_element_type=F32)
    for j in range(3):
        cols = slice((j + 1) * BR, (j + 2) * BR)
        for a in (1, 0, 2):
            delta = 96 * (j + 1) * (a - 1)
            in_low, in_high = max(delta, 0), 512 + min(delta, 0)
            out_low, out_high = max(-delta, 0), 512 - max(delta, 0)
            left = jnp.concatenate([xs[shift_slot(j, b), in_low:in_high, :] for b in range(3)], axis=1)
            start = 1 + 9 * j + 3 * a
            part = jnp.dot(left, w[start : start + 3].reshape(3 * KCH, BR), preferred_element_type=F32)
            if a == 1:
                total[:, cols] = part
            else:
                total[out_low:out_high, cols] += part
    extra = jnp.concatenate([pool, hsum, jnp.zeros((8, 512), F32)], axis=1)
    z = pos_ref[0]

    def rows(step, low, size):
        return total[pl.ds(pl.multiple_of(wrap(z + step) * 128 + low, 64), size), :]

    own_ref[0:128, :] = rows(0, 0, 128)
    own_ref[128:136, :] = extra
    plus_ref[0:64, :] = rows(2, 0, 64)
    plus_ref[64:128, :] = rows(1, 64, 64)
    plus_ref[128:136, :] = extra
    minus_ref[0:64, :] = rows(2, 64, 64)
    minus_ref[64:72, :] = extra
    minus_ref[72:136, :] = rows(-1, 0, 64)
    plus_half[...] = rows(1, 0, 64)
    minus_half[0:64, :] = rows(-1, 64, 64)
    minus_half[64:72, :] = extra


def bridge_kernel(plus_half, from_low, minus_half, from_high, *refs):
    refs[3][...] = plus_half[...] + from_low[0:64, :]
    refs[4][...] = minus_half[...] + from_high[0:72, :]


def pair_kernel(first_ref, second_ref, out_ref):
    out_ref[0] = first_ref[...]
    out_ref[1] = second_ref[...]


def group_kernel(*refs):
    parts, (out_ref, sums_ref) = refs[:4], refs[4:]
    total = jnp.zeros((16, 512), F32)
    for k in range(4):
        for side in range(2):
            out_ref[k, side] = parts[k][side, 0:8]
            total = total + parts[k][side, 8].astype(F32)
    sums_ref[...] = jnp.broadcast_to(jnp.sum(total, axis=0, keepdims=True), (8, 512))


def turn_kernel(pos_ref, *refs):
    pieces, (xt_ref, colsum_ref, joined) = refs[:4], refs[4:]
    for k in range(4):
        joined[:, wrap(pos_ref[1] - k)] = pieces[k][...].reshape(32, 16, CH)
    total = jnp.zeros((1, CH), F32)
    for m in range(4):
        wide = joined[8 * m : 8 * (m + 1)].reshape(512, CH).astype(F32)
        total = total + jnp.sum(wide, axis=0, keepdims=True)
        for slot, amount in enumerate(SHIFTS):
            xt_ref[slot, :, pl.ds(m * 512, 512)] = column_shift(wide, amount).T.astype(BF)
    colsum_ref[...] = jnp.broadcast_to(total, (8, CH))


def middle_kernel(pos_ref, own, from_low, from_high, half_a, half_b, x_ref, pw_ref, _, keep_ref, give_ref, pay_ref):
    top = own[0:64, :] + from_high[72:136, :] + half_a[...]
    bottom = own[64:136, :] + from_low[64:136, :] + half_b[...]
    pre = jnp.concatenate([top, bottom[0:64, :]], axis=0)
    act = jnp.maximum(pre, 0.0).astype(BF)
    low = pw_ref[0:1024, :]
    hg = x_ref[pl.ds(pl.multiple_of(pos_ref[0] * 128, 128), 128), KCH:]
    back = lax.dot_general(hg, low, ROWS_BY_COLS, preferred_element_type=F32)
    grads = jnp.where(pre > 0, back, 0.0)
    first = pos_ref[2] == 0
    keep_ref[0:8] = jnp.where(first, grads[:, 0:512], grads[:, 512:1024]).astype(BF).reshape(8, 16, 512)
    give_ref[0:8] = jnp.where(first, grads[:, 512:1024], grads[:, 0:512]).astype(BF).reshape(8, 16, 512)
    sums = jnp.concatenate([bottom[64:72, 0:512]] * 2, axis=0)
    one = sums.astype(BF).astype(F32)
    two = (sums - one).astype(BF).astype(F32)
    row = lax.broadcasted_iota(jnp.int32, sums.shape, 0)
    terms = jnp.where(row == 0, one, jnp.where(row == 1, two, jnp.where(row == 2, sums - one - two, 0.0))).astype(BF)
    keep_ref[8] = terms
    give_ref[8] = terms
    head = jnp.dot(act, low, preferred_element_type=F32).astype(BF)
    proj = lax.dot_general(act, hg, COLS_BY_COLS, preferred_element_type=F32).astype(BF)
    for t in range(GROUPS):
        pay_ref[t, 0:64, :] = proj[64 * t : 64 * (t + 1), :]
        pay_ref[t, 64:96, :] = head[32 * (t % 4) : 32 * (t % 4 + 1), :]


def pool_kernel(pos_ref, sums_ref, pw_ref, const_ref, grad_ref, outer_ref, whole):
    pool = sums_ref[:, 0:BR] * (1.0 / 4096.0)
    hsum = sums_ref[:, BR : 2 * BR]
    act = jnp.maximum(pool, 0.0).astype(BF)
    high = pw_ref[1024:1280, :]
    const_ref[...] = jnp.dot(act, high, preferred_element_type=F32)
    grad = lax.dot_general(hsum, high.astype(F32), ROWS_BY_COLS, precision=HIGH, preferred_element_type=F32)
    grad_ref[...] = jnp.where(pool > 0, grad, 0.0)
    whole[...] = 0.125 * lax.dot_general(
        act.astype(F32), hsum, COLS_BY_COLS, precision=HIGH, preferred_element_type=F32
    )
    chunk = pos_ref[0] * 4 + pos_ref[1]
    outer_ref[...] = whole[pl.ds(pl.multiple_of(chunk * 16, 16), 16), :]


def collect_kernel(pay_ref, part_ref):
    total = pay_ref[0, 0:64, :].astype(F32)
    for t in range(1, GROUPS):
        total = total + pay_ref[t, 0:64, :].astype(F32)
    part_ref[...] = total


def head_kernel(pos_ref, pay_ref, const_ref, head_ref, wide):
    for v in range(4):
        piece = pay_ref[4 * pos_ref[0] + v, 64:96, :].astype(F32) + const_ref[0:1, :]
        wide[0, pl.ds(v, 32, stride=4), :] = piece[:, 0:128]
        wide[1, pl.ds(v, 32, stride=4), :] = piece[:, 128:256]
    head_ref[:, 0:128] = wide[0].astype(BF)
    head_ref[:, 128:256] = wide[1].astype(BF)


def gather_copies(pos_ref, blocks, g, sem, pad):
    z, y, c = pos_ref[0], pos_ref[1], pos_ref[2]
    copies = []
    for side in range(2):
        half = c if side == 0 else 1 - c
        for place, far in enumerate((0, -1, 1, 2)):
            for k, step in enumerate((0, -1, 1, 2)):
                src = blocks[4 * side + place].at[k, side]
                v = wrap(y + jnp.where(half == 0, step, far))
                group = wrap(z + jnp.where(half == 0, far, step))
                cols = pl.ds(pl.multiple_of(512 * half, 512), 512)
                dst = g.at[pl.ds(2 * pad + 8 * group, 8), v, :, cols]
                copies.append(pltpu.make_async_copy(src, dst, sem.at[len(copies)]))
    return copies


def weight_grad_kernel(pos_ref, xt_ref, colsum_ref, grad_ref, *refs):
    blocks, (own_ref, other_ref), (g, dw, sem) = refs[:8], refs[-5:-3], refs[-3:]
    copies = gather_copies(pos_ref, blocks, g, sem, 0)
    for copy in copies:
        copy.start()
    for copy in copies:
        copy.wait()

    def grads(low, high, cols):
        return g[low // 64 : high // 64, :, :, cols].reshape(high - low, BR)

    dw[0] = jnp.dot(xt_ref[0], grads(0, HALF, slice(0, BR)), preferred_element_type=F32)
    for j in range(3):
        cols = slice((j + 1) * BR, (j + 2) * BR)
        for a in range(3):
            delta = 3 * (j + 1) * (a - 1) * 128
            x_low, x_high = max(delta, 0), HALF + min(delta, 0)
            g_low, g_high = max(-delta, 0), HALF - max(delta, 0)
            left = jnp.concatenate([xt_ref[shift_slot(j, b), :, x_low:x_high] for b in range(3)], axis=0)
            part = jnp.dot(left, grads(g_low, g_high, cols), preferred_element_type=F32)
            start = 1 + 9 * j + 3 * a
            dw[start : start + 3] = part.reshape(3, CH, BR)
    dw[28] = lax.dot_general(
        colsum_ref[...], grad_ref[...], COLS_BY_COLS, precision=HIGH, preferred_element_type=F32
    ) * (0.125 / 4096.0)
    c = pos_ref[2]
    own_ref[...] = dw[:, pl.ds(pl.multiple_of(c * 64, 64), 64), :].astype(BF)
    other_ref[...] = dw[:, pl.ds(pl.multiple_of((1 - c) * 64, 64), 64), :].astype(BF)


def field_grad_kernel(pos_ref, grad_ref, own, other, *refs):
    blocks, dx_ref, (g, w, whole, sem) = refs[:8], refs[-5], refs[-4:]
    copies = gather_copies(pos_ref, blocks, g, sem, PAD)
    for copy in copies:
        copy.start()
    c = pos_ref[2]
    w[:, pl.ds(pl.multiple_of(c * 64, 64), 64), :] = own[...]
    w[:, pl.ds(pl.multiple_of((1 - c) * 64, 64), 64), :] = other[...]
    g[0 : 2 * PAD] = jnp.zeros((2 * PAD, 4, 16, 1024), BF)
    g[2 * (PAD + GROUPS) :] = jnp.zeros((2 * PAD, 4, 16, 1024), BF)
    field = lax.dot_general(
        grad_ref[...], w[28].astype(F32), ROWS_BY_COLS, precision=HIGH, preferred_element_type=F32
    )[0:1, :] * (1.0 / 4096.0)
    for copy in copies:
        copy.wait()

    def grads(low, cols):
        return g[2 * (PAD + low) : 2 * (PAD + low + 4), :, :, cols].reshape(512, BR)

    for m in range(4):
        acc = field + lax.dot_general(
            grads(4 * m, slice(0, BR)), w[0], ROWS_BY_COLS, preferred_element_type=F32
        )
        for j in range(3):
            steps = []
            for a in range(3):
                low = 4 * m - 3 * (j + 1) * (a - 1)
                if low + 3 >= 0 and low < GROUPS:
                    steps.append((a, low))
            left = jnp.concatenate([grads(low, slice((j + 1) * BR, (j + 2) * BR)) for _, low in steps], axis=1)
            right = jnp.concatenate(
                [w[1 + 9 * j + 3 * a : 4 + 9 * j + 3 * a].reshape(3 * CH, BR) for a, _ in steps], axis=1
            )
            spread = lax.dot_general(left, right, ROWS_BY_COLS, preferred_element_type=F32)
            for b in range(3):
                acc = acc + column_shift(spread[:, b * CH : (b + 1) * CH], -(b - 1) * 3 * (j + 1))
        for row in range(8):
            for v in range(4):
                place = (4 * row + v) * 16
                whole[pl.ds(512 * m + 64 * row + v, 16, stride=4), :] = acc[place : place + 16, :]
    low, high = whole[:, 0:64], whole[:, 64:128]
    dx_ref[0] = jnp.where(c == 0, low, high).astype(BF)
    dx_ref[1] = jnp.where(c == 0, high, low).astype(BF)


def add_kernel(pos_ref, own, other, *outs):
    r = pos_ref[3]
    for k in range(4):
        rows = pl.ds(pl.multiple_of(wrap(r + k) * 464, 16), 464)
        outs[k][...] = (own[rows, :].astype(F32) + other[rows, :].astype(F32)).astype(BF)


def join_kernel(pos_ref, *refs):
    for k, step in enumerate((0, -1, 1, 2)):
        rows = pl.ds(pl.multiple_of(wrap(pos_ref[3] + step) * 464, 8), 464)
        refs[4][rows, :] = refs[k][...].astype(F32)


ROOM = {"forward_kernel": 28, "weight_grad_kernel": 26, "field_grad_kernel": 28, "turn_kernel": 16, "middle_kernel": 16}


def call(kernel, out_shape, scratch, flops, *args, scalar=True, raw=0):
    specs = [pl.BlockSpec(memory_space=pltpu.VMEM) for _ in args]
    if scalar:
        specs[0] = pl.BlockSpec(memory_space=pltpu.SMEM)
    for k in range(raw):
        specs[len(args) - 1 - k] = pl.BlockSpec(memory_space=pl.ANY)
    moved = sum(a.size * a.dtype.itemsize for a in jax.tree.leaves((args, out_shape)))
    return pl.pallas_call(
        kernel,
        out_shape=out_shape,
        in_specs=specs,
        out_specs=jax.tree.map(lambda _: pl.BlockSpec(memory_space=pltpu.VMEM), out_shape),
        scratch_shapes=scratch,
        compiler_params=pltpu.CompilerParams(vmem_limit_bytes=ROOM.get(kernel.__name__, 12) * 2**20),
        cost_estimate=pl.CostEstimate(flops=flops, bytes_accessed=moved, transcendentals=0),
        name=kernel.__name__,
    )(*args)


def gate(values, after):
    anywhere = pl.BlockSpec(memory_space=pl.ANY)
    return pl.pallas_call(
        lambda *refs: None,
        out_shape=tuple(jax.ShapeDtypeStruct(v.shape, v.dtype) for v in values),
        in_specs=[anywhere] * (len(values) + len(after)),
        out_specs=(anywhere,) * len(values),
        input_output_aliases={k: k for k in range(len(values))},
        cost_estimate=pl.CostEstimate(flops=0, bytes_accessed=0, transcendentals=0),
    )(*values, *after)


def swap(value):
    return lax.ppermute(value, "core", [(0, 1), (1, 0)])


def send(value, axis, step):
    return lax.ppermute(value, axis, [(k, (k + step) % 4) for k in range(4)])


def pair(value, axis, bit):
    return lax.ppermute(value, axis, [(k, k ^ bit) for k in range(4)])


def cross(value, step, turn):
    pairs = []
    for z in range(4):
        for y in range(4):
            for c in range(2):
                along_y = (c == 0) != turn
                to = (z, (y + step) % 4) if along_y else ((z + step) % 4, y)
                pairs.append(((4 * z + y) * 2 + c, (4 * to[0] + to[1]) * 2 + c))
    return lax.ppermute(value, ("z", "y", "core"), pairs)


def local(features, head_grad, branch_weight, proj_weight):
    shape = jax.ShapeDtypeStruct
    plane = ("z", "y")
    pos = jnp.stack([lax.axis_index(n).astype(jnp.int32) for n in ("z", "y", "core", "rep")])

    def exchange(value):
        return lax.all_to_all(value, plane, split_axis=0, concat_axis=0, tiled=True)

    first = call(
        split_kernel, shape((GROUPS, 32, KCH + BR), BF),
        [pltpu.VMEM((GROUPS + 2, 128, CH), F32)], 10**6,
        features.reshape(128, 2048), head_grad.reshape(128, BR), scalar=False,
    )
    below, above = send(branch_weight, "y", 1), send(branch_weight, "y", -1)
    x = exchange(first).reshape(512, KCH + BR)
    below, above = gate((below, above), (x,))
    blocks = [branch_weight, below, above, send(below[0:CUT], "y", 1), send(above[CUT:29], "y", -1)]
    blocks = blocks + [swap(b) for b in blocks]
    own, plus, minus, plus_half, minus_half, *pieces = call(
        forward_kernel,
        tuple(shape((n, 1024), F32) for n in (136, 136, 136, 64, 72)) + (shape((512, CH), BF),) * 4,
        [
            pltpu.VMEM((29, KCH, BR), BF), pltpu.VMEM((7, 512, KCH), BF), pltpu.VMEM((512, 1024), F32),
            pltpu.SemaphoreType.DMA((10,)),
        ],
        4 * 10**9, pos, x, head_grad.reshape(128, BR), *blocks, raw=10,
    )
    from_low, from_high = send(plus, "z", 1), send(minus, "z", -1)
    pieces = [pieces[0]] + [send(pieces[k], "y", k) for k in (1, 2, 3)]
    half_a, half_b = call(
        bridge_kernel, (shape((64, 1024), F32), shape((72, 1024), F32)), [], 10**5,
        plus_half, from_low, minus_half, from_high, *pieces[1:], scalar=False,
    )
    half_a, half_b = send(half_a, "z", 1), send(half_b, "z", -1)
    turned, colsum = call(
        turn_kernel, (shape((7, CH, HALF), BF), shape((8, CH), F32)), [pltpu.VMEM((32, 4, 16, CH), BF)], 10**8,
        pos, *pieces,
    )
    keep, give, pay = call(
        middle_kernel,
        (shape((9, 16, 512), BF), shape((9, 16, 512), BF), shape((GROUPS, 96, BR), BF)),
        [], 2 * 10**8, pos, own, from_low, from_high, half_a, half_b, x, proj_weight, colsum,
    )
    block = call(pair_kernel, shape((2, 9, 16, 512), BF), [], 10**5, keep, swap(give), scalar=False)
    near = [block, cross(block, 1, False), cross(block, -1, False), cross(block, 2, False)]
    group, sums = call(
        group_kernel, (shape((4, 2, 8, 16, 512), BF), shape((8, 512), F32)), [], 10**5, *near, scalar=False
    )
    every = [group] + [cross(group, step, True) for step in (1, -1, 2)]
    sums = jnp.where(pos[2] == 0, sums, swap(sums))
    const, pool_grad, outer = call(
        pool_kernel, (shape((8, BR), F32), shape((8, BR), F32), shape((16, BR), F32)), [pltpu.VMEM((256, BR), F32)],
        10**7, pos, sums, proj_weight,
    )
    pay = exchange(pay)
    part = call(collect_kernel, shape((64, BR), F32), [], 10**6, pay, scalar=False)
    part = jnp.concatenate([part + swap(part), outer], axis=0)
    part = part + pair(part, "rep", 1)
    part = part + pair(part, "rep", 2)
    part = jnp.broadcast_to(part.astype(BF)[None], (GROUPS, 80, BR))
    below, = gate((every[1],), (part,))
    every = [every[0], below] + every[2:4]
    every = every + [swap(piece) for piece in every]
    dw, dw_other = call(
        weight_grad_kernel,
        (shape((29, 64, BR), BF), shape((29, 64, BR), BF)),
        [pltpu.VMEM((2 * GROUPS, 4, 16, 1024), BF), pltpu.VMEM((29, CH, BR), F32), pltpu.SemaphoreType.DMA((32,))],
        4 * 10**9, pos, turned, colsum, pool_grad, *every, raw=8,
    )
    quarters = call(
        add_kernel, (shape((464, BR), BF),) * 4, [], 10**6, pos, dw.reshape(1856, BR), swap(dw_other).reshape(1856, BR)
    )
    dx = call(
        field_grad_kernel,
        shape((2, HALF, 64), BF),
        [
            pltpu.VMEM((2 * (GROUPS + 2 * PAD), 4, 16, 1024), BF), pltpu.VMEM((29, CH, BR), BF),
            pltpu.VMEM((HALF, CH), F32), pltpu.SemaphoreType.DMA((32,)),
        ],
        4 * 10**9, pos, pool_grad, branch_weight, blocks[5], *every, quarters[0], raw=9,
    )
    terms = [quarters[0]] + [send(quarters[k], "rep", k) for k in (1, 3, 2)]
    dw = sum(term.astype(F32) for term in terms).astype(BF)
    dw = [dw] + [send(dw, "rep", step) for step in (1, -1, 2)]
    grad_branch = call(join_kernel, shape((1856, BR), F32), [], 10**6, pos, *dw).reshape(29, 64, BR)
    (part,) = gate((exchange(part),), (dw[0],))
    part = part.astype(F32)
    grad_proj = jnp.concatenate([part[:, 0:64].reshape(1024, BR), part[:, 64:80].reshape(256, BR)], axis=0)
    (const,) = gate((const,), (dw[0],))
    head_out = call(head_kernel, shape((128, BR), BF), [pltpu.VMEM((2, 128, 128), F32)], 10**6, pos, pay, const)
    mine, theirs = dx[0], swap(dx[1])
    even = jnp.where(pos[2] == 0, mine, theirs).reshape(GROUPS, 1, 2, 64, 64)
    odd = jnp.where(pos[2] == 0, theirs, mine).reshape(GROUPS, 1, 2, 64, 64)
    grad_features = jnp.concatenate([even, odd], axis=1).reshape(1, 64, 64, 64)
    return head_out.reshape(head_grad.shape), grad_features, grad_branch, grad_proj


def solution(mesh):
    fine = Mesh(mesh.devices.reshape(4, 4, 2, 4), ("z", "y", "core", "rep"))
    tile = ("z", "y", "core")
    return jax.shard_map(
        local,
        mesh=fine,
        in_specs=(P("rep", tile, None, None), P("rep", tile, None, None), P(None, tile, None), P()),
        out_specs=(P("rep", tile, None, None), P("rep", None, None, tile), P(None, tile, None), P()),
        check_vma=False,
    )
```

```python
import jax
import jax.numpy as jnp
from jax import lax
from jax.experimental import pallas as pl
from jax.experimental.pallas import tpu as pltpu
from jax.sharding import Mesh, PartitionSpec as P

GROUPS = 16
CH = 128
KCH = 512
BR = 256
HALF = 2048
PAD = 9
CUT = 15
SHIFTS = (0, -3, 3, -6, 6, -9, 9)
F32 = jnp.float32
BF = jnp.bfloat16
HIGH = lax.Precision.HIGHEST
ROWS_BY_COLS = (((1,), (1,)), ((), ()))
COLS_BY_COLS = (((0,), (0,)), ((), ()))


def shift_slot(j, b):
    return SHIFTS.index((b - 1) * 3 * (j + 1))


def column_shift(value, amount):
    if amount == 0:
        return value
    n = value.shape[0]
    col = lax.broadcasted_iota(jnp.int32, value.shape, 0) & 15
    rolled = pltpu.roll(value, (-amount) % n, 0)
    return jnp.where((col + amount >= 0) & (col + amount < 16), rolled, 0.0)


def wrap(value):
    return lax.rem(value + 8, 4)


def split_kernel(x_ref, hg_ref, first_ref, wide):
    for t in range(GROUPS):
        wide[t] = x_ref[:, CH * t : CH * (t + 1)].astype(F32)
    for t in range(2):
        wide[GROUPS + t] = hg_ref[:, CH * t : CH * (t + 1)].astype(F32)
    for v in range(4):
        for t in range(GROUPS + 2):
            part = wide[t, pl.ds(v, 32, stride=4), :].astype(BF)
            if t < GROUPS:
                place = CH * (t % 4)
                first_ref[4 * (t // 4) + v, :, place : place + CH] = part
            else:
                place = KCH + CH * (t - GROUPS)
                for z in range(4):
                    first_ref[4 * z + v, :, place : place + CH] = part


def weight_copies(pos_ref, blocks, w, sem):
    y, c = pos_ref[1], pos_ref[2]
    places = [(0, 0, 29), (-1, 0, 29), (1, 0, 29), (2, 0, CUT), (2, CUT, 29)]
    copies = []
    for side in range(2):
        for k, (step, low, high) in enumerate(places):
            core = c if side == 0 else 1 - c
            start = pl.multiple_of(wrap(y + step) * CH + core * 64, 64)
            n = len(copies)
            copies.append(
                pltpu.make_async_copy(blocks[n], w.at[pl.ds(low, high - low), pl.ds(start, 64), :], sem.at[n])
            )
    return copies


def forward_kernel(pos_ref, x_ref, hg_ref, *refs):
    blocks, outs, pieces, (w, xs, total, sem) = refs[:10], refs[10:15], refs[15:19], refs[19:]
    own_ref, plus_ref, minus_ref, plus_half, minus_half = outs
    copies = weight_copies(pos_ref, blocks, w, sem)
    for copy in copies:
        copy.start()
    for step in range(4):
        pieces[step][...] = x_ref[:, pl.ds(pl.multiple_of(wrap(pos_ref[1] + step) * CH, CH), CH)]
    wide = x_ref[:, 0:KCH].astype(F32)
    colsum = jnp.broadcast_to(jnp.sum(wide, axis=0, keepdims=True), (8, KCH))
    for slot, amount in enumerate(SHIFTS):
        if amount:
            xs[slot] = column_shift(wide, amount).astype(BF)
        else:
            xs[slot] = x_ref[:, 0:KCH]
    hsum = jnp.broadcast_to(jnp.sum(hg_ref[...].astype(F32), axis=0, keepdims=True), (8, BR))
    for copy in copies:
        copy.wait()
    pool = jnp.dot(colsum, w[28].astype(F32), precision=HIGH, preferred_element_type=F32)
    total[:, 0:BR] = jnp.dot(xs[0], w[0], preferred_element_type=F32)
    for j in range(3):
        cols = slice((j + 1) * BR, (j + 2) * BR)
        for a in (1, 0, 2):
            delta = 96 * (j + 1) * (a - 1)
            in_low, in_high = max(delta, 0), 512 + min(delta, 0)
            out_low, out_high = max(-delta, 0), 512 - max(delta, 0)
            left = jnp.concatenate([xs[shift_slot(j, b), in_low:in_high, :] for b in range(3)], axis=1)
            start = 1 + 9 * j + 3 * a
            part = jnp.dot(left, w[start : start + 3].reshape(3 * KCH, BR), preferred_element_type=F32)
            if a == 1:
                total[:, cols] = part
            else:
                total[out_low:out_high, cols] += part
    extra = jnp.concatenate([pool, hsum, jnp.zeros((8, 512), F32)], axis=1)
    z = pos_ref[0]

    def rows(step, low, size):
        return total[pl.ds(pl.multiple_of(wrap(z + step) * 128 + low, 64), size), :]

    own_ref[0:128, :] = rows(0, 0, 128)
    own_ref[128:136, :] = extra
    plus_ref[0:64, :] = rows(2, 0, 64)
    plus_ref[64:128, :] = rows(1, 64, 64)
    plus_ref[128:136, :] = extra
    minus_ref[0:64, :] = rows(2, 64, 64)
    minus_ref[64:72, :] = extra
    minus_ref[72:136, :] = rows(-1, 0, 64)
    plus_half[...] = rows(1, 0, 64)
    minus_half[0:64, :] = rows(-1, 64, 64)
    minus_half[64:72, :] = extra


def bridge_kernel(plus_half, from_low, minus_half, from_high, *refs):
    refs[3][...] = plus_half[...] + from_low[0:64, :]
    refs[4][...] = minus_half[...] + from_high[0:72, :]


def pair_kernel(first_ref, second_ref, out_ref):
    out_ref[0] = first_ref[...]
    out_ref[1] = second_ref[...]


def group_kernel(*refs):
    parts, (out_ref, sums_ref) = refs[:4], refs[4:]
    total = jnp.zeros((16, 512), F32)
    for k in range(4):
        for side in range(2):
            out_ref[k, side] = parts[k][side, 0:8]
            total = total + parts[k][side, 8].astype(F32)
    sums_ref[...] = jnp.broadcast_to(jnp.sum(total, axis=0, keepdims=True), (8, 512))


def turn_kernel(pos_ref, *refs):
    pieces, (xt_ref, colsum_ref, joined) = refs[:4], refs[4:]
    for k in range(4):
        joined[:, wrap(pos_ref[1] - k)] = pieces[k][...].reshape(32, 16, CH)
    total = jnp.zeros((1, CH), F32)
    for m in range(4):
        wide = joined[8 * m : 8 * (m + 1)].reshape(512, CH).astype(F32)
        total = total + jnp.sum(wide, axis=0, keepdims=True)
        for slot, amount in enumerate(SHIFTS):
            xt_ref[slot, :, pl.ds(m * 512, 512)] = column_shift(wide, amount).T.astype(BF)
    colsum_ref[...] = jnp.broadcast_to(total, (8, CH))


def middle_kernel(pos_ref, own, from_low, from_high, half_a, half_b, x_ref, pw_ref, _, keep_ref, give_ref, pay_ref):
    top = own[0:64, :] + from_high[72:136, :] + half_a[...]
    bottom = own[64:136, :] + from_low[64:136, :] + half_b[...]
    pre = jnp.concatenate([top, bottom[0:64, :]], axis=0)
    act = jnp.maximum(pre, 0.0).astype(BF)
    low = pw_ref[0:1024, :]
    hg = x_ref[pl.ds(pl.multiple_of(pos_ref[0] * 128, 128), 128), KCH:]
    back = lax.dot_general(hg, low, ROWS_BY_COLS, preferred_element_type=F32)
    grads = jnp.where(pre > 0, back, 0.0)
    first = pos_ref[2] == 0
    keep_ref[0:8] = jnp.where(first, grads[:, 0:512], grads[:, 512:1024]).astype(BF).reshape(8, 16, 512)
    give_ref[0:8] = jnp.where(first, grads[:, 512:1024], grads[:, 0:512]).astype(BF).reshape(8, 16, 512)
    sums = jnp.concatenate([bottom[64:72, 0:512]] * 2, axis=0)
    one = sums.astype(BF).astype(F32)
    two = (sums - one).astype(BF).astype(F32)
    row = lax.broadcasted_iota(jnp.int32, sums.shape, 0)
    terms = jnp.where(row == 0, one, jnp.where(row == 1, two, jnp.where(row == 2, sums - one - two, 0.0))).astype(BF)
    keep_ref[8] = terms
    give_ref[8] = terms
    head = jnp.dot(act, low, preferred_element_type=F32).astype(BF)
    proj = lax.dot_general(act, hg, COLS_BY_COLS, preferred_element_type=F32).astype(BF)
    for t in range(GROUPS):
        pay_ref[t, 0:64, :] = proj[64 * t : 64 * (t + 1), :]
        pay_ref[t, 64:96, :] = head[32 * (t % 4) : 32 * (t % 4 + 1), :]


def pool_kernel(pos_ref, sums_ref, pw_ref, const_ref, grad_ref, outer_ref, whole):
    pool = sums_ref[:, 0:BR] * (1.0 / 4096.0)
    hsum = sums_ref[:, BR : 2 * BR]
    act = jnp.maximum(pool, 0.0).astype(BF)
    high = pw_ref[1024:1280, :]
    const_ref[...] = jnp.dot(act, high, preferred_element_type=F32)
    grad = lax.dot_general(hsum, high.astype(F32), ROWS_BY_COLS, precision=HIGH, preferred_element_type=F32)
    grad_ref[...] = jnp.where(pool > 0, grad, 0.0)
    whole[...] = 0.125 * lax.dot_general(
        act.astype(F32), hsum, COLS_BY_COLS, precision=HIGH, preferred_element_type=F32
    )
    chunk = pos_ref[0] * 4 + pos_ref[1]
    outer_ref[...] = whole[pl.ds(pl.multiple_of(chunk * 16, 16), 16), :]


def collect_kernel(pay_ref, part_ref):
    total = pay_ref[0, 0:64, :].astype(F32)
    for t in range(1, GROUPS):
        total = total + pay_ref[t, 0:64, :].astype(F32)
    part_ref[...] = total


def head_kernel(pos_ref, pay_ref, const_ref, head_ref, wide):
    for v in range(4):
        piece = pay_ref[4 * pos_ref[0] + v, 64:96, :].astype(F32) + const_ref[0:1, :]
        wide[0, pl.ds(v, 32, stride=4), :] = piece[:, 0:128]
        wide[1, pl.ds(v, 32, stride=4), :] = piece[:, 128:256]
    head_ref[:, 0:128] = wide[0].astype(BF)
    head_ref[:, 128:256] = wide[1].astype(BF)


def gather_copies(pos_ref, blocks, g, sem, pad):
    z, y, c = pos_ref[0], pos_ref[1], pos_ref[2]
    copies = []
    for side in range(2):
        half = c if side == 0 else 1 - c
        for place, far in enumerate((0, -1, 1, 2)):
            for k, step in enumerate((0, -1, 1, 2)):
                src = blocks[4 * side + place].at[k, side]
                v = wrap(y + jnp.where(half == 0, step, far))
                group = wrap(z + jnp.where(half == 0, far, step))
                cols = pl.ds(pl.multiple_of(512 * half, 512), 512)
                dst = g.at[pl.ds(2 * pad + 8 * group, 8), v, :, cols]
                copies.append(pltpu.make_async_copy(src, dst, sem.at[len(copies)]))
    return copies


def weight_grad_kernel(pos_ref, xt_ref, colsum_ref, grad_ref, *refs):
    blocks, (own_ref, other_ref), (g, dw, sem) = refs[:8], refs[-5:-3], refs[-3:]
    copies = gather_copies(pos_ref, blocks, g, sem, 0)
    for copy in copies:
        copy.start()
    for copy in copies:
        copy.wait()

    def grads(low, high, cols):
        return g[low // 64 : high // 64, :, :, cols].reshape(high - low, BR)

    dw[0] = jnp.dot(xt_ref[0], grads(0, HALF, slice(0, BR)), preferred_element_type=F32)
    for j in range(3):
        cols = slice((j + 1) * BR, (j + 2) * BR)
        for a in range(3):
            delta = 3 * (j + 1) * (a - 1) * 128
            x_low, x_high = max(delta, 0), HALF + min(delta, 0)
            g_low, g_high = max(-delta, 0), HALF - max(delta, 0)
            left = jnp.concatenate([xt_ref[shift_slot(j, b), :, x_low:x_high] for b in range(3)], axis=0)
            part = jnp.dot(left, grads(g_low, g_high, cols), preferred_element_type=F32)
            start = 1 + 9 * j + 3 * a
            dw[start : start + 3] = part.reshape(3, CH, BR)
    dw[28] = lax.dot_general(
        colsum_ref[...], grad_ref[...], COLS_BY_COLS, precision=HIGH, preferred_element_type=F32
    ) * (0.125 / 4096.0)
    c = pos_ref[2]
    own_ref[...] = dw[:, pl.ds(pl.multiple_of(c * 64, 64), 64), :].astype(BF)
    other_ref[...] = dw[:, pl.ds(pl.multiple_of((1 - c) * 64, 64), 64), :].astype(BF)


def field_grad_kernel(pos_ref, grad_ref, own, other, *refs):
    blocks, dx_ref, (g, w, whole, sem) = refs[:8], refs[-5], refs[-4:]
    copies = gather_copies(pos_ref, blocks, g, sem, PAD)
    for copy in copies:
        copy.start()
    c = pos_ref[2]
    w[:, pl.ds(pl.multiple_of(c * 64, 64), 64), :] = own[...]
    w[:, pl.ds(pl.multiple_of((1 - c) * 64, 64), 64), :] = other[...]
    g[0 : 2 * PAD] = jnp.zeros((2 * PAD, 4, 16, 1024), BF)
    g[2 * (PAD + GROUPS) :] = jnp.zeros((2 * PAD, 4, 16, 1024), BF)
    field = lax.dot_general(
        grad_ref[...], w[28].astype(F32), ROWS_BY_COLS, precision=HIGH, preferred_element_type=F32
    )[0:1, :] * (1.0 / 4096.0)
    for copy in copies:
        copy.wait()

    def grads(low, cols):
        return g[2 * (PAD + low) : 2 * (PAD + low + 4), :, :, cols].reshape(512, BR)

    for m in range(4):
        acc = field + lax.dot_general(
            grads(4 * m, slice(0, BR)), w[0], ROWS_BY_COLS, preferred_element_type=F32
        )
        for j in range(3):
            steps = []
            for a in range(3):
                low = 4 * m - 3 * (j + 1) * (a - 1)
                if low + 3 >= 0 and low < GROUPS:
                    steps.append((a, low))
            left = jnp.concatenate([grads(low, slice((j + 1) * BR, (j + 2) * BR)) for _, low in steps], axis=1)
            right = jnp.concatenate(
                [w[1 + 9 * j + 3 * a : 4 + 9 * j + 3 * a].reshape(3 * CH, BR) for a, _ in steps], axis=1
            )
            spread = lax.dot_general(left, right, ROWS_BY_COLS, preferred_element_type=F32)
            for b in range(3):
                acc = acc + column_shift(spread[:, b * CH : (b + 1) * CH], -(b - 1) * 3 * (j + 1))
        for row in range(8):
            for v in range(4):
                place = (4 * row + v) * 16
                whole[pl.ds(512 * m + 64 * row + v, 16, stride=4), :] = acc[place : place + 16, :]
    low, high = whole[:, 0:64], whole[:, 64:128]
    dx_ref[0] = jnp.where(c == 0, low, high).astype(BF)
    dx_ref[1] = jnp.where(c == 0, high, low).astype(BF)


def add_kernel(pos_ref, own, other, *outs):
    r = pos_ref[3]
    for k in range(4):
        rows = pl.ds(pl.multiple_of(wrap(r + k) * 464, 16), 464)
        outs[k][...] = (own[rows, :].astype(F32) + other[rows, :].astype(F32)).astype(BF)


def join_kernel(pos_ref, *refs):
    for k, step in enumerate((0, -1, 1, 2)):
        rows = pl.ds(pl.multiple_of(wrap(pos_ref[3] + step) * 464, 8), 464)
        refs[4][rows, :] = refs[k][...].astype(F32)


ROOM = {"forward_kernel": 28, "weight_grad_kernel": 26, "field_grad_kernel": 28, "turn_kernel": 16, "middle_kernel": 16}


def call(kernel, out_shape, scratch, flops, *args, scalar=True, raw=0):
    specs = [pl.BlockSpec(memory_space=pltpu.VMEM) for _ in args]
    if scalar:
        specs[0] = pl.BlockSpec(memory_space=pltpu.SMEM)
    for k in range(raw):
        specs[len(args) - 1 - k] = pl.BlockSpec(memory_space=pl.ANY)
    moved = sum(a.size * a.dtype.itemsize for a in jax.tree.leaves((args, out_shape)))
    return pl.pallas_call(
        kernel,
        out_shape=out_shape,
        in_specs=specs,
        out_specs=jax.tree.map(lambda _: pl.BlockSpec(memory_space=pltpu.VMEM), out_shape),
        scratch_shapes=scratch,
        compiler_params=pltpu.CompilerParams(vmem_limit_bytes=ROOM.get(kernel.__name__, 12) * 2**20),
        cost_estimate=pl.CostEstimate(flops=flops, bytes_accessed=moved, transcendentals=0),
        name=kernel.__name__,
    )(*args)


def gate(values, after):
    anywhere = pl.BlockSpec(memory_space=pl.ANY)
    return pl.pallas_call(
        lambda *refs: None,
        out_shape=tuple(jax.ShapeDtypeStruct(v.shape, v.dtype) for v in values),
        in_specs=[anywhere] * (len(values) + len(after)),
        out_specs=(anywhere,) * len(values),
        input_output_aliases={k: k for k in range(len(values))},
        cost_estimate=pl.CostEstimate(flops=0, bytes_accessed=0, transcendentals=0),
    )(*values, *after)


def swap(value):
    return lax.ppermute(value, "core", [(0, 1), (1, 0)])


def send(value, axis, step):
    return lax.ppermute(value, axis, [(k, (k + step) % 4) for k in range(4)])


def pair(value, axis, bit):
    return lax.ppermute(value, axis, [(k, k ^ bit) for k in range(4)])


def cross(value, step, turn):
    pairs = []
    for z in range(4):
        for y in range(4):
            for c in range(2):
                along_y = (c == 0) != turn
                to = (z, (y + step) % 4) if along_y else ((z + step) % 4, y)
                pairs.append(((4 * z + y) * 2 + c, (4 * to[0] + to[1]) * 2 + c))
    return lax.ppermute(value, ("z", "y", "core"), pairs)


def local(features, head_grad, branch_weight, proj_weight):
    shape = jax.ShapeDtypeStruct
    plane = ("z", "y")
    pos = jnp.stack([lax.axis_index(n).astype(jnp.int32) for n in ("z", "y", "core", "rep")])

    def exchange(value):
        return lax.all_to_all(value, plane, split_axis=0, concat_axis=0, tiled=True)

    first = call(
        split_kernel, shape((GROUPS, 32, KCH + BR), BF),
        [pltpu.VMEM((GROUPS + 2, 128, CH), F32)], 10**6,
        features.reshape(128, 2048), head_grad.reshape(128, BR), scalar=False,
    )
    below, above = send(branch_weight, "y", 1), send(branch_weight, "y", -1)
    x = exchange(first).reshape(512, KCH + BR)
    below, above = gate((below, above), (x,))
    blocks = [branch_weight, below, above, send(below[0:CUT], "y", 1), send(above[CUT:29], "y", -1)]
    blocks = blocks + [swap(b) for b in blocks]
    own, plus, minus, plus_half, minus_half, *pieces = call(
        forward_kernel,
        tuple(shape((n, 1024), F32) for n in (136, 136, 136, 64, 72)) + (shape((512, CH), BF),) * 4,
        [
            pltpu.VMEM((29, KCH, BR), BF), pltpu.VMEM((7, 512, KCH), BF), pltpu.VMEM((512, 1024), F32),
            pltpu.SemaphoreType.DMA((10,)),
        ],
        4 * 10**9, pos, x, head_grad.reshape(128, BR), *blocks, raw=10,
    )
    from_low, from_high = send(plus, "z", 1), send(minus, "z", -1)
    pieces = [pieces[0]] + [send(pieces[k], "y", k) for k in (1, 2, 3)]
    half_a, half_b = call(
        bridge_kernel, (shape((64, 1024), F32), shape((72, 1024), F32)), [], 10**5,
        plus_half, from_low, minus_half, from_high, *pieces[1:], scalar=False,
    )
    half_a, half_b = send(half_a, "z", 1), send(half_b, "z", -1)
    turned, colsum = call(
        turn_kernel, (shape((7, CH, HALF), BF), shape((8, CH), F32)), [pltpu.VMEM((32, 4, 16, CH), BF)], 10**8,
        pos, *pieces,
    )
    keep, give, pay = call(
        middle_kernel,
        (shape((9, 16, 512), BF), shape((9, 16, 512), BF), shape((GROUPS, 96, BR), BF)),
        [], 2 * 10**8, pos, own, from_low, from_high, half_a, half_b, x, proj_weight, colsum,
    )
    block = call(pair_kernel, shape((2, 9, 16, 512), BF), [], 10**5, keep, swap(give), scalar=False)
    near = [block, cross(block, 1, False), cross(block, -1, False), cross(block, 2, False)]
    group, sums = call(
        group_kernel, (shape((4, 2, 8, 16, 512), BF), shape((8, 512), F32)), [], 10**10, *near, scalar=False
    )
    every = [group] + [cross(group, step, True) for step in (1, -1, 2)]
    sums = jnp.where(pos[2] == 0, sums, swap(sums))
    const, pool_grad, outer = call(
        pool_kernel, (shape((8, BR), F32), shape((8, BR), F32), shape((16, BR), F32)), [pltpu.VMEM((256, BR), F32)],
        10**7, pos, sums, proj_weight,
    )
    pay = exchange(pay)
    part = call(collect_kernel, shape((64, BR), F32), [], 10**6, pay, scalar=False)
    part = jnp.concatenate([part + swap(part), outer], axis=0)
    part = part + pair(part, "rep", 1)
    part = part + pair(part, "rep", 2)
    part = jnp.broadcast_to(part.astype(BF)[None], (GROUPS, 80, BR))
    below, = gate((every[1],), (part,))
    every = [every[0], below] + every[2:4]
    every = every + [swap(piece) for piece in every]
    dw, dw_other = call(
        weight_grad_kernel,
        (shape((29, 64, BR), BF), shape((29, 64, BR), BF)),
        [pltpu.VMEM((2 * GROUPS, 4, 16, 1024), BF), pltpu.VMEM((29, CH, BR), F32), pltpu.SemaphoreType.DMA((32,))],
        4 * 10**9, pos, turned, colsum, pool_grad, *every, raw=8,
    )
    quarters = call(
        add_kernel, (shape((464, BR), BF),) * 4, [], 10**6, pos, dw.reshape(1856, BR), swap(dw_other).reshape(1856, BR)
    )
    dx = call(
        field_grad_kernel,
        shape((2, HALF, 64), BF),
        [
            pltpu.VMEM((2 * (GROUPS + 2 * PAD), 4, 16, 1024), BF), pltpu.VMEM((29, CH, BR), BF),
            pltpu.VMEM((HALF, CH), F32), pltpu.SemaphoreType.DMA((32,)),
        ],
        4 * 10**9, pos, pool_grad, branch_weight, blocks[5], *every, quarters[0], raw=9,
    )
    terms = [quarters[0]] + [send(quarters[k], "rep", k) for k in (1, 3, 2)]
    dw = sum(term.astype(F32) for term in terms).astype(BF)
    dw = [dw] + [send(dw, "rep", step) for step in (1, -1, 2)]
    grad_branch = call(join_kernel, shape((1856, BR), F32), [], 10**6, pos, *dw).reshape(29, 64, BR)
    (part,) = gate((exchange(part),), (dw[0],))
    part = part.astype(F32)
    grad_proj = jnp.concatenate([part[:, 0:64].reshape(1024, BR), part[:, 64:80].reshape(256, BR)], axis=0)
    (const,) = gate((const,), (dw[0],))
    head_out = call(head_kernel, shape((128, BR), BF), [pltpu.VMEM((2, 128, 128), F32)], 10**6, pos, pay, const)
    mine, theirs = dx[0], swap(dx[1])
    even = jnp.where(pos[2] == 0, mine, theirs).reshape(GROUPS, 1, 2, 64, 64)
    odd = jnp.where(pos[2] == 0, theirs, mine).reshape(GROUPS, 1, 2, 64, 64)
    grad_features = jnp.concatenate([even, odd], axis=1).reshape(1, 64, 64, 64)
    return head_out.reshape(head_grad.shape), grad_features, grad_branch, grad_proj


def solution(mesh):
    fine = Mesh(mesh.devices.reshape(4, 4, 2, 4), ("z", "y", "core", "rep"))
    tile = ("z", "y", "core")
    return jax.shard_map(
        local,
        mesh=fine,
        in_specs=(P("rep", tile, None, None), P("rep", tile, None, None), P(None, tile, None), P()),
        out_specs=(P("rep", tile, None, None), P("rep", None, None, tile), P(None, tile, None), P()),
        check_vma=False,
    )
```

```python
import jax
import jax.numpy as jnp
from jax import lax
from jax.experimental import pallas as pl
from jax.experimental.pallas import tpu as pltpu
from jax.sharding import Mesh, PartitionSpec as P

GROUPS = 16
CH = 128
KCH = 512
BR = 256
HALF = 2048
PAD = 9
CUT = 15
SHIFTS = (0, -3, 3, -6, 6, -9, 9)
F32 = jnp.float32
BF = jnp.bfloat16
HIGH = lax.Precision.HIGHEST
ROWS_BY_COLS = (((1,), (1,)), ((), ()))
COLS_BY_COLS = (((0,), (0,)), ((), ()))


def shift_slot(j, b):
    return SHIFTS.index((b - 1) * 3 * (j + 1))


def column_shift(value, amount):
    if amount == 0:
        return value
    n = value.shape[0]
    col = lax.broadcasted_iota(jnp.int32, value.shape, 0) & 15
    rolled = pltpu.roll(value, (-amount) % n, 0)
    return jnp.where((col + amount >= 0) & (col + amount < 16), rolled, 0.0)


def wrap(value):
    return lax.rem(value + 8, 4)


def split_kernel(x_ref, hg_ref, first_ref, wide):
    for t in range(GROUPS):
        wide[t] = x_ref[:, CH * t : CH * (t + 1)].astype(F32)
    for t in range(2):
        wide[GROUPS + t] = hg_ref[:, CH * t : CH * (t + 1)].astype(F32)
    for v in range(4):
        for t in range(GROUPS + 2):
            part = wide[t, pl.ds(v, 32, stride=4), :].astype(BF)
            if t < GROUPS:
                place = CH * (t % 4)
                first_ref[4 * (t // 4) + v, :, place : place + CH] = part
            else:
                place = KCH + CH * (t - GROUPS)
                for z in range(4):
                    first_ref[4 * z + v, :, place : place + CH] = part


def weight_copies(pos_ref, blocks, w, sem):
    y, c = pos_ref[1], pos_ref[2]
    places = [(0, 0, 29), (-1, 0, 29), (1, 0, 29), (2, 0, CUT), (2, CUT, 29)]
    copies = []
    for side in range(2):
        for k, (step, low, high) in enumerate(places):
            core = c if side == 0 else 1 - c
            start = pl.multiple_of(wrap(y + step) * CH + core * 64, 64)
            n = len(copies)
            copies.append(
                pltpu.make_async_copy(blocks[n], w.at[pl.ds(low, high - low), pl.ds(start, 64), :], sem.at[n])
            )
    return copies


def forward_kernel(pos_ref, x_ref, hg_ref, *refs):
    blocks, outs, pieces, (w, xs, total, sem) = refs[:10], refs[10:15], refs[15:19], refs[19:]
    own_ref, plus_ref, minus_ref, plus_half, minus_half = outs
    copies = weight_copies(pos_ref, blocks, w, sem)
    for copy in copies:
        copy.start()
    for step in range(4):
        pieces[step][...] = x_ref[:, pl.ds(pl.multiple_of(wrap(pos_ref[1] + step) * CH, CH), CH)]
    wide = x_ref[:, 0:KCH].astype(F32)
    colsum = jnp.broadcast_to(jnp.sum(wide, axis=0, keepdims=True), (8, KCH))
    for slot, amount in enumerate(SHIFTS):
        if amount:
            xs[slot] = column_shift(wide, amount).astype(BF)
        else:
            xs[slot] = x_ref[:, 0:KCH]
    hsum = jnp.broadcast_to(jnp.sum(hg_ref[...].astype(F32), axis=0, keepdims=True), (8, BR))
    for copy in copies:
        copy.wait()
    pool = jnp.dot(colsum, w[28].astype(F32), precision=HIGH, preferred_element_type=F32)
    total[:, 0:BR] = jnp.dot(xs[0], w[0], preferred_element_type=F32)
    for j in range(3):
        cols = slice((j + 1) * BR, (j + 2) * BR)
        for a in (1, 0, 2):
            delta = 96 * (j + 1) * (a - 1)
            in_low, in_high = max(delta, 0), 512 + min(delta, 0)
            out_low, out_high = max(-delta, 0), 512 - max(delta, 0)
            left = jnp.concatenate([xs[shift_slot(j, b), in_low:in_high, :] for b in range(3)], axis=1)
            start = 1 + 9 * j + 3 * a
            part = jnp.dot(left, w[start : start + 3].reshape(3 * KCH, BR), preferred_element_type=F32)
            if a == 1:
                total[:, cols] = part
            else:
                total[out_low:out_high, cols] += part
    extra = jnp.concatenate([pool, hsum, jnp.zeros((8, 512), F32)], axis=1)
    z = pos_ref[0]

    def rows(step, low, size):
        return total[pl.ds(pl.multiple_of(wrap(z + step) * 128 + low, 64), size), :]

    own_ref[0:128, :] = rows(0, 0, 128)
    own_ref[128:136, :] = extra
    plus_ref[0:64, :] = rows(2, 0, 64)
    plus_ref[64:128, :] = rows(1, 64, 64)
    plus_ref[128:136, :] = extra
    minus_ref[0:64, :] = rows(2, 64, 64)
    minus_ref[64:72, :] = extra
    minus_ref[72:136, :] = rows(-1, 0, 64)
    plus_half[...] = rows(1, 0, 64)
    minus_half[0:64, :] = rows(-1, 64, 64)
    minus_half[64:72, :] = extra


def bridge_kernel(plus_half, from_low, minus_half, from_high, *refs):
    refs[3][...] = plus_half[...] + from_low[0:64, :]
    refs[4][...] = minus_half[...] + from_high[0:72, :]


def pair_kernel(first_ref, second_ref, out_ref):
    out_ref[0] = first_ref[...]
    out_ref[1] = second_ref[...]


def group_kernel(*refs):
    parts, (out_ref, sums_ref) = refs[:4], refs[4:]
    total = jnp.zeros((16, 512), F32)
    for k in range(4):
        for side in range(2):
            out_ref[k, side] = parts[k][side, 0:8]
            total = total + parts[k][side, 8].astype(F32)
    sums_ref[...] = jnp.broadcast_to(jnp.sum(total, axis=0, keepdims=True), (8, 512))


def turn_kernel(pos_ref, *refs):
    pieces, (xt_ref, colsum_ref, joined) = refs[:4], refs[4:]
    for k in range(4):
        joined[:, wrap(pos_ref[1] - k)] = pieces[k][...].reshape(32, 16, CH)
    total = jnp.zeros((1, CH), F32)
    for m in range(4):
        wide = joined[8 * m : 8 * (m + 1)].reshape(512, CH).astype(F32)
        total = total + jnp.sum(wide, axis=0, keepdims=True)
        for slot, amount in enumerate(SHIFTS):
            xt_ref[slot, :, pl.ds(m * 512, 512)] = column_shift(wide, amount).T.astype(BF)
    colsum_ref[...] = jnp.broadcast_to(total, (8, CH))


def middle_kernel(pos_ref, own, from_low, from_high, half_a, half_b, x_ref, pw_ref, _, keep_ref, give_ref, pay_ref):
    top = own[0:64, :] + from_high[72:136, :] + half_a[...]
    bottom = own[64:136, :] + from_low[64:136, :] + half_b[...]
    pre = jnp.concatenate([top, bottom[0:64, :]], axis=0)
    act = jnp.maximum(pre, 0.0).astype(BF)
    low = pw_ref[0:1024, :]
    hg = x_ref[pl.ds(pl.multiple_of(pos_ref[0] * 128, 128), 128), KCH:]
    back = lax.dot_general(hg, low, ROWS_BY_COLS, preferred_element_type=F32)
    grads = jnp.where(pre > 0, back, 0.0)
    first = pos_ref[2] == 0
    keep_ref[0:8] = jnp.where(first, grads[:, 0:512], grads[:, 512:1024]).astype(BF).reshape(8, 16, 512)
    give_ref[0:8] = jnp.where(first, grads[:, 512:1024], grads[:, 0:512]).astype(BF).reshape(8, 16, 512)
    sums = jnp.concatenate([bottom[64:72, 0:512]] * 2, axis=0)
    one = sums.astype(BF).astype(F32)
    two = (sums - one).astype(BF).astype(F32)
    row = lax.broadcasted_iota(jnp.int32, sums.shape, 0)
    terms = jnp.where(row == 0, one, jnp.where(row == 1, two, jnp.where(row == 2, sums - one - two, 0.0))).astype(BF)
    keep_ref[8] = terms
    give_ref[8] = terms
    head = jnp.dot(act, low, preferred_element_type=F32).astype(BF)
    proj = lax.dot_general(act, hg, COLS_BY_COLS, preferred_element_type=F32).astype(BF)
    for t in range(GROUPS):
        pay_ref[t, 0:64, :] = proj[64 * t : 64 * (t + 1), :]
        pay_ref[t, 64:96, :] = head[32 * (t % 4) : 32 * (t % 4 + 1), :]


def pool_kernel(pos_ref, sums_ref, pw_ref, const_ref, grad_ref, outer_ref, whole):
    pool = sums_ref[:, 0:BR] * (1.0 / 4096.0)
    hsum = sums_ref[:, BR : 2 * BR]
    act = jnp.maximum(pool, 0.0).astype(BF)
    high = pw_ref[1024:1280, :]
    const_ref[...] = jnp.dot(act, high, preferred_element_type=F32)
    grad = lax.dot_general(hsum, high.astype(F32), ROWS_BY_COLS, precision=HIGH, preferred_element_type=F32)
    grad_ref[...] = jnp.where(pool > 0, grad, 0.0)
    whole[...] = 0.125 * lax.dot_general(
        act.astype(F32), hsum, COLS_BY_COLS, precision=HIGH, preferred_element_type=F32
    )
    chunk = pos_ref[0] * 4 + pos_ref[1]
    outer_ref[...] = whole[pl.ds(pl.multiple_of(chunk * 16, 16), 16), :]


def collect_kernel(pay_ref, _, part_ref):
    total = pay_ref[0, 0:64, :].astype(F32)
    for t in range(1, GROUPS):
        total = total + pay_ref[t, 0:64, :].astype(F32)
    part_ref[...] = total


def head_kernel(pos_ref, pay_ref, const_ref, head_ref, wide):
    for v in range(4):
        piece = pay_ref[4 * pos_ref[0] + v, 64:96, :].astype(F32) + const_ref[0:1, :]
        wide[0, pl.ds(v, 32, stride=4), :] = piece[:, 0:128]
        wide[1, pl.ds(v, 32, stride=4), :] = piece[:, 128:256]
    head_ref[:, 0:128] = wide[0].astype(BF)
    head_ref[:, 128:256] = wide[1].astype(BF)


def gather_copies(pos_ref, blocks, g, sem, pad):
    z, y, c = pos_ref[0], pos_ref[1], pos_ref[2]
    copies = []
    for side in range(2):
        half = c if side == 0 else 1 - c
        for place, far in enumerate((0, -1, 1, 2)):
            for k, step in enumerate((0, -1, 1, 2)):
                src = blocks[4 * side + place].at[k, side]
                v = wrap(y + jnp.where(half == 0, step, far))
                group = wrap(z + jnp.where(half == 0, far, step))
                cols = pl.ds(pl.multiple_of(512 * half, 512), 512)
                dst = g.at[pl.ds(2 * pad + 8 * group, 8), v, :, cols]
                copies.append(pltpu.make_async_copy(src, dst, sem.at[len(copies)]))
    return copies


def weight_grad_kernel(pos_ref, xt_ref, colsum_ref, grad_ref, *refs):
    blocks, (own_ref, other_ref), (g, dw, sem) = refs[:8], refs[-5:-3], refs[-3:]
    copies = gather_copies(pos_ref, blocks, g, sem, 0)
    for copy in copies:
        copy.start()
    for copy in copies:
        copy.wait()

    def grads(low, high, cols):
        return g[low // 64 : high // 64, :, :, cols].reshape(high - low, BR)

    dw[0] = jnp.dot(xt_ref[0], grads(0, HALF, slice(0, BR)), preferred_element_type=F32)
    for j in range(3):
        cols = slice((j + 1) * BR, (j + 2) * BR)
        for a in range(3):
            delta = 3 * (j + 1) * (a - 1) * 128
            x_low, x_high = max(delta, 0), HALF + min(delta, 0)
            g_low, g_high = max(-delta, 0), HALF - max(delta, 0)
            left = jnp.concatenate([xt_ref[shift_slot(j, b), :, x_low:x_high] for b in range(3)], axis=0)
            part = jnp.dot(left, grads(g_low, g_high, cols), preferred_element_type=F32)
            start = 1 + 9 * j + 3 * a
            dw[start : start + 3] = part.reshape(3, CH, BR)
    dw[28] = lax.dot_general(
        colsum_ref[...], grad_ref[...], COLS_BY_COLS, precision=HIGH, preferred_element_type=F32
    ) * (0.125 / 4096.0)
    c = pos_ref[2]
    own_ref[...] = dw[:, pl.ds(pl.multiple_of(c * 64, 64), 64), :].astype(BF)
    other_ref[...] = dw[:, pl.ds(pl.multiple_of((1 - c) * 64, 64), 64), :].astype(BF)


def field_grad_kernel(pos_ref, grad_ref, own, other, *refs):
    blocks, dx_ref, (g, w, whole, sem) = refs[:8], refs[-5], refs[-4:]
    copies = gather_copies(pos_ref, blocks, g, sem, PAD)
    for copy in copies:
        copy.start()
    c = pos_ref[2]
    w[:, pl.ds(pl.multiple_of(c * 64, 64), 64), :] = own[...]
    w[:, pl.ds(pl.multiple_of((1 - c) * 64, 64), 64), :] = other[...]
    g[0 : 2 * PAD] = jnp.zeros((2 * PAD, 4, 16, 1024), BF)
    g[2 * (PAD + GROUPS) :] = jnp.zeros((2 * PAD, 4, 16, 1024), BF)
    field = lax.dot_general(
        grad_ref[...], w[28].astype(F32), ROWS_BY_COLS, precision=HIGH, preferred_element_type=F32
    )[0:1, :] * (1.0 / 4096.0)
    for copy in copies:
        copy.wait()

    def grads(low, cols):
        return g[2 * (PAD + low) : 2 * (PAD + low + 4), :, :, cols].reshape(512, BR)

    for m in range(4):
        acc = field + lax.dot_general(
            grads(4 * m, slice(0, BR)), w[0], ROWS_BY_COLS, preferred_element_type=F32
        )
        for j in range(3):
            steps = []
            for a in range(3):
                low = 4 * m - 3 * (j + 1) * (a - 1)
                if low + 3 >= 0 and low < GROUPS:
                    steps.append((a, low))
            left = jnp.concatenate([grads(low, slice((j + 1) * BR, (j + 2) * BR)) for _, low in steps], axis=1)
            right = jnp.concatenate(
                [w[1 + 9 * j + 3 * a : 4 + 9 * j + 3 * a].reshape(3 * CH, BR) for a, _ in steps], axis=1
            )
            spread = lax.dot_general(left, right, ROWS_BY_COLS, preferred_element_type=F32)
            for b in range(3):
                acc = acc + column_shift(spread[:, b * CH : (b + 1) * CH], -(b - 1) * 3 * (j + 1))
        for row in range(8):
            for v in range(4):
                place = (4 * row + v) * 16
                whole[pl.ds(512 * m + 64 * row + v, 16, stride=4), :] = acc[place : place + 16, :]
    low, high = whole[:, 0:64], whole[:, 64:128]
    dx_ref[0] = jnp.where(c == 0, low, high).astype(BF)
    dx_ref[1] = jnp.where(c == 0, high, low).astype(BF)


def add_kernel(pos_ref, own, other, *outs):
    r = pos_ref[3]
    for k in range(4):
        rows = pl.ds(pl.multiple_of(wrap(r + k) * 464, 16), 464)
        outs[k][...] = (own[rows, :].astype(F32) + other[rows, :].astype(F32)).astype(BF)


def join_kernel(pos_ref, *refs):
    for k, step in enumerate((0, -1, 1, 2)):
        rows = pl.ds(pl.multiple_of(wrap(pos_ref[3] + step) * 464, 8), 464)
        refs[4][rows, :] = refs[k][...].astype(F32)


ROOM = {"forward_kernel": 28, "weight_grad_kernel": 18, "field_grad_kernel": 22, "turn_kernel": 16, "middle_kernel": 16}


def call(kernel, out_shape, scratch, flops, *args, scalar=True, raw=0):
    specs = [pl.BlockSpec(memory_space=pltpu.VMEM) for _ in args]
    if scalar:
        specs[0] = pl.BlockSpec(memory_space=pltpu.SMEM)
    for k in range(raw):
        specs[len(args) - 1 - k] = pl.BlockSpec(memory_space=pl.ANY)
    moved = sum(a.size * a.dtype.itemsize for a in jax.tree.leaves((args, out_shape)))
    return pl.pallas_call(
        kernel,
        out_shape=out_shape,
        in_specs=specs,
        out_specs=jax.tree.map(lambda _: pl.BlockSpec(memory_space=pltpu.VMEM), out_shape),
        scratch_shapes=scratch,
        compiler_params=pltpu.CompilerParams(vmem_limit_bytes=ROOM.get(kernel.__name__, 12) * 2**20),
        cost_estimate=pl.CostEstimate(flops=flops, bytes_accessed=moved, transcendentals=0),
        name=kernel.__name__,
    )(*args)


def gate(values, after):
    anywhere = pl.BlockSpec(memory_space=pl.ANY)
    return pl.pallas_call(
        lambda *refs: None,
        out_shape=tuple(jax.ShapeDtypeStruct(v.shape, v.dtype) for v in values),
        in_specs=[anywhere] * (len(values) + len(after)),
        out_specs=(anywhere,) * len(values),
        input_output_aliases={k: k for k in range(len(values))},
        cost_estimate=pl.CostEstimate(flops=0, bytes_accessed=0, transcendentals=0),
    )(*values, *after)


def swap(value):
    return lax.ppermute(value, "core", [(0, 1), (1, 0)])


def send(value, axis, step):
    return lax.ppermute(value, axis, [(k, (k + step) % 4) for k in range(4)])


def pair(value, axis, bit):
    return lax.ppermute(value, axis, [(k, k ^ bit) for k in range(4)])


def cross(value, step, turn):
    pairs = []
    for z in range(4):
        for y in range(4):
            for c in range(2):
                along_y = (c == 0) != turn
                to = (z, (y + step) % 4) if along_y else ((z + step) % 4, y)
                pairs.append(((4 * z + y) * 2 + c, (4 * to[0] + to[1]) * 2 + c))
    return lax.ppermute(value, ("z", "y", "core"), pairs)


def local(features, head_grad, branch_weight, proj_weight):
    shape = jax.ShapeDtypeStruct
    plane = ("z", "y")
    pos = jnp.stack([lax.axis_index(n).astype(jnp.int32) for n in ("z", "y", "core", "rep")])

    def exchange(value):
        return lax.all_to_all(value, plane, split_axis=0, concat_axis=0, tiled=True)

    first = call(
        split_kernel, shape((GROUPS, 32, KCH + BR), BF),
        [pltpu.VMEM((GROUPS + 2, 128, CH), F32)], 10**6,
        features.reshape(128, 2048), head_grad.reshape(128, BR), scalar=False,
    )
    below, above = send(branch_weight, "y", 1), send(branch_weight, "y", -1)
    x = exchange(first).reshape(512, KCH + BR)
    below, above = gate((below, above), (x,))
    blocks = [branch_weight, below, above, send(below[0:CUT], "y", 1), send(above[CUT:29], "y", -1)]
    blocks = blocks + [swap(b) for b in blocks]
    own, plus, minus, plus_half, minus_half, *pieces = call(
        forward_kernel,
        tuple(shape((n, 1024), F32) for n in (136, 136, 136, 64, 72)) + (shape((512, CH), BF),) * 4,
        [
            pltpu.VMEM((29, KCH, BR), BF), pltpu.VMEM((7, 512, KCH), BF), pltpu.VMEM((512, 1024), F32),
            pltpu.SemaphoreType.DMA((10,)),
        ],
        4 * 10**9, pos, x, head_grad.reshape(128, BR), *blocks, raw=10,
    )
    from_low, from_high = send(plus, "z", 1), send(minus, "z", -1)
    pieces = [pieces[0]] + [send(pieces[k], "y", k) for k in (1, 2, 3)]
    half_a, half_b = call(
        bridge_kernel, (shape((64, 1024), F32), shape((72, 1024), F32)), [], 10**5,
        plus_half, from_low, minus_half, from_high, *pieces[1:], scalar=False,
    )
    half_a, half_b = send(half_a, "z", 1), send(half_b, "z", -1)
    turned, colsum = call(
        turn_kernel, (shape((7, CH, HALF), BF), shape((8, CH), F32)), [pltpu.VMEM((32, 4, 16, CH), BF)], 10**8,
        pos, *pieces,
    )
    keep, give, pay = call(
        middle_kernel,
        (shape((9, 16, 512), BF), shape((9, 16, 512), BF), shape((GROUPS, 96, BR), BF)),
        [], 2 * 10**8, pos, own, from_low, from_high, half_a, half_b, x, proj_weight, colsum,
    )
    block = call(pair_kernel, shape((2, 9, 16, 512), BF), [], 10**5, keep, swap(give), scalar=False)
    near = [block, cross(block, 1, False), cross(block, -1, False), cross(block, 2, False)]
    group, sums = call(
        group_kernel, (shape((4, 2, 8, 16, 512), BF), shape((8, 512), F32)), [], 10**10, *near, scalar=False
    )
    every = [group] + [cross(group, step, True) for step in (1, -1, 2)]
    sums = jnp.where(pos[2] == 0, sums, swap(sums))
    const, pool_grad, outer = call(
        pool_kernel, (shape((8, BR), F32), shape((8, BR), F32), shape((16, BR), F32)), [pltpu.VMEM((256, BR), F32)],
        10**7, pos, sums, proj_weight,
    )
    pay = exchange(pay)
    part = call(collect_kernel, shape((64, BR), F32), [], 10**6, pay, outer, scalar=False)
    part = jnp.concatenate([part + swap(part), outer], axis=0)
    part = part + pair(part, "rep", 1)
    part = part + pair(part, "rep", 2)
    part = jnp.broadcast_to(part.astype(BF)[None], (GROUPS, 80, BR))
    below, = gate((every[1],), (part,))
    every = [every[0], below] + every[2:4]
    every = every + [swap(piece) for piece in every]
    dw, dw_other = call(
        weight_grad_kernel,
        (shape((29, 64, BR), BF), shape((29, 64, BR), BF)),
        [pltpu.VMEM((2 * GROUPS, 4, 16, 1024), BF), pltpu.VMEM((29, CH, BR), F32), pltpu.SemaphoreType.DMA((32,))],
        4 * 10**9, pos, turned, colsum, pool_grad, *every, raw=8,
    )
    quarters = call(
        add_kernel, (shape((464, BR), BF),) * 4, [], 10**6, pos, dw.reshape(1856, BR), swap(dw_other).reshape(1856, BR)
    )
    dx = call(
        field_grad_kernel,
        shape((2, HALF, 64), BF),
        [
            pltpu.VMEM((2 * (GROUPS + 2 * PAD), 4, 16, 1024), BF), pltpu.VMEM((29, CH, BR), BF),
            pltpu.VMEM((HALF, CH), F32), pltpu.SemaphoreType.DMA((32,)),
        ],
        4 * 10**9, pos, pool_grad, branch_weight, blocks[5], *every, quarters[0], raw=9,
    )
    terms = [quarters[0]] + [send(quarters[k], "rep", k) for k in (1, 3, 2)]
    dw = sum(term.astype(F32) for term in terms).astype(BF)
    dw = [dw] + [send(dw, "rep", step) for step in (1, -1, 2)]
    grad_branch = call(join_kernel, shape((1856, BR), F32), [], 10**6, pos, *dw).reshape(29, 64, BR)
    (part,) = gate((exchange(part),), (dw[0],))
    part = part.astype(F32)
    grad_proj = jnp.concatenate([part[:, 0:64].reshape(1024, BR), part[:, 64:80].reshape(256, BR)], axis=0)
    (const,) = gate((const,), (dw[0],))
    head_out = call(head_kernel, shape((128, BR), BF), [pltpu.VMEM((2, 128, 128), F32)], 10**6, pos, pay, const)
    mine, theirs = dx[0], swap(dx[1])
    even = jnp.where(pos[2] == 0, mine, theirs).reshape(GROUPS, 1, 2, 64, 64)
    odd = jnp.where(pos[2] == 0, theirs, mine).reshape(GROUPS, 1, 2, 64, 64)
    grad_features = jnp.concatenate([even, odd], axis=1).reshape(1, 64, 64, 64)
    return head_out.reshape(head_grad.shape), grad_features, grad_branch, grad_proj


def solution(mesh):
    fine = Mesh(mesh.devices.reshape(4, 4, 2, 4), ("z", "y", "core", "rep"))
    tile = ("z", "y", "core")
    return jax.shard_map(
        local,
        mesh=fine,
        in_specs=(P("rep", tile, None, None), P("rep", tile, None, None), P(None, tile, None), P()),
        out_specs=(P("rep", tile, None, None), P("rep", None, None, tile), P(None, tile, None), P()),
        check_vma=False,
    )
```

```python
import jax
import jax.numpy as jnp
from jax import lax
from jax.experimental import pallas as pl
from jax.experimental.pallas import tpu as pltpu
from jax.sharding import Mesh, PartitionSpec as P

GROUPS = 16
CH = 128
KCH = 512
BR = 256
HALF = 2048
PAD = 9
CUT = 15
SHIFTS = (0, -3, 3, -6, 6, -9, 9)
F32 = jnp.float32
BF = jnp.bfloat16
HIGH = lax.Precision.HIGHEST
ROWS_BY_COLS = (((1,), (1,)), ((), ()))
COLS_BY_COLS = (((0,), (0,)), ((), ()))


def shift_slot(j, b):
    return SHIFTS.index((b - 1) * 3 * (j + 1))


def column_shift(value, amount):
    if amount == 0:
        return value
    n = value.shape[0]
    col = lax.broadcasted_iota(jnp.int32, value.shape, 0) & 15
    rolled = pltpu.roll(value, (-amount) % n, 0)
    return jnp.where((col + amount >= 0) & (col + amount < 16), rolled, 0.0)


def wrap(value):
    return lax.rem(value + 8, 4)


def split_kernel(x_ref, hg_ref, first_ref, wide):
    for t in range(GROUPS):
        wide[t] = x_ref[:, CH * t : CH * (t + 1)].astype(F32)
    for t in range(2):
        wide[GROUPS + t] = hg_ref[:, CH * t : CH * (t + 1)].astype(F32)
    for v in range(4):
        for t in range(GROUPS + 2):
            part = wide[t, pl.ds(v, 32, stride=4), :].astype(BF)
            if t < GROUPS:
                place = CH * (t % 4)
                first_ref[4 * (t // 4) + v, :, place : place + CH] = part
            else:
                place = KCH + CH * (t - GROUPS)
                for z in range(4):
                    first_ref[4 * z + v, :, place : place + CH] = part


def weight_copies(pos_ref, blocks, w, sem):
    y, c = pos_ref[1], pos_ref[2]
    places = [(0, 0, 29), (-1, 0, 29), (1, 0, 29), (2, 0, CUT), (2, CUT, 29)]
    copies = []
    for side in range(2):
        for k, (step, low, high) in enumerate(places):
            core = c if side == 0 else 1 - c
            start = pl.multiple_of(wrap(y + step) * CH + core * 64, 64)
            n = len(copies)
            copies.append(
                pltpu.make_async_copy(blocks[n], w.at[pl.ds(low, high - low), pl.ds(start, 64), :], sem.at[n])
            )
    return copies


def forward_kernel(pos_ref, x_ref, hg_ref, *refs):
    blocks, outs, pieces, (w, xs, total, sem) = refs[:10], refs[10:15], refs[15:19], refs[19:]
    own_ref, plus_ref, minus_ref, plus_half, minus_half = outs
    copies = weight_copies(pos_ref, blocks, w, sem)
    for copy in copies:
        copy.start()
    for step in range(4):
        pieces[step][...] = x_ref[:, pl.ds(pl.multiple_of(wrap(pos_ref[1] + step) * CH, CH), CH)]
    wide = x_ref[:, 0:KCH].astype(F32)
    colsum = jnp.broadcast_to(jnp.sum(wide, axis=0, keepdims=True), (8, KCH))
    for slot, amount in enumerate(SHIFTS):
        if amount:
            xs[slot] = column_shift(wide, amount).astype(BF)
        else:
            xs[slot] = x_ref[:, 0:KCH]
    hsum = jnp.broadcast_to(jnp.sum(hg_ref[...].astype(F32), axis=0, keepdims=True), (8, BR))
    for copy in copies:
        copy.wait()
    pool = jnp.dot(colsum, w[28].astype(F32), precision=HIGH, preferred_element_type=F32)
    total[:, 0:BR] = jnp.dot(xs[0], w[0], preferred_element_type=F32)
    for j in range(3):
        cols = slice((j + 1) * BR, (j + 2) * BR)
        for a in (1, 0, 2):
            delta = 96 * (j + 1) * (a - 1)
            in_low, in_high = max(delta, 0), 512 + min(delta, 0)
            out_low, out_high = max(-delta, 0), 512 - max(delta, 0)
            left = jnp.concatenate([xs[shift_slot(j, b), in_low:in_high, :] for b in range(3)], axis=1)
            start = 1 + 9 * j + 3 * a
            part = jnp.dot(left, w[start : start + 3].reshape(3 * KCH, BR), preferred_element_type=F32)
            if a == 1:
                total[:, cols] = part
            else:
                total[out_low:out_high, cols] += part
    extra = jnp.concatenate([pool, hsum, jnp.zeros((8, 512), F32)], axis=1)
    z = pos_ref[0]

    def rows(step, low, size):
        return total[pl.ds(pl.multiple_of(wrap(z + step) * 128 + low, 64), size), :]

    own_ref[0:128, :] = rows(0, 0, 128)
    own_ref[128:136, :] = extra
    plus_ref[0:64, :] = rows(2, 0, 64)
    plus_ref[64:128, :] = rows(1, 64, 64)
    plus_ref[128:136, :] = extra
    minus_ref[0:64, :] = rows(2, 64, 64)
    minus_ref[64:72, :] = extra
    minus_ref[72:136, :] = rows(-1, 0, 64)
    plus_half[...] = rows(1, 0, 64)
    minus_half[0:64, :] = rows(-1, 64, 64)
    minus_half[64:72, :] = extra


def bridge_kernel(plus_half, from_low, minus_half, from_high, *refs):
    refs[3][...] = plus_half[...] + from_low[0:64, :]
    refs[4][...] = minus_half[...] + from_high[0:72, :]


def pair_kernel(first_ref, second_ref, out_ref):
    out_ref[0] = first_ref[...]
    out_ref[1] = second_ref[...]


def group_kernel(*refs):
    parts, (out_ref, sums_ref) = refs[:4], refs[4:]
    total = jnp.zeros((16, 512), F32)
    for k in range(4):
        for side in range(2):
            out_ref[k, side] = parts[k][side, 0:8]
            total = total + parts[k][side, 8].astype(F32)
    sums_ref[...] = jnp.broadcast_to(jnp.sum(total, axis=0, keepdims=True), (8, 512))


def turn_kernel(pos_ref, *refs):
    pieces, (xt_ref, colsum_ref, joined) = refs[:4], refs[4:]
    for k in range(4):
        joined[:, wrap(pos_ref[1] - k)] = pieces[k][...].reshape(32, 16, CH)
    total = jnp.zeros((1, CH), F32)
    for m in range(4):
        wide = joined[8 * m : 8 * (m + 1)].reshape(512, CH).astype(F32)
        total = total + jnp.sum(wide, axis=0, keepdims=True)
        for slot, amount in enumerate(SHIFTS):
            xt_ref[slot, :, pl.ds(m * 512, 512)] = column_shift(wide, amount).T.astype(BF)
    colsum_ref[...] = jnp.broadcast_to(total, (8, CH))


def middle_kernel(pos_ref, own, from_low, from_high, half_a, half_b, x_ref, pw_ref, _, keep_ref, give_ref, pay_ref):
    top = own[0:64, :] + from_high[72:136, :] + half_a[...]
    bottom = own[64:136, :] + from_low[64:136, :] + half_b[...]
    pre = jnp.concatenate([top, bottom[0:64, :]], axis=0)
    act = jnp.maximum(pre, 0.0).astype(BF)
    low = pw_ref[0:1024, :]
    hg = x_ref[pl.ds(pl.multiple_of(pos_ref[0] * 128, 128), 128), KCH:]
    back = lax.dot_general(hg, low, ROWS_BY_COLS, preferred_element_type=F32)
    grads = jnp.where(pre > 0, back, 0.0)
    first = pos_ref[2] == 0
    keep_ref[0:8] = jnp.where(first, grads[:, 0:512], grads[:, 512:1024]).astype(BF).reshape(8, 16, 512)
    give_ref[0:8] = jnp.where(first, grads[:, 512:1024], grads[:, 0:512]).astype(BF).reshape(8, 16, 512)
    sums = jnp.concatenate([bottom[64:72, 0:512]] * 2, axis=0)
    one = sums.astype(BF).astype(F32)
    two = (sums - one).astype(BF).astype(F32)
    row = lax.broadcasted_iota(jnp.int32, sums.shape, 0)
    terms = jnp.where(row == 0, one, jnp.where(row == 1, two, jnp.where(row == 2, sums - one - two, 0.0))).astype(BF)
    keep_ref[8] = terms
    give_ref[8] = terms
    head = jnp.dot(act, low, preferred_element_type=F32).astype(BF)
    proj = lax.dot_general(act, hg, COLS_BY_COLS, preferred_element_type=F32).astype(BF)
    for t in range(GROUPS):
        pay_ref[t, 0:64, :] = proj[64 * t : 64 * (t + 1), :]
        pay_ref[t, 64:96, :] = head[32 * (t % 4) : 32 * (t % 4 + 1), :]


def pool_kernel(pos_ref, sums_ref, pw_ref, const_ref, grad_ref, outer_ref, whole):
    pool = sums_ref[:, 0:BR] * (1.0 / 4096.0)
    hsum = sums_ref[:, BR : 2 * BR]
    act = jnp.maximum(pool, 0.0).astype(BF)
    high = pw_ref[1024:1280, :]
    const_ref[...] = jnp.dot(act, high, preferred_element_type=F32)
    grad = lax.dot_general(hsum, high.astype(F32), ROWS_BY_COLS, precision=HIGH, preferred_element_type=F32)
    grad_ref[...] = jnp.where(pool > 0, grad, 0.0)
    whole[...] = 0.125 * lax.dot_general(
        act.astype(F32), hsum, COLS_BY_COLS, precision=HIGH, preferred_element_type=F32
    )
    chunk = pos_ref[0] * 4 + pos_ref[1]
    outer_ref[...] = whole[pl.ds(pl.multiple_of(chunk * 16, 16), 16), :]


def collect_kernel(pay_ref, _, part_ref):
    total = pay_ref[0, 0:64, :].astype(F32)
    for t in range(1, GROUPS):
        total = total + pay_ref[t, 0:64, :].astype(F32)
    part_ref[...] = total


def head_kernel(pos_ref, pay_ref, const_ref, head_ref, wide):
    for v in range(4):
        piece = pay_ref[4 * pos_ref[0] + v, 64:96, :].astype(F32) + const_ref[0:1, :]
        wide[0, pl.ds(v, 32, stride=4), :] = piece[:, 0:128]
        wide[1, pl.ds(v, 32, stride=4), :] = piece[:, 128:256]
    head_ref[:, 0:128] = wide[0].astype(BF)
    head_ref[:, 128:256] = wide[1].astype(BF)


def gather_copies(pos_ref, blocks, g, sem, pad):
    z, y, c = pos_ref[0], pos_ref[1], pos_ref[2]
    copies = []
    for side in range(2):
        half = c if side == 0 else 1 - c
        for place, far in enumerate((0, -1, 1, 2)):
            for k, step in enumerate((0, -1, 1, 2)):
                src = blocks[4 * side + place].at[k, side]
                v = wrap(y + jnp.where(half == 0, step, far))
                group = wrap(z + jnp.where(half == 0, far, step))
                cols = pl.ds(pl.multiple_of(512 * half, 512), 512)
                dst = g.at[pl.ds(2 * pad + 8 * group, 8), v, :, cols]
                copies.append(pltpu.make_async_copy(src, dst, sem.at[len(copies)]))
    return copies


def weight_grad_kernel(pos_ref, xt_ref, colsum_ref, grad_ref, *refs):
    blocks, (own_ref, other_ref), (g, dw, sem) = refs[:8], refs[-5:-3], refs[-3:]
    copies = gather_copies(pos_ref, blocks, g, sem, 0)
    for copy in copies:
        copy.start()
    for copy in copies:
        copy.wait()

    def grads(low, high, cols):
        return g[low // 64 : high // 64, :, :, cols].reshape(high - low, BR)

    dw[0] = jnp.dot(xt_ref[0], grads(0, HALF, slice(0, BR)), preferred_element_type=F32)
    for j in range(3):
        cols = slice((j + 1) * BR, (j + 2) * BR)
        for a in range(3):
            delta = 3 * (j + 1) * (a - 1) * 128
            x_low, x_high = max(delta, 0), HALF + min(delta, 0)
            g_low, g_high = max(-delta, 0), HALF - max(delta, 0)
            left = jnp.concatenate([xt_ref[shift_slot(j, b), :, x_low:x_high] for b in range(3)], axis=0)
            part = jnp.dot(left, grads(g_low, g_high, cols), preferred_element_type=F32)
            start = 1 + 9 * j + 3 * a
            dw[start : start + 3] = part.reshape(3, CH, BR)
    dw[28] = lax.dot_general(
        colsum_ref[...], grad_ref[...], COLS_BY_COLS, precision=HIGH, preferred_element_type=F32
    ) * (0.125 / 4096.0)
    c = pos_ref[2]
    own_ref[...] = dw[:, pl.ds(pl.multiple_of(c * 64, 64), 64), :].astype(BF)
    other_ref[...] = dw[:, pl.ds(pl.multiple_of((1 - c) * 64, 64), 64), :].astype(BF)


def field_grad_kernel(pos_ref, grad_ref, own, other, *refs):
    blocks, dx_ref, (g, w, whole, sem) = refs[:8], refs[-5], refs[-4:]
    copies = gather_copies(pos_ref, blocks, g, sem, PAD)
    for copy in copies:
        copy.start()
    c = pos_ref[2]
    w[:, pl.ds(pl.multiple_of(c * 64, 64), 64), :] = own[...]
    w[:, pl.ds(pl.multiple_of((1 - c) * 64, 64), 64), :] = other[...]
    g[0 : 2 * PAD] = jnp.zeros((2 * PAD, 4, 16, 1024), BF)
    g[2 * (PAD + GROUPS) :] = jnp.zeros((2 * PAD, 4, 16, 1024), BF)
    field = lax.dot_general(
        grad_ref[...], w[28].astype(F32), ROWS_BY_COLS, precision=HIGH, preferred_element_type=F32
    )[0:1, :] * (1.0 / 4096.0)
    for copy in copies:
        copy.wait()

    def grads(low, cols):
        return g[2 * (PAD + low) : 2 * (PAD + low + 4), :, :, cols].reshape(512, BR)

    for m in range(4):
        acc = field + lax.dot_general(
            grads(4 * m, slice(0, BR)), w[0], ROWS_BY_COLS, preferred_element_type=F32
        )
        for j in range(3):
            steps = []
            for a in range(3):
                low = 4 * m - 3 * (j + 1) * (a - 1)
                if low + 3 >= 0 and low < GROUPS:
                    steps.append((a, low))
            left = jnp.concatenate([grads(low, slice((j + 1) * BR, (j + 2) * BR)) for _, low in steps], axis=1)
            right = jnp.concatenate(
                [w[1 + 9 * j + 3 * a : 4 + 9 * j + 3 * a].reshape(3 * CH, BR) for a, _ in steps], axis=1
            )
            spread = lax.dot_general(left, right, ROWS_BY_COLS, preferred_element_type=F32)
            for b in range(3):
                acc = acc + column_shift(spread[:, b * CH : (b + 1) * CH], -(b - 1) * 3 * (j + 1))
        for row in range(8):
            for v in range(4):
                place = (4 * row + v) * 16
                whole[pl.ds(512 * m + 64 * row + v, 16, stride=4), :] = acc[place : place + 16, :]
    low, high = whole[:, 0:64], whole[:, 64:128]
    dx_ref[0] = jnp.where(c == 0, low, high).astype(BF)
    dx_ref[1] = jnp.where(c == 0, high, low).astype(BF)


def add_kernel(pos_ref, own, other, *outs):
    r = pos_ref[3]
    for k in range(4):
        rows = pl.ds(pl.multiple_of(wrap(r + k) * 464, 16), 464)
        outs[k][...] = (own[rows, :].astype(F32) + other[rows, :].astype(F32)).astype(BF)


def join_kernel(pos_ref, *refs):
    for k, step in enumerate((0, -1, 1, 2)):
        rows = pl.ds(pl.multiple_of(wrap(pos_ref[3] + step) * 464, 8), 464)
        refs[4][rows, :] = refs[k][...].astype(F32)


ROOM = {"forward_kernel": 28, "weight_grad_kernel": 18, "field_grad_kernel": 22, "turn_kernel": 16, "middle_kernel": 16}


def call(kernel, out_shape, scratch, flops, *args, scalar=True, raw=0):
    specs = [pl.BlockSpec(memory_space=pltpu.VMEM) for _ in args]
    if scalar:
        specs[0] = pl.BlockSpec(memory_space=pltpu.SMEM)
    for k in range(raw):
        specs[len(args) - 1 - k] = pl.BlockSpec(memory_space=pl.ANY)
    moved = sum(a.size * a.dtype.itemsize for a in jax.tree.leaves((args, out_shape)))
    return pl.pallas_call(
        kernel,
        out_shape=out_shape,
        in_specs=specs,
        out_specs=jax.tree.map(lambda _: pl.BlockSpec(memory_space=pltpu.VMEM), out_shape),
        scratch_shapes=scratch,
        compiler_params=pltpu.CompilerParams(vmem_limit_bytes=ROOM.get(kernel.__name__, 12) * 2**20),
        cost_estimate=pl.CostEstimate(flops=flops, bytes_accessed=moved, transcendentals=0),
        name=kernel.__name__,
    )(*args)


def gate(values, after):
    anywhere = pl.BlockSpec(memory_space=pl.ANY)
    return pl.pallas_call(
        lambda *refs: None,
        out_shape=tuple(jax.ShapeDtypeStruct(v.shape, v.dtype) for v in values),
        in_specs=[anywhere] * (len(values) + len(after)),
        out_specs=(anywhere,) * len(values),
        input_output_aliases={k: k for k in range(len(values))},
        cost_estimate=pl.CostEstimate(flops=0, bytes_accessed=0, transcendentals=0),
    )(*values, *after)


def swap(value):
    return lax.ppermute(value, "core", [(0, 1), (1, 0)])


def send(value, axis, step):
    return lax.ppermute(value, axis, [(k, (k + step) % 4) for k in range(4)])


def pair(value, axis, bit):
    return lax.ppermute(value, axis, [(k, k ^ bit) for k in range(4)])


def cross(value, step, turn):
    pairs = []
    for z in range(4):
        for y in range(4):
            for c in range(2):
                along_y = (c == 0) != turn
                to = (z, (y + step) % 4) if along_y else ((z + step) % 4, y)
                pairs.append(((4 * z + y) * 2 + c, (4 * to[0] + to[1]) * 2 + c))
    return lax.ppermute(value, ("z", "y", "core"), pairs)


def local(features, head_grad, branch_weight, proj_weight):
    shape = jax.ShapeDtypeStruct
    plane = ("z", "y")
    pos = jnp.stack([lax.axis_index(n).astype(jnp.int32) for n in ("z", "y", "core", "rep")])

    def exchange(value):
        return lax.all_to_all(value, plane, split_axis=0, concat_axis=0, tiled=True)

    first = call(
        split_kernel, shape((GROUPS, 32, KCH + BR), BF),
        [pltpu.VMEM((GROUPS + 2, 128, CH), F32)], 10**6,
        features.reshape(128, 2048), head_grad.reshape(128, BR), scalar=False,
    )
    below, above = send(branch_weight, "y", 1), send(branch_weight, "y", -1)
    x = exchange(first).reshape(512, KCH + BR)
    below, above = gate((below, above), (x,))
    blocks = [branch_weight, below, above, send(below[0:CUT], "y", 1), send(above[CUT:29], "y", -1)]
    blocks = blocks + [swap(b) for b in blocks]
    own, plus, minus, plus_half, minus_half, *pieces = call(
        forward_kernel,
        tuple(shape((n, 1024), F32) for n in (136, 136, 136, 64, 72)) + (shape((512, CH), BF),) * 4,
        [
            pltpu.VMEM((29, KCH, BR), BF), pltpu.VMEM((7, 512, KCH), BF), pltpu.VMEM((512, 1024), F32),
            pltpu.SemaphoreType.DMA((10,)),
        ],
        4 * 10**9, pos, x, head_grad.reshape(128, BR), *blocks, raw=10,
    )
    from_low, from_high = send(plus, "z", 1), send(minus, "z", -1)
    pieces = [pieces[0]] + [send(pieces[k], "y", k) for k in (1, 2, 3)]
    half_a, half_b = call(
        bridge_kernel, (shape((64, 1024), F32), shape((72, 1024), F32)), [], 10**5,
        plus_half, from_low, minus_half, from_high, *pieces[1:], scalar=False,
    )
    half_a, half_b = send(half_a, "z", 1), send(half_b, "z", -1)
    turned, colsum = call(
        turn_kernel, (shape((7, CH, HALF), BF), shape((8, CH), F32)), [pltpu.VMEM((32, 4, 16, CH), BF)], 10**8,
        pos, *pieces,
    )
    keep, give, pay = call(
        middle_kernel,
        (shape((9, 16, 512), BF), shape((9, 16, 512), BF), shape((GROUPS, 96, BR), BF)),
        [], 2 * 10**8, pos, own, from_low, from_high, half_a, half_b, x, proj_weight, colsum,
    )
    block = call(pair_kernel, shape((2, 9, 16, 512), BF), [], 10**5, keep, swap(give), scalar=False)
    near = [block, cross(block, 1, False), cross(block, -1, False), cross(block, 2, False)]
    group, sums = call(
        group_kernel, (shape((4, 2, 8, 16, 512), BF), shape((8, 512), F32)), [], 10**10, *near, scalar=False
    )
    every = [group] + [cross(group, step, True) for step in (1, -1, 2)]
    sums = jnp.where(pos[2] == 0, sums, swap(sums))
    const, pool_grad, outer = call(
        pool_kernel, (shape((8, BR), F32), shape((8, BR), F32), shape((16, BR), F32)), [pltpu.VMEM((256, BR), F32)],
        10**7, pos, sums, proj_weight,
    )
    pay = exchange(pay)
    part = call(collect_kernel, shape((64, BR), F32), [], 10**6, pay, outer, scalar=False)
    part = jnp.concatenate([part + swap(part), outer], axis=0)
    part = (part + pair(part, "rep", 1)) + (pair(part, "rep", 2) + pair(part, "rep", 3))
    part = jnp.broadcast_to(part.astype(BF)[None], (GROUPS, 80, BR))
    below, = gate((every[1],), (part,))
    every = [every[0], below] + every[2:4]
    every = every + [swap(piece) for piece in every]
    dw, dw_other = call(
        weight_grad_kernel,
        (shape((29, 64, BR), BF), shape((29, 64, BR), BF)),
        [pltpu.VMEM((2 * GROUPS, 4, 16, 1024), BF), pltpu.VMEM((29, CH, BR), F32), pltpu.SemaphoreType.DMA((32,))],
        4 * 10**9, pos, turned, colsum, pool_grad, *every, raw=8,
    )
    quarters = call(
        add_kernel, (shape((464, BR), BF),) * 4, [], 10**6, pos, dw.reshape(1856, BR), swap(dw_other).reshape(1856, BR)
    )
    dx = call(
        field_grad_kernel,
        shape((2, HALF, 64), BF),
        [
            pltpu.VMEM((2 * (GROUPS + 2 * PAD), 4, 16, 1024), BF), pltpu.VMEM((29, CH, BR), BF),
            pltpu.VMEM((HALF, CH), F32), pltpu.SemaphoreType.DMA((32,)),
        ],
        4 * 10**9, pos, pool_grad, branch_weight, blocks[5], *every, quarters[0], raw=9,
    )
    terms = [quarters[0]] + [send(quarters[k], "rep", k) for k in (1, 3, 2)]
    dw = sum(term.astype(F32) for term in terms).astype(BF)
    dw = [dw] + [send(dw, "rep", step) for step in (1, -1, 2)]
    grad_branch = call(join_kernel, shape((1856, BR), F32), [], 10**6, pos, *dw).reshape(29, 64, BR)
    (part,) = gate((exchange(part),), (dw[0],))
    part = part.astype(F32)
    grad_proj = jnp.concatenate([part[:, 0:64].reshape(1024, BR), part[:, 64:80].reshape(256, BR)], axis=0)
    (const,) = gate((const,), (dw[0],))
    head_out = call(head_kernel, shape((128, BR), BF), [pltpu.VMEM((2, 128, 128), F32)], 10**6, pos, pay, const)
    mine, theirs = dx[0], swap(dx[1])
    even = jnp.where(pos[2] == 0, mine, theirs).reshape(GROUPS, 1, 2, 64, 64)
    odd = jnp.where(pos[2] == 0, theirs, mine).reshape(GROUPS, 1, 2, 64, 64)
    grad_features = jnp.concatenate([even, odd], axis=1).reshape(1, 64, 64, 64)
    return head_out.reshape(head_grad.shape), grad_features, grad_branch, grad_proj


def solution(mesh):
    fine = Mesh(mesh.devices.reshape(4, 4, 2, 4), ("z", "y", "core", "rep"))
    tile = ("z", "y", "core")
    return jax.shard_map(
        local,
        mesh=fine,
        in_specs=(P("rep", tile, None, None), P("rep", tile, None, None), P(None, tile, None), P()),
        out_specs=(P("rep", tile, None, None), P("rep", None, None, tile), P(None, tile, None), P()),
        check_vma=False,
    )
```

```python
import jax
import jax.numpy as jnp
from jax import lax
from jax.experimental import pallas as pl
from jax.experimental.pallas import tpu as pltpu
from jax.sharding import Mesh, PartitionSpec as P

GROUPS = 16
CH = 128
KCH = 512
BR = 256
HALF = 2048
PAD = 9
CUT = 15
SHIFTS = (0, -3, 3, -6, 6, -9, 9)
F32 = jnp.float32
BF = jnp.bfloat16
HIGH = lax.Precision.HIGHEST
ROWS_BY_COLS = (((1,), (1,)), ((), ()))
COLS_BY_COLS = (((0,), (0,)), ((), ()))


def shift_slot(j, b):
    return SHIFTS.index((b - 1) * 3 * (j + 1))


def column_shift(value, amount):
    if amount == 0:
        return value
    n = value.shape[0]
    col = lax.broadcasted_iota(jnp.int32, value.shape, 0) & 15
    rolled = pltpu.roll(value, (-amount) % n, 0)
    return jnp.where((col + amount >= 0) & (col + amount < 16), rolled, 0.0)


def wrap(value):
    return lax.rem(value + 8, 4)


def split_kernel(x_ref, hg_ref, first_ref, wide):
    for t in range(GROUPS):
        wide[t] = x_ref[:, CH * t : CH * (t + 1)].astype(F32)
    for t in range(2):
        wide[GROUPS + t] = hg_ref[:, CH * t : CH * (t + 1)].astype(F32)
    for v in range(4):
        for t in range(GROUPS + 2):
            part = wide[t, pl.ds(v, 32, stride=4), :].astype(BF)
            if t < GROUPS:
                place = CH * (t % 4)
                first_ref[4 * (t // 4) + v, :, place : place + CH] = part
            else:
                place = KCH + CH * (t - GROUPS)
                for z in range(4):
                    first_ref[4 * z + v, :, place : place + CH] = part


def weight_copies(pos_ref, blocks, w, sem):
    y, c = pos_ref[1], pos_ref[2]
    places = [(0, 0, 29), (-1, 0, 29), (1, 0, 29), (2, 0, CUT), (2, CUT, 29)]
    copies = []
    for side in range(2):
        for k, (step, low, high) in enumerate(places):
            core = c if side == 0 else 1 - c
            start = pl.multiple_of(wrap(y + step) * CH + core * 64, 64)
            n = len(copies)
            copies.append(
                pltpu.make_async_copy(blocks[n], w.at[pl.ds(low, high - low), pl.ds(start, 64), :], sem.at[n])
            )
    return copies


def forward_kernel(pos_ref, x_ref, hg_ref, *refs):
    blocks, outs, pieces, (w, xs, total, sem) = refs[:10], refs[10:15], refs[15:19], refs[19:]
    own_ref, plus_ref, minus_ref, plus_half, minus_half = outs
    copies = weight_copies(pos_ref, blocks, w, sem)
    for copy in copies:
        copy.start()
    for step in range(4):
        pieces[step][...] = x_ref[:, pl.ds(pl.multiple_of(wrap(pos_ref[1] + step) * CH, CH), CH)]
    wide = x_ref[:, 0:KCH].astype(F32)
    colsum = jnp.broadcast_to(jnp.sum(wide, axis=0, keepdims=True), (8, KCH))
    for slot, amount in enumerate(SHIFTS):
        if amount:
            xs[slot] = column_shift(wide, amount).astype(BF)
        else:
            xs[slot] = x_ref[:, 0:KCH]
    hsum = jnp.broadcast_to(jnp.sum(hg_ref[...].astype(F32), axis=0, keepdims=True), (8, BR))
    for copy in copies:
        copy.wait()
    pool = jnp.dot(colsum, w[28].astype(F32), precision=HIGH, preferred_element_type=F32)
    total[:, 0:BR] = jnp.dot(xs[0], w[0], preferred_element_type=F32)
    for j in range(3):
        cols = slice((j + 1) * BR, (j + 2) * BR)
        for a in (1, 0, 2):
            delta = 96 * (j + 1) * (a - 1)
            in_low, in_high = max(delta, 0), 512 + min(delta, 0)
            out_low, out_high = max(-delta, 0), 512 - max(delta, 0)
            left = jnp.concatenate([xs[shift_slot(j, b), in_low:in_high, :] for b in range(3)], axis=1)
            start = 1 + 9 * j + 3 * a
            part = jnp.dot(left, w[start : start + 3].reshape(3 * KCH, BR), preferred_element_type=F32)
            if a == 1:
                total[:, cols] = part
            else:
                total[out_low:out_high, cols] += part
    extra = jnp.concatenate([pool, hsum, jnp.zeros((8, 512), F32)], axis=1)
    z = pos_ref[0]

    def rows(step, low, size):
        return total[pl.ds(pl.multiple_of(wrap(z + step) * 128 + low, 64), size), :]

    own_ref[0:128, :] = rows(0, 0, 128)
    own_ref[128:136, :] = extra
    plus_ref[0:64, :] = rows(2, 0, 64)
    plus_ref[64:128, :] = rows(1, 64, 64)
    plus_ref[128:136, :] = extra
    minus_ref[0:64, :] = rows(2, 64, 64)
    minus_ref[64:72, :] = extra
    minus_ref[72:136, :] = rows(-1, 0, 64)
    plus_half[...] = rows(1, 0, 64)
    minus_half[0:64, :] = rows(-1, 64, 64)
    minus_half[64:72, :] = extra


def bridge_kernel(plus_half, from_low, minus_half, from_high, *refs):
    refs[3][...] = plus_half[...] + from_low[0:64, :]
    refs[4][...] = minus_half[...] + from_high[0:72, :]


def pair_kernel(first_ref, second_ref, out_ref):
    out_ref[0] = first_ref[...]
    out_ref[1] = second_ref[...]


def group_kernel(*refs):
    parts, (out_ref, sums_ref) = refs[:4], refs[4:]
    total = jnp.zeros((16, 512), F32)
    for k in range(4):
        for side in range(2):
            out_ref[k, side] = parts[k][side, 0:8]
            total = total + parts[k][side, 8].astype(F32)
    sums_ref[...] = jnp.broadcast_to(jnp.sum(total, axis=0, keepdims=True), (8, 512))


def turn_kernel(pos_ref, *refs):
    pieces, (xt_ref, colsum_ref, joined) = refs[:4], refs[4:]
    for k in range(4):
        joined[:, wrap(pos_ref[1] - k)] = pieces[k][...].reshape(32, 16, CH)
    total = jnp.zeros((1, CH), F32)
    for m in range(4):
        wide = joined[8 * m : 8 * (m + 1)].reshape(512, CH).astype(F32)
        total = total + jnp.sum(wide, axis=0, keepdims=True)
        for slot, amount in enumerate(SHIFTS):
            xt_ref[slot, :, pl.ds(m * 512, 512)] = column_shift(wide, amount).T.astype(BF)
    colsum_ref[...] = jnp.broadcast_to(total, (8, CH))


def middle_kernel(pos_ref, own, from_low, from_high, half_a, half_b, x_ref, pw_ref, _, keep_ref, give_ref, pay_ref):
    top = own[0:64, :] + from_high[72:136, :] + half_a[...]
    bottom = own[64:136, :] + from_low[64:136, :] + half_b[...]
    pre = jnp.concatenate([top, bottom[0:64, :]], axis=0)
    act = jnp.maximum(pre, 0.0).astype(BF)
    low = pw_ref[0:1024, :]
    hg = x_ref[pl.ds(pl.multiple_of(pos_ref[0] * 128, 128), 128), KCH:]
    back = lax.dot_general(hg, low, ROWS_BY_COLS, preferred_element_type=F32)
    grads = jnp.where(pre > 0, back, 0.0)
    first = pos_ref[2] == 0
    keep_ref[0:8] = jnp.where(first, grads[:, 0:512], grads[:, 512:1024]).astype(BF).reshape(8, 16, 512)
    give_ref[0:8] = jnp.where(first, grads[:, 512:1024], grads[:, 0:512]).astype(BF).reshape(8, 16, 512)
    sums = jnp.concatenate([bottom[64:72, 0:512]] * 2, axis=0)
    one = sums.astype(BF).astype(F32)
    two = (sums - one).astype(BF).astype(F32)
    row = lax.broadcasted_iota(jnp.int32, sums.shape, 0)
    terms = jnp.where(row == 0, one, jnp.where(row == 1, two, jnp.where(row == 2, sums - one - two, 0.0))).astype(BF)
    keep_ref[8] = terms
    give_ref[8] = terms
    head = jnp.dot(act, low, preferred_element_type=F32).astype(BF)
    proj = lax.dot_general(act, hg, COLS_BY_COLS, preferred_element_type=F32).astype(BF)
    for t in range(GROUPS):
        pay_ref[t, 0:64, :] = proj[64 * t : 64 * (t + 1), :]
        pay_ref[t, 64:96, :] = head[32 * (t % 4) : 32 * (t % 4 + 1), :]


def pool_kernel(pos_ref, sums_ref, pw_ref, const_ref, grad_ref, outer_ref, whole):
    pool = sums_ref[:, 0:BR] * (1.0 / 4096.0)
    hsum = sums_ref[:, BR : 2 * BR]
    act = jnp.maximum(pool, 0.0).astype(BF)
    high = pw_ref[1024:1280, :]
    const_ref[...] = jnp.dot(act, high, preferred_element_type=F32)
    grad = lax.dot_general(hsum, high.astype(F32), ROWS_BY_COLS, precision=HIGH, preferred_element_type=F32)
    grad_ref[...] = jnp.where(pool > 0, grad, 0.0)
    whole[...] = 0.125 * lax.dot_general(
        act.astype(F32), hsum, COLS_BY_COLS, precision=HIGH, preferred_element_type=F32
    )
    chunk = pos_ref[0] * 4 + pos_ref[1]
    outer_ref[...] = whole[pl.ds(pl.multiple_of(chunk * 16, 16), 16), :]


def collect_kernel(pay_ref, _, part_ref):
    total = pay_ref[0, 0:64, :].astype(F32)
    for t in range(1, GROUPS):
        total = total + pay_ref[t, 0:64, :].astype(F32)
    part_ref[...] = total


def head_kernel(pos_ref, pay_ref, const_ref, head_ref, wide):
    for v in range(4):
        piece = pay_ref[4 * pos_ref[0] + v, 64:96, :].astype(F32) + const_ref[0:1, :]
        wide[0, pl.ds(v, 32, stride=4), :] = piece[:, 0:128]
        wide[1, pl.ds(v, 32, stride=4), :] = piece[:, 128:256]
    head_ref[:, 0:128] = wide[0].astype(BF)
    head_ref[:, 128:256] = wide[1].astype(BF)


def gather_copies(pos_ref, blocks, g, sem, pad):
    z, y, c = pos_ref[0], pos_ref[1], pos_ref[2]
    copies = []
    for side in range(2):
        half = c if side == 0 else 1 - c
        for place, far in enumerate((0, -1, 1, 2)):
            for k, step in enumerate((0, -1, 1, 2)):
                src = blocks[4 * side + place].at[k, side]
                v = wrap(y + jnp.where(half == 0, step, far))
                group = wrap(z + jnp.where(half == 0, far, step))
                cols = pl.ds(pl.multiple_of(512 * half, 512), 512)
                dst = g.at[pl.ds(2 * pad + 8 * group, 8), v, :, cols]
                copies.append(pltpu.make_async_copy(src, dst, sem.at[len(copies)]))
    return copies


def weight_grad_kernel(pos_ref, xt_ref, colsum_ref, grad_ref, *refs):
    blocks, (own_ref, other_ref), (g, dw, sem) = refs[:8], refs[-5:-3], refs[-3:]
    copies = gather_copies(pos_ref, blocks, g, sem, 0)
    for copy in copies:
        copy.start()
    for copy in copies:
        copy.wait()

    def grads(low, high, cols):
        return g[low // 64 : high // 64, :, :, cols].reshape(high - low, BR)

    dw[0] = jnp.dot(xt_ref[0], grads(0, HALF, slice(0, BR)), preferred_element_type=F32)
    for j in range(3):
        cols = slice((j + 1) * BR, (j + 2) * BR)
        for a in range(3):
            delta = 3 * (j + 1) * (a - 1) * 128
            x_low, x_high = max(delta, 0), HALF + min(delta, 0)
            g_low, g_high = max(-delta, 0), HALF - max(delta, 0)
            left = jnp.concatenate([xt_ref[shift_slot(j, b), :, x_low:x_high] for b in range(3)], axis=0)
            part = jnp.dot(left, grads(g_low, g_high, cols), preferred_element_type=F32)
            start = 1 + 9 * j + 3 * a
            dw[start : start + 3] = part.reshape(3, CH, BR)
    dw[28] = lax.dot_general(
        colsum_ref[...], grad_ref[...], COLS_BY_COLS, precision=HIGH, preferred_element_type=F32
    ) * (0.125 / 4096.0)
    c = pos_ref[2]
    own_ref[...] = dw[:, pl.ds(pl.multiple_of(c * 64, 64), 64), :].astype(BF)
    other_ref[...] = dw[:, pl.ds(pl.multiple_of((1 - c) * 64, 64), 64), :].astype(BF)


def field_grad_kernel(pos_ref, grad_ref, own, other, *refs):
    blocks, dx_ref, (g, w, whole, sem) = refs[:8], refs[-5], refs[-4:]
    copies = gather_copies(pos_ref, blocks, g, sem, PAD)
    for copy in copies:
        copy.start()
    c = pos_ref[2]
    w[:, pl.ds(pl.multiple_of(c * 64, 64), 64), :] = own[...]
    w[:, pl.ds(pl.multiple_of((1 - c) * 64, 64), 64), :] = other[...]
    g[0 : 2 * PAD] = jnp.zeros((2 * PAD, 4, 16, 1024), BF)
    g[2 * (PAD + GROUPS) :] = jnp.zeros((2 * PAD, 4, 16, 1024), BF)
    field = lax.dot_general(
        grad_ref[...], w[28].astype(F32), ROWS_BY_COLS, precision=HIGH, preferred_element_type=F32
    )[0:1, :] * (1.0 / 4096.0)
    for copy in copies:
        copy.wait()

    def grads(low, cols):
        return g[2 * (PAD + low) : 2 * (PAD + low + 4), :, :, cols].reshape(512, BR)

    for m in range(4):
        acc = field + lax.dot_general(
            grads(4 * m, slice(0, BR)), w[0], ROWS_BY_COLS, preferred_element_type=F32
        )
        for j in range(3):
            steps = []
            for a in range(3):
                low = 4 * m - 3 * (j + 1) * (a - 1)
                if low + 3 >= 0 and low < GROUPS:
                    steps.append((a, low))
            left = jnp.concatenate([grads(low, slice((j + 1) * BR, (j + 2) * BR)) for _, low in steps], axis=1)
            right = jnp.concatenate(
                [w[1 + 9 * j + 3 * a : 4 + 9 * j + 3 * a].reshape(3 * CH, BR) for a, _ in steps], axis=1
            )
            spread = lax.dot_general(left, right, ROWS_BY_COLS, preferred_element_type=F32)
            for b in range(3):
                acc = acc + column_shift(spread[:, b * CH : (b + 1) * CH], -(b - 1) * 3 * (j + 1))
        for row in range(8):
            for v in range(4):
                place = (4 * row + v) * 16
                whole[pl.ds(512 * m + 64 * row + v, 16, stride=4), :] = acc[place : place + 16, :]
    low, high = whole[:, 0:64], whole[:, 64:128]
    dx_ref[0] = jnp.where(c == 0, low, high).astype(BF)
    dx_ref[1] = jnp.where(c == 0, high, low).astype(BF)


def add_kernel(pos_ref, own, other, *outs):
    r = pos_ref[3]
    for k in range(4):
        rows = pl.ds(pl.multiple_of(wrap(r + k) * 464, 16), 464)
        outs[k][...] = (own[rows, :].astype(F32) + other[rows, :].astype(F32)).astype(BF)


def join_kernel(pos_ref, *refs):
    for k, step in enumerate((0, -1, 1, 2)):
        rows = pl.ds(pl.multiple_of(wrap(pos_ref[3] + step) * 464, 8), 464)
        refs[4][rows, :] = refs[k][...].astype(F32)


ROOM = {"forward_kernel": 28, "weight_grad_kernel": 44, "field_grad_kernel": 22, "turn_kernel": 16, "middle_kernel": 16}


def call(kernel, out_shape, scratch, flops, *args, scalar=True, raw=0):
    specs = [pl.BlockSpec(memory_space=pltpu.VMEM) for _ in args]
    if scalar:
        specs[0] = pl.BlockSpec(memory_space=pltpu.SMEM)
    for k in range(raw):
        specs[len(args) - 1 - k] = pl.BlockSpec(memory_space=pl.ANY)
    moved = sum(a.size * a.dtype.itemsize for a in jax.tree.leaves((args, out_shape)))
    return pl.pallas_call(
        kernel,
        out_shape=out_shape,
        in_specs=specs,
        out_specs=jax.tree.map(lambda _: pl.BlockSpec(memory_space=pltpu.VMEM), out_shape),
        scratch_shapes=scratch,
        compiler_params=pltpu.CompilerParams(vmem_limit_bytes=ROOM.get(kernel.__name__, 12) * 2**20),
        cost_estimate=pl.CostEstimate(flops=flops, bytes_accessed=moved, transcendentals=0),
        name=kernel.__name__,
    )(*args)


def gate(values, after):
    anywhere = pl.BlockSpec(memory_space=pl.ANY)
    return pl.pallas_call(
        lambda *refs: None,
        out_shape=tuple(jax.ShapeDtypeStruct(v.shape, v.dtype) for v in values),
        in_specs=[anywhere] * (len(values) + len(after)),
        out_specs=(anywhere,) * len(values),
        input_output_aliases={k: k for k in range(len(values))},
        cost_estimate=pl.CostEstimate(flops=0, bytes_accessed=0, transcendentals=0),
    )(*values, *after)


def swap(value):
    return lax.ppermute(value, "core", [(0, 1), (1, 0)])


def send(value, axis, step):
    return lax.ppermute(value, axis, [(k, (k + step) % 4) for k in range(4)])


def pair(value, axis, bit):
    return lax.ppermute(value, axis, [(k, k ^ bit) for k in range(4)])


def cross(value, step, turn):
    pairs = []
    for z in range(4):
        for y in range(4):
            for c in range(2):
                along_y = (c == 0) != turn
                to = (z, (y + step) % 4) if along_y else ((z + step) % 4, y)
                pairs.append(((4 * z + y) * 2 + c, (4 * to[0] + to[1]) * 2 + c))
    return lax.ppermute(value, ("z", "y", "core"), pairs)


def local(features, head_grad, branch_weight, proj_weight):
    shape = jax.ShapeDtypeStruct
    plane = ("z", "y")
    pos = jnp.stack([lax.axis_index(n).astype(jnp.int32) for n in ("z", "y", "core", "rep")])

    def exchange(value):
        return lax.all_to_all(value, plane, split_axis=0, concat_axis=0, tiled=True)

    first = call(
        split_kernel, shape((GROUPS, 32, KCH + BR), BF),
        [pltpu.VMEM((GROUPS + 2, 128, CH), F32)], 10**6,
        features.reshape(128, 2048), head_grad.reshape(128, BR), scalar=False,
    )
    below, above = send(branch_weight, "y", 1), send(branch_weight, "y", -1)
    x = exchange(first).reshape(512, KCH + BR)
    below, above = gate((below, above), (x,))
    blocks = [branch_weight, below, above, send(below[0:CUT], "y", 1), send(above[CUT:29], "y", -1)]
    blocks = blocks + [swap(b) for b in blocks]
    own, plus, minus, plus_half, minus_half, *pieces = call(
        forward_kernel,
        tuple(shape((n, 1024), F32) for n in (136, 136, 136, 64, 72)) + (shape((512, CH), BF),) * 4,
        [
            pltpu.VMEM((29, KCH, BR), BF), pltpu.VMEM((7, 512, KCH), BF), pltpu.VMEM((512, 1024), F32),
            pltpu.SemaphoreType.DMA((10,)),
        ],
        4 * 10**9, pos, x, head_grad.reshape(128, BR), *blocks, raw=10,
    )
    from_low, from_high = send(plus, "z", 1), send(minus, "z", -1)
    pieces = [pieces[0]] + [send(pieces[k], "y", k) for k in (1, 2, 3)]
    half_a, half_b = call(
        bridge_kernel, (shape((64, 1024), F32), shape((72, 1024), F32)), [], 10**5,
        plus_half, from_low, minus_half, from_high, *pieces[1:], scalar=False,
    )
    half_a, half_b = send(half_a, "z", 1), send(half_b, "z", -1)
    turned, colsum = call(
        turn_kernel, (shape((7, CH, HALF), BF), shape((8, CH), F32)), [pltpu.VMEM((32, 4, 16, CH), BF)], 10**8,
        pos, *pieces,
    )
    keep, give, pay = call(
        middle_kernel,
        (shape((9, 16, 512), BF), shape((9, 16, 512), BF), shape((GROUPS, 96, BR), BF)),
        [], 2 * 10**8, pos, own, from_low, from_high, half_a, half_b, x, proj_weight, colsum,
    )
    block = call(pair_kernel, shape((2, 9, 16, 512), BF), [], 10**5, keep, swap(give), scalar=False)
    near = [block, cross(block, 1, False), cross(block, -1, False), cross(block, 2, False)]
    group, sums = call(
        group_kernel, (shape((4, 2, 8, 16, 512), BF), shape((8, 512), F32)), [], 10**10, *near, scalar=False
    )
    every = [group] + [cross(group, step, True) for step in (1, -1, 2)]
    sums = jnp.where(pos[2] == 0, sums, swap(sums))
    const, pool_grad, outer = call(
        pool_kernel, (shape((8, BR), F32), shape((8, BR), F32), shape((16, BR), F32)), [pltpu.VMEM((256, BR), F32)],
        10**7, pos, sums, proj_weight,
    )
    pay = exchange(pay)
    part = call(collect_kernel, shape((64, BR), F32), [], 10**6, pay, outer, scalar=False)
    part = jnp.concatenate([part + swap(part), outer], axis=0)
    part = (part + pair(part, "rep", 1)) + (pair(part, "rep", 2) + pair(part, "rep", 3))
    part = jnp.broadcast_to(part.astype(BF)[None], (GROUPS, 80, BR))
    below, = gate((every[1],), (part,))
    every = [every[0], below] + every[2:4]
    every = every + [swap(piece) for piece in every]
    dw, dw_other = call(
        weight_grad_kernel,
        (shape((29, 64, BR), BF), shape((29, 64, BR), BF)),
        [pltpu.VMEM((2 * GROUPS, 4, 16, 1024), BF), pltpu.VMEM((29, CH, BR), F32), pltpu.SemaphoreType.DMA((32,))],
        4 * 10**9, pos, turned, colsum, pool_grad, *every, raw=8,
    )
    quarters = call(
        add_kernel, (shape((464, BR), BF),) * 4, [], 10**6, pos, dw.reshape(1856, BR), swap(dw_other).reshape(1856, BR)
    )
    dx = call(
        field_grad_kernel,
        shape((2, HALF, 64), BF),
        [
            pltpu.VMEM((2 * (GROUPS + 2 * PAD), 4, 16, 1024), BF), pltpu.VMEM((29, CH, BR), BF),
            pltpu.VMEM((HALF, CH), F32), pltpu.SemaphoreType.DMA((32,)),
        ],
        4 * 10**9, pos, pool_grad, branch_weight, blocks[5], *every, quarters[0], raw=9,
    )
    terms = [quarters[0]] + [send(quarters[k], "rep", k) for k in (1, 3, 2)]
    dw = sum(term.astype(F32) for term in terms).astype(BF)
    dw = [dw] + [send(dw, "rep", step) for step in (1, -1, 2)]
    grad_branch = call(join_kernel, shape((1856, BR), F32), [], 10**6, pos, *dw).reshape(29, 64, BR)
    (part,) = gate((exchange(part),), (dw[0],))
    part = part.astype(F32)
    grad_proj = jnp.concatenate([part[:, 0:64].reshape(1024, BR), part[:, 64:80].reshape(256, BR)], axis=0)
    (const,) = gate((const,), (dw[0],))
    head_out = call(head_kernel, shape((128, BR), BF), [pltpu.VMEM((2, 128, 128), F32)], 10**6, pos, pay, const)
    mine, theirs = dx[0], swap(dx[1])
    even = jnp.where(pos[2] == 0, mine, theirs).reshape(GROUPS, 1, 2, 64, 64)
    odd = jnp.where(pos[2] == 0, theirs, mine).reshape(GROUPS, 1, 2, 64, 64)
    grad_features = jnp.concatenate([even, odd], axis=1).reshape(1, 64, 64, 64)
    return head_out.reshape(head_grad.shape), grad_features, grad_branch, grad_proj


def solution(mesh):
    fine = Mesh(mesh.devices.reshape(4, 4, 2, 4), ("z", "y", "core", "rep"))
    tile = ("z", "y", "core")
    return jax.shard_map(
        local,
        mesh=fine,
        in_specs=(P("rep", tile, None, None), P("rep", tile, None, None), P(None, tile, None), P()),
        out_specs=(P("rep", tile, None, None), P("rep", None, None, tile), P(None, tile, None), P()),
        check_vma=False,
    )
```
